32 devices in a mesh: dp: 8 (over z, y), fsdp: 4 (over x, core).
Axes of the slice: x: 2, y: 2, z: 4, core: 2. Of those that a mesh axis runs over, the one named last changes fastest.
Arguments:
- tokens: bfloat16 [4, 32, 256, 768], P('fsdp', 'dp'), may hold values from -6 to 6
- visible_index: int32 [4, 32, 256], P('fsdp'), may hold values from 0 to 1023, as said below
- cotangent: bfloat16 [4, 32, 1024, 768], P('fsdp', None, 'dp'), may hold values from -6 to 6
- qkv_weight: float32 [768, 2304], P('dp', 'fsdp'), may hold values from -0.21875 to 0.21875
- out_weight: float32 [768, 768], P('dp', 'fsdp'), may hold values from -1.25 to 1.25
- up_weight: float32 [768, 3072], P('dp', 'fsdp'), may hold values from -0.21875 to 0.21875
- down_weight: float32 [3072, 768], P('dp', 'fsdp'), may hold values from -0.109375 to 0.109375
- vectors: float32 [12, 768], P('fsdp', 'dp'), may hold values from -3 to 4
- qkv_first: float32 [768, 2304], P('dp', 'fsdp'), may hold values from -14 to 14
- out_first: float32 [768, 768], P('dp', 'fsdp'), may hold values from -4 to 4
- up_first: float32 [768, 3072], P('dp', 'fsdp'), may hold values from -12 to 12
- down_first: float32 [3072, 768], P('dp', 'fsdp'), may hold values from -20 to 20
- vector_first: float32 [12, 768], P('fsdp', 'dp'), may hold values from -32 to 32
- qkv_second: float32 [768, 2304], P('dp', 'fsdp'), may hold values from 2.29376 to 36.0448
- out_second: float32 [768, 768], P('dp', 'fsdp'), may hold values from 0.262144 to 4.25984
- up_second: float32 [768, 3072], P('dp', 'fsdp'), may hold values from 1.96608 to 32.768
- down_second: float32 [3072, 768], P('dp', 'fsdp'), may hold values from 5.89824 to 95.0272
- vector_second: float32 [12, 768], P('fsdp', 'dp'), may hold values from 13.1072 to 196.608
Outputs:
- full_layout: bfloat16 [4, 32, 1024, 768], P('fsdp', None, 'dp')
- tokens_grad: float32 [4, 32, 256, 768], P('fsdp', 'dp')
- qkv_first_new: float32 [768, 2304], P('dp', 'fsdp')
- qkv_second_new: float32 [768, 2304], P('dp', 'fsdp')
- qkv_new: float32 [768, 2304], P('dp', 'fsdp')
- qkv_copy: bfloat16 [768, 2304], P('dp', 'fsdp')
- out_first_new: float32 [768, 768], P('dp', 'fsdp')
- out_second_new: float32 [768, 768], P('dp', 'fsdp')
- out_new: float32 [768, 768], P('dp', 'fsdp')
- out_copy: bfloat16 [768, 768], P('dp', 'fsdp')
- up_first_new: float32 [768, 3072], P('dp', 'fsdp')
- up_second_new: float32 [768, 3072], P('dp', 'fsdp')
- up_new: float32 [768, 3072], P('dp', 'fsdp')
- up_copy: bfloat16 [768, 3072], P('dp', 'fsdp')
- down_first_new: float32 [3072, 768], P('dp', 'fsdp')
- down_second_new: float32 [3072, 768], P('dp', 'fsdp')
- down_new: float32 [3072, 768], P('dp', 'fsdp')
- down_copy: bfloat16 [3072, 768], P('dp', 'fsdp')
- vector_first_new: float32 [12, 768], P('fsdp', 'dp')
- vector_second_new: float32 [12, 768], P('fsdp', 'dp')
- vector_new: float32 [12, 768], P('fsdp', 'dp')
- grad_norm: float32 [], replicated
The draws below stay inside these ranges and needn't reach their ends.
Inputs may be any that keep to these rules, and one draw needn't show every extreme that they name: `visible_index`: for every chip and every block b of 128 consecutive patches, exactly 32 entries lie in the block, and entries b * 32 to (b + 1) * 32 - 1 of the chip are those of block b, ascending and distinct.
All inputs are finite; a program needn't handle non-finite values.
Results may differ from the reference program's by a relative error of at most 0.019.
Values may be sent and summed in bfloat16 or wider, within the bound.
No kernel may reach another device: no remote copies, remote signals or barrier semaphores. Data moves between devices by JAX's collectives and lax.ppermute only.
A program may use at most 192 MiB of HBM per device.

```python
import math
import jax
import jax.numpy as jnp
from jax import lax

D = 768
FF = 3072
HD = 64
P_SIZE = 1024
VEC = 12
STEP = 10
GROUPS = 4
CHIPS_G = 32
V = 256
BLOCKS = 8
BLK = 128
VB = 32
HEADS = 12
TOKENS = 32768


def draw_visible_index(key, part):
    key = jax.random.fold_in(key, 7)
    shape_all = (GROUPS, CHIPS_G, BLOCKS, BLK)
    scores = jax.random.randint(key, shape_all, 0, 2 ** 20) * BLK + lax.broadcasted_iota(jnp.int32, shape_all, 3)
    ranked = jnp.argsort(scores, axis=-1)[..., :VB].astype(jnp.int32)
    picked = jnp.sort(ranked, axis=-1)
    block_base = lax.broadcasted_iota(jnp.int32, (GROUPS, CHIPS_G, BLOCKS, VB), 2) * BLK
    return (picked + block_base).reshape(GROUPS, CHIPS_G, V)


def draw_vectors(key, part):
    key = jax.random.fold_in(key, 5)
    first_key, second_key, third_key = jax.random.split(key, 3)
    column = lax.broadcasted_iota(jnp.float32, (VEC, D), 1) / (D - 1)
    row_ids = lax.broadcasted_iota(jnp.int32, (VEC, D), 0)
    jitter = jax.random.uniform(first_key, (VEC, D), jnp.float32, 0.8, 1.25)
    rising = 0.6 * jnp.exp(column * jnp.log(3.0))
    offsets = 0.3 * jnp.clip(jax.random.normal(second_key, (VEC, D), jnp.float32), -4.0, 4.0)
    masked = 0.9 * jnp.clip(jax.random.normal(third_key, (VEC, D), jnp.float32), -3.0, 3.0)
    gains = rising * jitter
    is_gain = (row_ids == 0) | (row_ids == 4)
    return jnp.where(is_gain, gains, jnp.where(row_ids == 11, masked, offsets))


def steps_of(key, shape, cuts, least, top_value):
    def one(dim, parts):
        heights = jax.random.uniform(jax.random.fold_in(jax.random.fold_in(key, 6), dim), (parts,), jnp.float32, least / len(cuts), top_value / len(cuts))
        return jnp.repeat(jnp.exp(heights), shape[dim] // parts).reshape((-1,) + (1,) * (len(shape) - dim - 1))

    loudness = one(*cuts[0])
    for cut in cuts[1:]:
        loudness = loudness * one(*cut)
    return loudness


def bell_draw(key, shape, deviation, limit, pieces=(), kind=jnp.bfloat16):
    factor_of = steps_of(key, shape, pieces, -0.22, 0.18) if pieces else 1.0
    values = jax.random.normal(key, shape, jnp.float32) * deviation * factor_of
    return jnp.minimum(jnp.maximum(values, -limit), limit).astype(kind)


def setup_inputs(seed: int = 0) -> dict:
    keys = jax.random.split(jax.random.key(seed), 19)
    return {
        "tokens": bell_draw(keys[0], (GROUPS, CHIPS_G, V, D), 1.0, 6.0, ((0, 4), (1, 8))),
        "visible_index": draw_visible_index(jax.random.fold_in(keys[18], 71), 0),
        "cotangent": bell_draw(keys[2], (GROUPS, CHIPS_G, P_SIZE, D), 1.0, 6.0, ((0, 4), (2, 8))),
        "qkv_weight": bell_draw(keys[3], (D, 3 * D), D ** -0.5, 0.21875, ((0, 8), (1, 4)), jnp.float32),
        "out_weight": bell_draw(keys[4], (D, D), (D // 32) ** -0.5, 1.25, ((0, 8), (1, 4)), jnp.float32),
        "up_weight": bell_draw(keys[5], (D, FF), D ** -0.5, 0.21875, ((0, 8), (1, 4)), jnp.float32),
        "down_weight": bell_draw(keys[6], (FF, D), FF ** -0.5, 0.109375, ((0, 8), (1, 4)), jnp.float32),
        "vectors": draw_vectors(jax.random.fold_in(keys[18], 71), 0),
        "qkv_first": bell_draw(keys[8], (D, 3 * D), (0.012 * TOKENS ** 0.5), 14.0, ((0, 8), (1, 4)), jnp.float32),
        "out_first": bell_draw(keys[9], (D, D), (0.004 * TOKENS ** 0.5), 4.0, ((0, 8), (1, 4)), jnp.float32),
        "up_first": bell_draw(keys[10], (D, FF), (0.011 * TOKENS ** 0.5), 12.0, ((0, 8), (1, 4)), jnp.float32),
        "down_first": bell_draw(keys[11], (FF, D), (0.019 * TOKENS ** 0.5), 20.0, ((0, 8), (1, 4)), jnp.float32),
        "vector_first": bell_draw(keys[12], (VEC, D), (0.028 * TOKENS ** 0.5), 32.0, ((0, 4), (1, 8)), jnp.float32),
        "qkv_second": jnp.clip(jnp.exp(math.log(36.0448) - 2.7545702 * jax.random.uniform(keys[13], (D, 3 * D), jnp.float32) ** steps_of(keys[13], (D, 3 * D), ((0, 8), (1, 4)), -0.2, 0.2)), 2.29376, 36.0448),
        "out_second": jnp.clip(jnp.exp(math.log(4.25984) - 2.7880929 * jax.random.uniform(keys[14], (D, D), jnp.float32) ** steps_of(keys[14], (D, D), ((0, 8), (1, 4)), -0.2, 0.2)), 0.262144, 4.25984),
        "up_second": jnp.clip(jnp.exp(math.log(32.768) - 2.8134108 * jax.random.uniform(keys[15], (D, FF), jnp.float32) ** steps_of(keys[15], (D, FF), ((0, 8), (1, 4)), -0.2, 0.2)), 1.96608, 32.768),
        "down_second": jnp.clip(jnp.exp(math.log(95.0272) - 2.779509 * jax.random.uniform(keys[16], (FF, D), jnp.float32) ** steps_of(keys[16], (FF, D), ((0, 8), (1, 4)), -0.2, 0.2)), 5.89824, 95.0272),
        "vector_second": jnp.clip(jnp.exp(math.log(196.608) - 2.7080502 * jax.random.uniform(keys[17], (VEC, D), jnp.float32) ** steps_of(keys[17], (VEC, D), ((0, 4), (1, 8)), -0.2, 0.2)), 13.1072, 196.608),
    }


@jax.custom_vjp
def low(v):
    return lax.optimization_barrier(v.astype(jnp.bfloat16)).astype(jnp.float32)

@jax.custom_vjp
def low_back(v):
    return v

def low_keep(v):
    return (low(v), None)

def low_pass(kept, grad):
    return (grad,)

def back_keep(v):
    return (v, None)

def back_low(kept, grad):
    return (low(grad),)
low.defvjp(low_keep, low_pass)
low_back.defvjp(back_keep, back_low)
precise = lax.Precision.HIGHEST

def layer_norm(values, gain_row, offset):
    center = values - lax.optimization_barrier(jnp.mean(values, axis=-1, keepdims=True))
    spread = lax.optimization_barrier(jnp.mean(center * center, axis=-1, keepdims=True))
    return center * lax.rsqrt(spread + 1e-05) * gain_row + offset

def attend(block_in):
    queries, key_rows, values = block_in
    scores = low_back(jnp.einsum('cqhe,ckhe->chqk', queries, key_rows, precision=precise)) * HD ** (-0.5)
    attn_probs = low(jax.nn.softmax(scores, axis=-1))
    return jnp.einsum('chqk,ckhe->cqhe', attn_probs, values, precision=precise)

def adam_step(weight, gradient, first_mom, second, clip_factor, step_rate, decay_rate):
    scaled = gradient * clip_factor
    first_new = 0.5 * first_mom + 0.5 * scaled
    second_new = 0.5 * second + 0.5 * scaled * scaled
    correction = 1.0 - 0.5 ** STEP
    update = first_new / correction / (jnp.sqrt(second_new / correction) + 1e-08)
    return (first_new, second_new, weight - step_rate * (update + decay_rate * weight))

def reference(tokens, visible_index, cotangent, qkv_weight, out_weight, up_weight, down_weight, vectors, qkv_first, out_first, up_first, down_first, vector_first, qkv_second, out_second, up_second, down_second, vector_second):
    chip_total = GROUPS * CHIPS_G
    places = visible_index.reshape(chip_total, V).astype(jnp.int32)
    chip_rows = lax.broadcasted_iota(jnp.int32, (chip_total, V), 0)
    shown_mask = jnp.zeros((chip_total, P_SIZE), jnp.float32).at[chip_rows, places].set(1.0)
    hidden = 1.0 - shown_mask
    group_count = chip_total // 16

    def by_group(array):
        return array.reshape(group_count, 16, V, HEADS, HD)

    def forward(inputs, qkv_w, out_w, up_w, down_w, vecs):
        qkv_low = low(qkv_w)
        out_low = low(out_w)
        up_low = low(up_w)
        down_low = low(down_w)
        params = low(vecs)
        normed = low(layer_norm(inputs, params[0], params[1]))
        value_bias = jnp.concatenate([jnp.zeros((2 * D,), jnp.float32), params[2]])
        mixed_all = low_back(low(jnp.matmul(normed, qkv_low, precision=precise) + value_bias))
        mixed_all = mixed_all.reshape(chip_total, V, 3, HEADS, HD)
        head_out = lax.map(jax.checkpoint(attend), (by_group(mixed_all[:, :, 0]), by_group(mixed_all[:, :, 1]), by_group(mixed_all[:, :, 2])))
        context = low_back(low(head_out.reshape(chip_total, V, D)))
        branch = low_back(jnp.matmul(context, out_low, precision=precise) + params[3])
        middle = inputs + branch
        normed_two = low(layer_norm(middle, params[4], params[5]))
        gate_pre = low_back(jnp.matmul(normed_two, up_low, precision=precise) + params[6:10].reshape(FF))
        active = low(jax.nn.gelu(gate_pre, approximate=False))
        feed_out = low_back(jnp.matmul(active, down_low, precision=precise) + params[10])
        result = low(middle + feed_out)
        placed = jnp.zeros((chip_total, P_SIZE, D), jnp.float32).at[chip_rows, places].set(result)
        return placed + hidden[:, :, None] * params[11]
    inputs = tokens.astype(jnp.float32).reshape(chip_total, V, D)
    full_out, pullback = jax.vjp(forward, inputs, qkv_weight, out_weight, up_weight, down_weight, vectors)
    gradients = pullback(cotangent.astype(jnp.float32).reshape(chip_total, P_SIZE, D))
    squares = jnp.sum(gradients[1] * gradients[1]) + jnp.sum(gradients[2] * gradients[2])
    squares = squares + jnp.sum(gradients[3] * gradients[3]) + jnp.sum(gradients[4] * gradients[4])
    squares = squares + jnp.sum(gradients[5] * gradients[5])
    grad_norm = jnp.sqrt(squares)
    threshold = 0.05 * D * math.sqrt(TOKENS)
    clip_factor = jnp.minimum(1.0, threshold / grad_norm)
    qkv_out = adam_step(qkv_weight, gradients[1], qkv_first, qkv_second, clip_factor, 0.6 / math.sqrt(D), 0.05)
    out_out = adam_step(out_weight, gradients[2], out_first, out_second, clip_factor, 0.6 / math.sqrt(D // 32), 0.05)
    up_out = adam_step(up_weight, gradients[3], up_first, up_second, clip_factor, 0.6 / math.sqrt(D), 0.05)
    down_out = adam_step(down_weight, gradients[4], down_first, down_second, clip_factor, 0.6 / math.sqrt(FF), 0.05)
    vec_out = adam_step(vectors, gradients[5], vector_first, vector_second, clip_factor, 0.45, 0.0)
    full_layout = full_out.astype(jnp.bfloat16).reshape(GROUPS, CHIPS_G, P_SIZE, D)
    tokens_grad = gradients[0].reshape(GROUPS, CHIPS_G, V, D)
    return (full_layout, tokens_grad, qkv_out[0], qkv_out[1], qkv_out[2], qkv_out[2].astype(jnp.bfloat16), out_out[0], out_out[1], out_out[2], out_out[2].astype(jnp.bfloat16), up_out[0], up_out[1], up_out[2], up_out[2].astype(jnp.bfloat16), down_out[0], down_out[1], down_out[2], down_out[2].astype(jnp.bfloat16), vec_out[0], vec_out[1], vec_out[2], grad_norm)
```

```python
import math

import jax
import jax.numpy as jnp
from jax import lax
from jax.sharding import PartitionSpec as P

HD = 64
STEP = 10


def norm_rows(values, gain_row, offset):
    center = values - jnp.mean(values, axis=-1, keepdims=True)
    spread = jnp.mean(center * center, axis=-1, keepdims=True)
    return center * lax.rsqrt(spread + 1e-05) * gain_row + offset


def gelu_exact(values):
    return jax.nn.gelu(values, approximate=False)


def contract_rows(left, right):
    return lax.dot_general(
        left, right, (((0,), (0,)), ((), ())), preferred_element_type=jnp.float32
    )


def contract_cols(left, right):
    return lax.dot_general(
        left, right, (((1,), (1,)), ((), ())), preferred_element_type=jnp.float32
    )


def adam_step(weight, gradient, first_mom, second, clip_factor, step_rate, decay_rate):
    scaled = gradient * clip_factor
    first_new = 0.5 * first_mom + 0.5 * scaled
    second_new = 0.5 * second + 0.5 * scaled * scaled
    correction = 1.0 - 0.5**STEP
    update = first_new / correction / (jnp.sqrt(second_new / correction) + 1e-08)
    return (first_new, second_new, weight - step_rate * (update + decay_rate * weight))


def on_device(
    tokens,
    visible_index,
    cotangent,
    qkv_weight,
    out_weight,
    up_weight,
    down_weight,
    vectors,
    qkv_first,
    out_first,
    up_first,
    down_first,
    vector_first,
    qkv_second,
    out_second,
    up_second,
    down_second,
    vector_second,
):
    chip_count = tokens.shape[1]
    seq_len = tokens.shape[2]
    model_width = tokens.shape[3]
    block_count = lax.axis_size("dp")
    block_seen = seq_len // block_count
    block_len = cotangent.shape[2]
    chips_group = chip_count * block_count
    head_count = model_width // HD
    row_count = chip_count * seq_len
    score_scale = HD ** (-0.5)
    group_axis = lax.axis_size("fsdp")
    device_count = block_count * group_axis
    qkv_low = qkv_weight.astype(jnp.bfloat16)
    out_low = out_weight.astype(jnp.bfloat16)
    up_low = up_weight.astype(jnp.bfloat16)
    down_low = down_weight.astype(jnp.bfloat16)
    vector_low = vectors.astype(jnp.bfloat16)
    both = ("dp", "fsdp")

    def gather_whole(shard):
        rows, cols = shard.shape
        pieces = lax.all_gather(shard, both, axis=0, tiled=False)
        pieces = pieces.reshape(block_count, group_axis, rows, cols).transpose(0, 2, 1, 3)
        return pieces.reshape(block_count * rows, group_axis * cols)

    def scatter_sum(whole):
        rows, cols = whole.shape[0] // block_count, whole.shape[1] // group_axis
        pieces = whole.astype(jnp.bfloat16).reshape(block_count, rows, group_axis, cols)
        pieces = pieces.transpose(0, 2, 1, 3).reshape(device_count * rows, cols)
        return lax.psum_scatter(pieces, both, scatter_dimension=0, tiled=True).astype(jnp.float32)

    vector_copies = jnp.broadcast_to(vector_low, (device_count,) + vector_low.shape)
    vector_full = lax.all_to_all(vector_copies, both, split_axis=0, concat_axis=0, tiled=True)
    vec_rows, vec_cols = vectors.shape
    vector_full = vector_full.reshape(block_count, group_axis, vec_rows, vec_cols)
    vector_full = vector_full.transpose(1, 2, 0, 3).reshape(group_axis * vec_rows, -1)
    qkv_full = gather_whole(qkv_low)
    out_full = gather_whole(out_low)
    up_full = gather_whole(up_low)
    down_full = gather_whole(down_low)
    params = vector_full.astype(jnp.float32)
    inputs = tokens.reshape(row_count, model_width).astype(jnp.float32)
    normed, pull_one = jax.vjp(norm_rows, inputs, params[0], params[1])
    normed_low = normed.astype(jnp.bfloat16)
    value_bias = jnp.concatenate([jnp.zeros((2 * model_width,), jnp.float32), params[2]])
    mixed_all = (
        jnp.dot(normed_low, qkv_full, preferred_element_type=jnp.float32) + value_bias
    ).astype(jnp.bfloat16)
    mixed_all = mixed_all.reshape(chip_count, seq_len, 3, head_count, HD)
    queries = mixed_all[:, :, 0]
    key_rows = mixed_all[:, :, 1]
    values = mixed_all[:, :, 2]
    scores = (
        jnp.einsum("cqhe,ckhe->chqk", queries, key_rows, preferred_element_type=jnp.float32)
        * score_scale
    )
    row_peak = jnp.max(scores, axis=-1, keepdims=True)
    exponent = jnp.exp(scores - row_peak)
    row_total = jnp.sum(exponent, axis=-1, keepdims=True)
    log_total = row_peak + jnp.log(row_total)
    attn_low = (exponent / row_total).astype(jnp.bfloat16)
    context = jnp.einsum("chqk,ckhe->cqhe", attn_low, values, preferred_element_type=jnp.float32)
    context = context.astype(jnp.bfloat16).reshape(row_count, model_width)
    middle = inputs + jnp.dot(context, out_full, preferred_element_type=jnp.float32) + params[3]
    normed_two, pull_two = jax.vjp(norm_rows, middle, params[4], params[5])
    normed_two_low = normed_two.astype(jnp.bfloat16)
    gate_pre = jnp.dot(normed_two_low, up_full, preferred_element_type=jnp.float32) + params[
        6:10
    ].reshape(-1)
    active, pull_gelu = jax.vjp(gelu_exact, gate_pre)
    active_low = active.astype(jnp.bfloat16)
    result = (
        middle + jnp.dot(active_low, down_full, preferred_element_type=jnp.float32) + params[10]
    )
    result_low = result.astype(jnp.bfloat16)
    mask_value = params[11]
    block_rows = result_low.reshape(chip_count, block_count, block_seen, model_width)
    arrived = lax.all_to_all(block_rows, "dp", split_axis=1, concat_axis=0, tiled=True)
    arrived = arrived.reshape(chips_group, block_seen, model_width)
    my_block = lax.axis_index("dp")
    places = visible_index[0].reshape(chips_group, block_count, block_seen)
    places = lax.dynamic_index_in_dim(places, my_block, 1, keepdims=False) - my_block * block_len
    slot_ids = lax.broadcasted_iota(jnp.int32, (chips_group, block_len, block_seen), 1)
    pick = (places[:, None, :] == slot_ids).astype(jnp.bfloat16)
    gaps = 1.0 - jnp.sum(pick.astype(jnp.float32), axis=-1)
    filled = jnp.einsum("cpv,cvd->cpd", pick, arrived, preferred_element_type=jnp.float32)
    filled = filled + gaps[..., None] * mask_value
    full_layout = filled.astype(jnp.bfloat16).reshape(1, chips_group, block_len, model_width)
    cot_full = cotangent[0]
    cot_seen = jnp.einsum("cpv,cpd->cvd", pick, cot_full, preferred_element_type=jnp.float32)
    mask_grad = jnp.einsum(
        "cp,cpd->d", gaps.astype(jnp.bfloat16), cot_full, preferred_element_type=jnp.float32
    )
    returned = lax.all_to_all(
        cot_seen.astype(jnp.bfloat16).reshape(block_count, chip_count, block_seen, model_width),
        "dp",
        split_axis=0,
        concat_axis=2,
        tiled=True,
    )
    result_grad = returned.reshape(row_count, model_width).astype(jnp.float32)
    qkv_back, out_back, up_back, down_back = qkv_full, out_full, up_full, down_full
    feed_grad = result_grad.astype(jnp.bfloat16)
    down_bias_grad = jnp.sum(feed_grad.astype(jnp.float32), axis=0)
    down_grad = contract_rows(active_low, feed_grad)
    active_grad = contract_cols(feed_grad, down_back)
    gate_grad = pull_gelu(active_grad)[0].astype(jnp.bfloat16)
    up_bias_grad = jnp.sum(gate_grad.astype(jnp.float32), axis=0)
    up_grad = contract_rows(normed_two_low, gate_grad)
    normed_two_grad = contract_cols(gate_grad, up_back)
    middle_part, gain_two_grad, shift_two_grad = pull_two(normed_two_grad)
    middle_grad = result_grad + middle_part
    branch_grad = middle_grad.astype(jnp.bfloat16)
    out_bias_grad = jnp.sum(branch_grad.astype(jnp.float32), axis=0)
    out_grad = contract_rows(context, branch_grad)
    context_grad = contract_cols(branch_grad, out_back).astype(jnp.bfloat16)
    context_grad = context_grad.reshape(chip_count, seq_len, head_count, HD)
    again_scores = (
        jnp.einsum("cqhe,ckhe->chqk", queries, key_rows, preferred_element_type=jnp.float32)
        * score_scale
    )
    attn_full = jnp.exp(again_scores - log_total)
    attn_again = attn_full.astype(jnp.bfloat16)
    value_grad = jnp.einsum(
        "chqk,cqhe->ckhe", attn_again, context_grad, preferred_element_type=jnp.float32
    )
    prob_grad = jnp.einsum(
        "cqhe,ckhe->chqk", context_grad, values, preferred_element_type=jnp.float32
    )
    inner_sum = jnp.sum(attn_full * prob_grad, axis=-1, keepdims=True)
    score_grad = (attn_full * (prob_grad - inner_sum) * score_scale).astype(jnp.bfloat16)
    query_grad = jnp.einsum(
        "chqk,ckhe->cqhe", score_grad, key_rows, preferred_element_type=jnp.float32
    )
    key_grad = jnp.einsum(
        "chqk,cqhe->ckhe", score_grad, queries, preferred_element_type=jnp.float32
    )
    mixed_grad = jnp.stack([query_grad, key_grad, value_grad], axis=2).astype(jnp.bfloat16)
    mixed_grad = mixed_grad.reshape(row_count, 3 * model_width)
    value_bias_grad = jnp.sum(mixed_grad[:, 2 * model_width :].astype(jnp.float32), axis=0)
    qkv_grad = contract_rows(normed_low, mixed_grad)
    normed_grad = contract_cols(mixed_grad, qkv_back)
    input_part, gain_one_grad, shift_one_grad = pull_one(normed_grad)
    tokens_grad = (middle_grad + input_part).reshape(1, chip_count, seq_len, model_width)
    vector_grad = jnp.concatenate(
        [
            jnp.stack(
                [
                    gain_one_grad,
                    shift_one_grad,
                    value_bias_grad,
                    out_bias_grad,
                    gain_two_grad,
                    shift_two_grad,
                ]
            ),
            up_bias_grad.reshape(-1, model_width),
            jnp.stack([down_bias_grad, mask_grad]),
        ],
        axis=0,
    )
    vector_parts = vector_grad.reshape(group_axis, vec_rows, block_count, vec_cols)
    vector_parts = vector_parts.transpose(2, 0, 1, 3).reshape(device_count, vec_rows, vec_cols)
    vector_parts = lax.all_to_all(vector_parts, both, split_axis=0, concat_axis=0, tiled=True)
    shares = (
        scatter_sum(qkv_grad),
        scatter_sum(out_grad),
        scatter_sum(up_grad),
        scatter_sum(down_grad),
        jnp.sum(vector_parts, axis=0),
    )
    squares = (
        jnp.sum(shares[0] * shares[0])
        + jnp.sum(shares[1] * shares[1])
        + jnp.sum(shares[2] * shares[2])
    )
    squares = squares + jnp.sum(shares[3] * shares[3]) + jnp.sum(shares[4] * shares[4])
    square_parts = jnp.broadcast_to(squares, (device_count, 1))
    grad_total = jnp.sum(lax.all_to_all(square_parts, both, split_axis=0, concat_axis=0, tiled=True))
    grad_norm = jnp.sqrt(grad_total)
    tokens_all = lax.axis_size("dp") * lax.axis_size("fsdp") * chip_count * seq_len
    threshold = 0.05 * model_width * math.sqrt(tokens_all)
    clip_factor = jnp.minimum(1.0, threshold / grad_norm)
    ff_width = up_weight.shape[1] * lax.axis_size("fsdp")
    qkv_out = adam_step(
        qkv_weight,
        shares[0],
        qkv_first,
        qkv_second,
        clip_factor,
        0.6 / math.sqrt(model_width),
        0.05,
    )
    out_out = adam_step(
        out_weight,
        shares[1],
        out_first,
        out_second,
        clip_factor,
        0.6 / math.sqrt(model_width // 32),
        0.05,
    )
    up_out = adam_step(
        up_weight, shares[2], up_first, up_second, clip_factor, 0.6 / math.sqrt(model_width), 0.05
    )
    down_out = adam_step(
        down_weight,
        shares[3],
        down_first,
        down_second,
        clip_factor,
        0.6 / math.sqrt(ff_width),
        0.05,
    )
    vec_out = adam_step(vectors, shares[4], vector_first, vector_second, clip_factor, 0.45, 0.0)
    return (
        full_layout,
        tokens_grad,
        qkv_out[0],
        qkv_out[1],
        qkv_out[2],
        qkv_out[2].astype(jnp.bfloat16),
        out_out[0],
        out_out[1],
        out_out[2],
        out_out[2].astype(jnp.bfloat16),
        up_out[0],
        up_out[1],
        up_out[2],
        up_out[2].astype(jnp.bfloat16),
        down_out[0],
        down_out[1],
        down_out[2],
        down_out[2].astype(jnp.bfloat16),
        vec_out[0],
        vec_out[1],
        vec_out[2],
        grad_norm,
    )


def solution(mesh):
    in_specs = (
        P("fsdp", "dp", None, None),
        P("fsdp", None, None),
        P("fsdp", None, "dp", None),
        P("dp", "fsdp"),
        P("dp", "fsdp"),
        P("dp", "fsdp"),
        P("dp", "fsdp"),
        P("fsdp", "dp"),
        P("dp", "fsdp"),
        P("dp", "fsdp"),
        P("dp", "fsdp"),
        P("dp", "fsdp"),
        P("fsdp", "dp"),
        P("dp", "fsdp"),
        P("dp", "fsdp"),
        P("dp", "fsdp"),
        P("dp", "fsdp"),
        P("fsdp", "dp"),
    )
    out_specs = (
        P("fsdp", None, "dp", None),
        P("fsdp", "dp", None, None),
        P("dp", "fsdp"),
        P("dp", "fsdp"),
        P("dp", "fsdp"),
        P("dp", "fsdp"),
        P("dp", "fsdp"),
        P("dp", "fsdp"),
        P("dp", "fsdp"),
        P("dp", "fsdp"),
        P("dp", "fsdp"),
        P("dp", "fsdp"),
        P("dp", "fsdp"),
        P("dp", "fsdp"),
        P("dp", "fsdp"),
        P("dp", "fsdp"),
        P("dp", "fsdp"),
        P("dp", "fsdp"),
        P("fsdp", "dp"),
        P("fsdp", "dp"),
        P("fsdp", "dp"),
        P(),
    )
    return jax.shard_map(
        on_device, mesh=mesh, in_specs=in_specs, out_specs=out_specs, check_vma=False
    )
```

```python
import functools
import math

import jax
import jax.numpy as jnp
from jax import lax
from jax.experimental import pallas as pl
from jax.experimental.pallas import tpu as pltpu
from jax.sharding import PartitionSpec as P

HD = 64
STEP = 10
F32 = jnp.float32
BF16 = jnp.bfloat16
VMEM_BYTES = 60 * 1024 * 1024


def params_for(**more):
    return pltpu.CompilerParams(vmem_limit_bytes=VMEM_BYTES, **more)


def dot_nn(left, right):
    return lax.dot_general(left, right, (((1,), (0,)), ((), ())), preferred_element_type=F32)


def dot_nt(left, right):
    return lax.dot_general(left, right, (((1,), (1,)), ((), ())), preferred_element_type=F32)


def dot_tn(left, right):
    return lax.dot_general(left, right, (((0,), (0,)), ((), ())), preferred_element_type=F32)


def norm_parts(values):
    center = values - jnp.mean(values, axis=-1, keepdims=True)
    spread = jnp.mean(center * center, axis=-1, keepdims=True)
    factor = lax.rsqrt(spread + 1e-05)
    return center * factor, factor


def norm_back(grad, hat, factor, gain):
    scaled = grad * gain
    inner = jnp.mean(scaled * hat, axis=-1, keepdims=True)
    return factor * (scaled - jnp.mean(scaled, axis=-1, keepdims=True) - hat * inner)


def gelu_pair(gate):
    size = jnp.abs(gate) * (0.5**0.5)
    ratio = 1.0 / (1.0 + 0.3275911 * size)
    bell = jnp.exp(-size * size)
    tail = ratio * (
        0.254829592
        + ratio * (-0.284496736 + ratio * (1.421413741 + ratio * (-1.453152027 + ratio * 1.061405429)))
    )
    half = 0.5 * tail * bell
    cdf = jnp.where(gate >= 0, 1.0 - half, half)
    return gate * cdf, cdf + gate * (bell * (0.5 / math.pi) ** 0.5)


def load_grid(table, refs, me_ref, dest, sems, rows, first=0):
    copies = []
    for ref, places in zip(refs, table):
        for pos, (rel_d, rel_f, off) in enumerate(places):
            d = rel_d ^ me_ref[0]
            f = rel_f ^ me_ref[1]
            height = ref.shape[1]
            start = pl.multiple_of(d * rows + off, 16)
            copy = pltpu.make_async_copy(
                ref.at[pos], dest.at[f, pl.ds(start, height)], sems.at[first + len(copies)]
            )
            copy.start()
            copies.append(copy)
    return copies


def load_down(table, refs, me_ref, dest, sems, share, first=0):
    copies = []
    for ref, places in zip(refs, table):
        for pos, (rel_d, rel_f, off) in enumerate(places):
            if share is None:
                pairs = [(ref.at[pos], dest)]
            else:
                half, wide = share
                d = rel_d ^ me_ref[0]
                f = rel_f ^ me_ref[1]
                lane = pl.multiple_of(d * wide, 128)
                pairs = []
                for k in range(2):
                    row = pl.multiple_of(f * (2 * half) + k * half + off, 16)
                    pairs.append(
                        (
                            ref.at[pos, :, pl.ds(k * wide, wide)],
                            dest.at[pl.ds(row, ref.shape[1]), pl.ds(lane, wide)],
                        )
                    )
            for src, dst in pairs:
                copy = pltpu.make_async_copy(src, dst, sems.at[first + len(copies)])
                copy.start()
                copies.append(copy)
    return copies


def any_specs(count):
    return [pl.BlockSpec(memory_space=pl.ANY)] * count


SMEM_SPEC = pl.BlockSpec(memory_space=pltpu.SMEM)


def full_spec(shape):
    return pl.BlockSpec(shape, lambda i: (0,) * len(shape))


def attend_body(table, rows, heads, wide, *refs):
    n = len(table)
    me_ref, x_ref, vec_ref, bias_ref = refs[:4]
    w_refs = refs[4 : 4 + n]
    normed_ref, mixed_ref, probs_ref, context_ref, weight, sems = refs[4 + n :]
    count = sum(len(t) for t in table)

    @pl.when(pl.program_id(0) == 0)
    def _():
        for copy in load_grid(table, w_refs, me_ref, weight, sems, rows):
            copy.wait()

    hat, _ = norm_parts(x_ref[0].astype(F32))
    normed = (hat * vec_ref[0:1, :] + vec_ref[1:2, :]).astype(BF16)
    normed_ref[0] = normed
    shares = weight.shape[0]
    for f in range(shares):
        mixed = dot_nn(normed, weight[f, :, :wide]) + bias_ref[f]
        mixed_ref[f, 0] = mixed.astype(BF16)
    per = wide // HD

    def part(which, head):
        g = which * heads + head
        return mixed_ref[g // per, 0, :, (g % per) * HD : (g % per + 1) * HD]

    for head in range(heads):
        scores = dot_nt(part(0, head) * jnp.asarray(HD ** (-0.5), BF16), part(1, head))
        peak = jnp.max(scores, axis=-1, keepdims=True)
        expo = jnp.exp(scores - peak)
        total = jnp.sum(expo, axis=-1, keepdims=True)
        probs = (expo * (1.0 / total)).astype(BF16)
        probs_ref[0, head] = probs
        context_ref[0, :, head * HD : (head + 1) * HD] = dot_nn(probs, part(2, head)).astype(BF16)


def attend_forward(me, x, vec, bias, table, arrays, rows, wide):
    chips, seq, model = x.shape
    heads = model // HD
    shares = bias.shape[0]
    cols = arrays[0].shape[-1]
    count = sum(len(t) for t in table)
    return pl.pallas_call(
        functools.partial(attend_body, table, rows, heads, wide),
        grid=(chips,),
        in_specs=[
            SMEM_SPEC,
            pl.BlockSpec((1, seq, model), lambda i: (i, 0, 0)),
            full_spec(vec.shape),
            full_spec(bias.shape),
        ]
        + any_specs(len(arrays)),
        out_specs=[
            pl.BlockSpec((1, seq, model), lambda i: (i, 0, 0)),
            pl.BlockSpec((shares, 1, seq, wide), lambda i: (0, i, 0, 0)),
            pl.BlockSpec((1, heads, seq, seq), lambda i: (i, 0, 0, 0)),
            pl.BlockSpec((1, seq, model), lambda i: (i, 0, 0)),
        ],
        out_shape=[
            jax.ShapeDtypeStruct((chips, seq, model), BF16),
            jax.ShapeDtypeStruct((shares, chips, seq, wide), BF16),
            jax.ShapeDtypeStruct((chips, heads, seq, seq), BF16),
            jax.ShapeDtypeStruct((chips, seq, model), BF16),
        ],
        scratch_shapes=[
            pltpu.VMEM((shares, model, cols), BF16),
            pltpu.SemaphoreType.DMA((count,)),
        ],
        compiler_params=params_for(),
        name="attend_forward",
    )(me, x, vec, bias, *arrays)


def feed_up_body(q_table, u_table, rows, wide, *refs):
    nq, nu = len(q_table), len(u_table)
    me_ref, x_ref, context_ref, vec_ref, bias_ref = refs[:5]
    q_refs = refs[5 : 5 + nq]
    u_refs = refs[5 + nq : 5 + nq + nu]
    (
        middle_ref,
        normed_ref,
        active_ref,
        slope_ref,
        out_ref,
        packed,
        up,
        sems,
    ) = refs[5 + nq + nu :]
    count = sum(len(t) for t in q_table)
    shares, _, cols = packed.shape
    slim = cols - wide

    @pl.when(pl.program_id(0) == 0)
    def _():
        first = load_grid(q_table, q_refs, me_ref, packed, sems, rows)
        second = load_grid(u_table, u_refs, me_ref, up, sems, rows, first=count)
        for copy in first:
            copy.wait()
        for f in range(shares):
            out_ref[:, f * slim : (f + 1) * slim] = packed[f, :, wide:]
        for copy in second:
            copy.wait()

    branch = dot_nn(context_ref[0], out_ref[...])
    middle = x_ref[0].astype(F32) + branch + vec_ref[3:4, :]
    middle_ref[0] = middle
    hat, _ = norm_parts(middle)
    normed = (hat * vec_ref[4:5, :] + vec_ref[5:6, :]).astype(BF16)
    normed_ref[0] = normed
    span = up.shape[2]
    for f in range(shares):
        gate = dot_nn(normed, up[f]) + bias_ref[:, f * span : (f + 1) * span]
        active, slope = gelu_pair(gate)
        active_ref[0, :, f * span : (f + 1) * span] = active.astype(BF16)
        slope_ref[0, :, f * span : (f + 1) * span] = slope.astype(BF16)


def feed_up(me, x, context, vec, bias, q_table, q_arrays, u_table, u_arrays, rows, wide):
    chips, seq, model = x.shape
    ff = bias.shape[1]
    cols = q_arrays[0].shape[-1]
    span = u_arrays[0].shape[-1]
    shares = ff // span
    count = sum(len(t) for t in q_table) + sum(len(t) for t in u_table)
    tile = lambda w: pl.BlockSpec((1, seq, w), lambda i: (i, 0, 0))
    return pl.pallas_call(
        functools.partial(feed_up_body, q_table, u_table, rows, wide),
        grid=(chips,),
        in_specs=[SMEM_SPEC, tile(model), tile(model), full_spec(vec.shape), full_spec(bias.shape)]
        + any_specs(len(q_arrays) + len(u_arrays)),
        out_specs=[tile(model), tile(model), tile(ff), tile(ff), full_spec((model, model))],
        out_shape=[
            jax.ShapeDtypeStruct((chips, seq, model), F32),
            jax.ShapeDtypeStruct((chips, seq, model), BF16),
            jax.ShapeDtypeStruct((chips, seq, ff), BF16),
            jax.ShapeDtypeStruct((chips, seq, ff), BF16),
            jax.ShapeDtypeStruct((model, model), BF16),
        ],
        scratch_shapes=[
            pltpu.VMEM((shares, model, cols), BF16),
            pltpu.VMEM((shares, model, span), BF16),
            pltpu.SemaphoreType.DMA((count,)),
        ],
        compiler_params=params_for(),
        name="feed_up",
    )(me, x, context, vec, bias, *q_arrays, *u_arrays)


def feed_down_body(u_table, d_table, rows, share, *refs):
    nu, nd = len(u_table), len(d_table)
    me_ref, grad_ref, middle_ref, active_ref, slope_ref, vec_ref, out_ref = refs[:7]
    u_refs = refs[7 : 7 + nu]
    d_refs = refs[7 + nu : 7 + nu + nd]
    (
        result_ref,
        gate_grad_ref,
        middle_grad_ref,
        branch_grad_ref,
        context_grad_ref,
        sums_ref,
        bias_sums_ref,
        up,
        down,
        sems,
    ) = refs[7 + nu + nd :]
    count = sum(len(t) for t in u_table)
    shares, model, span = up.shape
    step = pl.program_id(0)

    @pl.when(step == 0)
    def _():
        first = load_grid(u_table, u_refs, me_ref, up, sems, rows)
        second = load_down(d_table, d_refs, me_ref, down, sems, share, first=count)
        sums_ref[...] = jnp.zeros_like(sums_ref)
        bias_sums_ref[...] = jnp.zeros_like(bias_sums_ref)
        for copy in first + second:
            copy.wait()

    seq = middle_ref.shape[1]
    middle = middle_ref[0]
    feed_grad = grad_ref[:, 0].reshape(seq, model)
    result = middle + dot_nt(active_ref[0], down[...]) + vec_ref[10:11, :]
    result_ref[:, 0] = result.astype(BF16).reshape(result_ref.shape[0], -1, model)
    normed_grad = jnp.zeros((seq, model), F32)
    for f in range(shares):
        lanes = slice(f * span, (f + 1) * span)
        active_grad = dot_nn(feed_grad, down[:, lanes])
        gate_grad = (active_grad * slope_ref[0, :, lanes].astype(F32)).astype(BF16)
        gate_grad_ref[0, :, lanes] = gate_grad
        bias_sums_ref[:, lanes] += jnp.sum(gate_grad.astype(F32), axis=0, keepdims=True)
        normed_grad += dot_nt(gate_grad, up[f])
    hat, factor = norm_parts(middle)
    gain = vec_ref[4:5, :]
    grad_full = feed_grad.astype(F32)
    middle_grad = grad_full + norm_back(normed_grad, hat, factor, gain)
    middle_grad_ref[0] = middle_grad
    branch_grad = middle_grad.astype(BF16)
    branch_grad_ref[0] = branch_grad
    context_grad_ref[0] = dot_nt(branch_grad, out_ref[...]).astype(BF16)
    sums_ref[0:1, :] += jnp.sum(branch_grad.astype(F32), axis=0, keepdims=True)
    sums_ref[1:2, :] += jnp.sum(normed_grad * hat, axis=0, keepdims=True)
    sums_ref[2:3, :] += jnp.sum(normed_grad, axis=0, keepdims=True)
    sums_ref[3:4, :] += jnp.sum(grad_full, axis=0, keepdims=True)


def feed_down(
    me, grad, middle, active, slope, vec, out_whole, u_table, u_arrays, d_table, d_arrays, rows, share
):
    chips, seq, model = middle.shape
    ff = active.shape[2]
    blocks, _, seen, _ = grad.shape
    span = u_arrays[0].shape[-1]
    shares = ff // span
    count = sum(len(t) for t in u_table) + 2 * sum(len(t) for t in d_table)
    tile = lambda w: pl.BlockSpec((1, seq, w), lambda i: (i, 0, 0))
    spread = pl.BlockSpec((blocks, 1, seen, model), lambda i: (0, i, 0, 0))
    return pl.pallas_call(
        functools.partial(feed_down_body, u_table, d_table, rows, share),
        grid=(chips,),
        in_specs=[
            SMEM_SPEC,
            spread,
            tile(model),
            tile(ff),
            tile(ff),
            full_spec(vec.shape),
            full_spec(out_whole.shape),
        ]
        + any_specs(len(u_arrays) + len(d_arrays)),
        out_specs=[
            spread,
            tile(ff),
            tile(model),
            tile(model),
            tile(model),
            full_spec((8, model)),
            full_spec((1, ff)),
        ],
        out_shape=[
            jax.ShapeDtypeStruct(grad.shape, BF16),
            jax.ShapeDtypeStruct((chips, seq, ff), BF16),
            jax.ShapeDtypeStruct((chips, seq, model), F32),
            jax.ShapeDtypeStruct((chips, seq, model), BF16),
            jax.ShapeDtypeStruct((chips, seq, model), BF16),
            jax.ShapeDtypeStruct((8, model), F32),
            jax.ShapeDtypeStruct((1, ff), F32),
        ],
        scratch_shapes=[
            pltpu.VMEM((shares, model, span), BF16),
            pltpu.VMEM((model, ff), BF16),
            pltpu.SemaphoreType.DMA((count,)),
        ],
        compiler_params=params_for(),
        name="feed_down",
    )(me, grad, middle, active, slope, vec, out_whole, *u_arrays, *d_arrays)


def attend_back_body(heads, mixed_ref, probs_ref, context_ref, grad_ref, mixed_grad_ref, sums_ref):
    wide = mixed_ref.shape[3]
    per = wide // HD

    @pl.when(pl.program_id(0) == 0)
    def _():
        sums_ref[...] = jnp.zeros_like(sums_ref)

    def place(which, head):
        g = which * heads + head
        return g // per, slice((g % per) * HD, (g % per + 1) * HD)

    def part(which, head):
        f, lanes = place(which, head)
        return mixed_ref[f, 0, :, lanes]

    for head in range(heads):
        lanes = slice(head * HD, (head + 1) * HD)
        out_grad = grad_ref[0, :, lanes]
        probs = probs_ref[0, head]
        query, key, value = part(0, head), part(1, head), part(2, head)
        value_grad = dot_tn(probs, out_grad).astype(BF16)
        prob_grad = dot_nt(out_grad, value)
        inner = jnp.sum(
            out_grad.astype(F32) * context_ref[0, :, lanes].astype(F32), axis=-1, keepdims=True
        )
        score_grad = (probs.astype(F32) * ((prob_grad - inner) * HD ** (-0.5))).astype(BF16)
        grads = (dot_nn(score_grad, key).astype(BF16), dot_tn(score_grad, query).astype(BF16), value_grad)
        for which in range(3):
            f, spot = place(which, head)
            mixed_grad_ref[f, 0, :, spot] = grads[which]
        sums_ref[0:1, lanes] += jnp.sum(value_grad.astype(F32), axis=0, keepdims=True)


def attend_back(mixed, probs, context, context_grad):
    shares, chips, seq, wide = mixed.shape
    model = context.shape[2]
    heads = model // HD
    tile = pl.BlockSpec((1, seq, model), lambda i: (i, 0, 0))
    packed = pl.BlockSpec((shares, 1, seq, wide), lambda i: (0, i, 0, 0))
    return pl.pallas_call(
        functools.partial(attend_back_body, heads),
        grid=(chips,),
        in_specs=[packed, pl.BlockSpec((1, heads, seq, seq), lambda i: (i, 0, 0, 0)), tile, tile],
        out_specs=[packed, full_spec((8, model))],
        out_shape=[
            jax.ShapeDtypeStruct(mixed.shape, BF16),
            jax.ShapeDtypeStruct((8, model), F32),
        ],
        compiler_params=params_for(),
        name="attend_back",
    )(mixed, probs, context, context_grad)


def tokens_back_body(table, rows, *refs):
    n = len(table)
    me_ref, x_ref, grad_ref, mixed_grad_ref, vec_ref = refs[:5]
    w_refs = refs[5 : 5 + n]
    tokens_ref, sums_ref, weight, sems = refs[5 + n :]
    wide = mixed_grad_ref.shape[3]

    @pl.when(pl.program_id(0) == 0)
    def _():
        sums_ref[...] = jnp.zeros_like(sums_ref)
        for copy in load_grid(table, w_refs, me_ref, weight, sems, rows):
            copy.wait()

    normed_grad = dot_nt(mixed_grad_ref[0, 0], weight[0, :, :wide])
    for f in range(1, weight.shape[0]):
        normed_grad += dot_nt(mixed_grad_ref[f, 0], weight[f, :, :wide])
    hat, factor = norm_parts(x_ref[0].astype(F32))
    tokens_ref[0] = grad_ref[0] + norm_back(normed_grad, hat, factor, vec_ref[0:1, :])
    sums_ref[0:1, :] += jnp.sum(normed_grad * hat, axis=0, keepdims=True)
    sums_ref[1:2, :] += jnp.sum(normed_grad, axis=0, keepdims=True)


def tokens_back(me, x, middle_grad, mixed_grad, vec, table, arrays, rows):
    chips, seq, model = x.shape
    shares, _, _, wide = mixed_grad.shape
    cols = arrays[0].shape[-1]
    count = sum(len(t) for t in table)
    tile = pl.BlockSpec((1, seq, model), lambda i: (i, 0, 0))
    return pl.pallas_call(
        functools.partial(tokens_back_body, table, rows),
        grid=(chips,),
        in_specs=[
            SMEM_SPEC,
            tile,
            tile,
            pl.BlockSpec((shares, 1, seq, wide), lambda i: (0, i, 0, 0)),
            full_spec(vec.shape),
        ]
        + any_specs(len(arrays)),
        out_specs=[tile, full_spec((8, model))],
        out_shape=[
            jax.ShapeDtypeStruct((chips, seq, model), F32),
            jax.ShapeDtypeStruct((8, model), F32),
        ],
        scratch_shapes=[
            pltpu.VMEM((shares, model, cols), BF16),
            pltpu.SemaphoreType.DMA((count,)),
        ],
        compiler_params=params_for(),
        name="tokens_back",
    )(me, x, middle_grad, mixed_grad, vec, *arrays)


def place_of(order, rel_d, rel_f):
    pos = 0
    for is_dp, value in order:
        bit = ((rel_d if is_dp else rel_f) // value) % 2
        pos = pos * 2 + bit
    return pos


def up_grad_body(order, rows, me_ref, left_ref, right_ref, out_ref):
    f = pl.program_id(0)
    grad = dot_tn(left_ref[...], right_ref[...])
    if order is None:
        out_ref[f] = grad.astype(BF16)
    else:
        for d in range(grad.shape[0] // rows):
            pos = place_of(order, d ^ me_ref[0], f ^ me_ref[1])
            out_ref[pos] = grad[d * rows : (d + 1) * rows].astype(BF16)


def up_grad_blocks(me, left, right, order, rows, shares):
    tokens, model = left.shape
    span = right.shape[1] // shares
    shape = (shares, model, span) if order is None else (shares * model // rows, rows, span)
    return pl.pallas_call(
        functools.partial(up_grad_body, order, rows),
        grid=(shares,),
        in_specs=[
            SMEM_SPEC,
            full_spec(left.shape),
            pl.BlockSpec((tokens, span), lambda i: (0, i)),
        ],
        out_specs=full_spec(shape),
        out_shape=jax.ShapeDtypeStruct(shape, BF16),
        compiler_params=params_for(),
        name="up_grad",
    )(me, left, right)


def down_grad_body(order, half, me_ref, grad_ref, active_ref, out_ref):
    d = pl.program_id(0)
    grad_seen = grad_ref[...]
    whole = dot_tn(grad_seen, active_ref[...])
    if order is None:
        out_ref[...] = whole.astype(BF16)
    else:
        wide = whole.shape[1]
        for f in range(whole.shape[0] // (2 * half)):
            pos = place_of(order, d ^ me_ref[0], f ^ me_ref[1])
            for k in range(2):
                start = (2 * f + k) * half
                out_ref[pos, :, k * wide : (k + 1) * wide] = whole[start : start + half].astype(BF16)


def down_grad_blocks(me, grad, active, order, half, wide):
    tokens, model = grad.shape
    ff = active.shape[1]
    if order is None:
        steps, width, shape = 4, ff // 4, (model, ff)
        out_spec = pl.BlockSpec((model, width), lambda i: (0, i))
    else:
        steps, width = ff // wide, wide
        shape = (steps * model // (2 * half), half, 2 * wide)
        out_spec = full_spec(shape)
    return pl.pallas_call(
        functools.partial(down_grad_body, order, half),
        grid=(steps,),
        in_specs=[
            SMEM_SPEC,
            full_spec(grad.shape),
            pl.BlockSpec((tokens, width), lambda i: (0, i)),
        ],
        out_specs=out_spec,
        out_shape=jax.ShapeDtypeStruct(shape, BF16),
        compiler_params=params_for(),
        name="down_grad",
    )(me, grad, active)


def qkv_grad_body(order, rows, me_ref, normed_ref, mixed_grad_ref, context_ref, branch_ref, out_ref, slots):
    f = pl.program_id(0)
    shares = slots.shape[0]
    wide = mixed_grad_ref.shape[2]
    slim = slots.shape[2]

    @pl.when(f == 0)
    def _():
        whole = dot_tn(context_ref[...], branch_ref[...]).astype(BF16)
        for k in range(shares):
            slots[k] = whole[:, k * slim : (k + 1) * slim]

    grad = dot_tn(normed_ref[...], mixed_grad_ref[0]).astype(BF16)
    side = slots[f]
    if order is None:
        out_ref[f, :, :wide] = grad
        out_ref[f, :, wide:] = side
    else:
        for d in range(grad.shape[0] // rows):
            pos = place_of(order, d ^ me_ref[0], f ^ me_ref[1])
            out_ref[pos, :, :wide] = grad[d * rows : (d + 1) * rows]
            out_ref[pos, :, wide:] = side[d * rows : (d + 1) * rows]


def qkv_grad_blocks(me, normed, mixed_grad, context, branch_grad, order, rows):
    tokens, model = normed.shape
    shares, _, wide = mixed_grad.shape
    slim = model // shares
    cols = wide + slim
    shape = (shares, model, cols) if order is None else (shares * model // rows, rows, cols)
    return pl.pallas_call(
        functools.partial(qkv_grad_body, order, rows),
        grid=(shares,),
        in_specs=[
            SMEM_SPEC,
            full_spec(normed.shape),
            pl.BlockSpec((1, tokens, wide), lambda i: (i, 0, 0)),
            full_spec(context.shape),
            full_spec(branch_grad.shape),
        ],
        out_specs=full_spec(shape),
        out_shape=jax.ShapeDtypeStruct(shape, BF16),
        scratch_shapes=[pltpu.VMEM((shares, model, slim), BF16)],
        compiler_params=params_for(),
        name="qkv_grad",
    )(me, normed, mixed_grad, context, branch_grad)


DP, FSDP = "dp", "fsdp"


def swap(value, axis, bit):
    size = lax.axis_size(axis)
    return lax.ppermute(value, axis, [(i, i ^ bit) for i in range(size)])


def grow(value, step, dim=0):
    return jnp.concatenate([value, swap(value, *step)], axis=dim)


def add_low(left, right):
    return (left.astype(F32) + right.astype(F32)).astype(BF16)


def fold(value, step, dim=0, low=True):
    keep = lax.index_in_dim(value, 0, dim, keepdims=False)
    send = lax.index_in_dim(value, 1, dim, keepdims=False)
    arrived = swap(send, *step)
    if low:
        return add_low(keep, arrived)
    return keep.astype(F32) + arrived.astype(F32)


def rel_table(steps, last, off):
    places = []
    for pos in range(2 ** len(steps)):
        rel = {DP: 0, FSDP: 0}
        for k, (axis, bit) in enumerate(steps):
            if (pos >> k) & 1:
                rel[axis] ^= bit
        if last is not None:
            rel[last[0]] ^= last[1]
        places.append((rel[DP], rel[FSDP], off))
    return tuple(places)


CORE, XS, YS, Z_NEAR, Z_FAR = (FSDP, 1), (FSDP, 2), (DP, 1), (DP, 2), (DP, 4)
XY = [Z_FAR, Z_NEAR, XS, YS]
YX = [Z_FAR, Z_NEAR, YS, XS]


def grow_end(value, second):
    for step in second:
        value = grow(value, step)
    return value, swap(value, *CORE)


def order_of(steps):
    return [(axis == DP, bit) for axis, bit in steps]


def adam_step(weight, gradient, first_mom, second, clip_factor, step_rate, decay_rate):
    scaled = gradient * clip_factor
    first_new = 0.5 * first_mom + 0.5 * scaled
    second_new = 0.5 * second + 0.5 * scaled * scaled
    correction = 1.0 - 0.5**STEP
    update = first_new / correction / (jnp.sqrt(second_new / correction) + 1e-08)
    return (first_new, second_new, weight - step_rate * (update + decay_rate * weight))


def on_device(
    tokens,
    visible_index,
    cotangent,
    qkv_weight,
    out_weight,
    up_weight,
    down_weight,
    vectors,
    qkv_first,
    out_first,
    up_first,
    down_first,
    vector_first,
    qkv_second,
    out_second,
    up_second,
    down_second,
    vector_second,
):
    _, chip_count, seq_len, model_width = tokens.shape
    dp_size, fsdp_size = lax.axis_size(DP), lax.axis_size(FSDP)
    device_count = dp_size * fsdp_size
    both = (DP, FSDP)
    block_count = dp_size
    block_seen = seq_len // block_count
    block_len = cotangent.shape[2]
    chips_group = chip_count * block_count
    rows, wide = qkv_weight.shape
    slim = out_weight.shape[1]
    span = up_weight.shape[1]
    ff_width = span * fsdp_size
    half = slim // 2
    tall = down_weight.shape[0]
    folded = (dp_size, fsdp_size) == (8, 4)

    share_q = jnp.concatenate([qkv_weight, out_weight], axis=1).astype(BF16)
    share_u = up_weight.astype(BF16)
    down_turned = down_weight.astype(BF16).T

    vec_rows, vec_cols = vectors.shape
    vector_copies = jnp.broadcast_to(vectors.astype(BF16), (device_count, vec_rows, vec_cols))
    vec = lax.all_to_all(vector_copies, both, split_axis=0, concat_axis=0, tiled=True)
    vec = vec.reshape(dp_size, fsdp_size, vec_rows, vec_cols).transpose(1, 2, 0, 3)
    vec = vec.reshape(fsdp_size * vec_rows, model_width).astype(F32)

    if folded:
        me = jnp.stack([lax.axis_index(DP), lax.axis_index(FSDP)]).astype(jnp.int32)
        share_d = jnp.concatenate([down_turned[:half], down_turned[half:]], axis=1)
        cur = grow(grow(share_q[None], Z_FAR), Z_NEAR)
        cut = rows // 2
        q_arrays = grow_end(cur[:, :cut], [XS, YS]) + grow_end(cur[:, cut:], [YS, XS])
        q_table = (
            rel_table(XY, None, 0),
            rel_table(XY, CORE, 0),
            rel_table(YX, None, cut),
            rel_table(YX, CORE, cut),
        )
        cur = jnp.stack([share_u, share_d])[:, None]
        cur = grow(grow(cur, Z_FAR, 1), Z_NEAR, 1)
        u_arrays = grow_end(cur[0], [XS, YS])
        d_arrays = grow_end(cur[1], [YS, XS])
        u_table = (rel_table(XY, None, 0), rel_table(XY, CORE, 0))
        d_table = (rel_table(YX, None, 0), rel_table(YX, CORE, 0))
        order_d = [CORE, XS, YS, Z_NEAR, Z_FAR]
        order_u = [CORE, YS, XS, Z_NEAR, Z_FAR]
        q_order, u_order, d_order = order_of(order_d), order_of(order_u), order_of(order_d)
        down_share = (half, tall)
    else:
        me = jnp.zeros((2,), jnp.int32)

        def gather_whole(share):
            whole = lax.all_gather(share, both, axis=0, tiled=False)
            whole = whole.reshape((dp_size, fsdp_size) + share.shape).transpose(1, 0, 2, 3)
            return whole.reshape(fsdp_size, dp_size * share.shape[0], share.shape[1])

        q_arrays = (gather_whole(share_q),)
        u_arrays = (gather_whole(share_u),)
        down_whole = lax.all_gather(down_turned, both, axis=0, tiled=False)
        down_whole = down_whole.reshape(dp_size, fsdp_size, slim, tall).transpose(1, 2, 0, 3)
        d_arrays = (down_whole.reshape(1, model_width, ff_width),)
        q_table = u_table = (tuple((0, f, 0) for f in range(fsdp_size)),)
        d_table = (((0, 0, 0),),)
        q_order = u_order = d_order = None
        down_share = None

    my_block = lax.axis_index(DP)
    places = visible_index[0].reshape(chips_group, block_count, block_seen)
    places = lax.dynamic_index_in_dim(places, my_block, 1, keepdims=False) - my_block * block_len
    slot_ids = lax.broadcasted_iota(jnp.int32, (chips_group, block_len, block_seen), 1)
    pick = (places[:, None, :] == slot_ids).astype(BF16)
    gaps = 1.0 - jnp.sum(pick.astype(F32), axis=-1)
    cot = cotangent[0]
    cot_seen = jnp.einsum("cpv,cpd->cvd", pick, cot, preferred_element_type=F32).astype(BF16)
    cot_seen = cot_seen.reshape(block_count, chip_count, block_seen, model_width)
    mask_grad = jnp.einsum("cp,cpd->d", gaps.astype(BF16), cot, preferred_element_type=F32)
    grad = lax.all_to_all(cot_seen, DP, split_axis=0, concat_axis=0, tiled=True)
    whole_tiles = block_seen % 16 == 0
    if not whole_tiles:
        grad = grad.transpose(1, 0, 2, 3).reshape(1, chip_count, seq_len, model_width)

    x = tokens[0]
    value_bias = jnp.concatenate([jnp.zeros((2 * model_width,), F32), vec[2]])
    value_bias = value_bias.reshape(fsdp_size, 1, wide)
    up_bias = vec[6:10].reshape(1, ff_width)
    normed, mixed, probs, context = attend_forward(me, x, vec, value_bias, q_table, q_arrays, rows, wide)
    middle, normed_two, active, slope, out_whole = feed_up(
        me, x, context, vec, up_bias, q_table, q_arrays, u_table, u_arrays, rows, wide
    )
    result, gate_grad, middle_grad, branch_grad, context_grad, sums_two, up_sums = feed_down(
        me, grad, middle, active, slope, vec, out_whole, u_table, u_arrays, d_table, d_arrays, rows, down_share
    )
    token_count = chip_count * seq_len
    flat = lambda v: v.reshape(token_count, v.shape[-1])
    grad_rows = flat(grad.transpose(1, 0, 2, 3).reshape(chip_count, seq_len, model_width))
    down_blocks = down_grad_blocks(me, grad_rows, flat(active), d_order, half, tall)
    up_blocks = up_grad_blocks(me, flat(normed_two), flat(gate_grad), u_order, rows, fsdp_size)

    if not whole_tiles:
        result = result.reshape(chip_count, block_count, block_seen, model_width).transpose(1, 0, 2, 3)
    arrived = lax.all_to_all(result, DP, split_axis=0, concat_axis=0, tiled=True)
    arrived = arrived.reshape(chips_group, block_seen, model_width)

    mixed_grad, sums_value = attend_back(mixed, probs, context, context_grad)
    q_blocks = qkv_grad_blocks(
        me,
        flat(normed),
        mixed_grad.reshape(fsdp_size, token_count, wide),
        flat(context),
        flat(branch_grad),
        q_order,
        rows,
    )
    tokens_grad, sums_one = tokens_back(me, x, middle_grad, mixed_grad, vec, q_table, q_arrays, rows)

    filled = jnp.einsum("cpv,cvd->cpd", pick, arrived, preferred_element_type=F32)
    filled = filled + gaps[..., None] * vec[11]
    full_layout = filled.astype(BF16).reshape(1, chips_group, block_len, model_width)

    if folded:

        def fold_all(blocks, steps):
            for k, step in enumerate(steps):
                blocks = blocks.reshape((2, blocks.shape[0] // 2) + blocks.shape[1:])
                blocks = fold(blocks, step, 0, k < len(steps) - 1)
            return blocks[0]

        d_sum = fold_all(down_blocks, order_d)
        u_sum = fold_all(up_blocks, order_u)
        cur = fold(q_blocks.reshape((2, 16) + q_blocks.shape[1:]), CORE)
        cur = cur.reshape((2, 2, 4) + cur.shape[1:])
        left = fold(fold(cur[:, :, :, :cut], XS), YS)
        right = fold(fold(cur[:, :, :, cut:], YS, 1), XS)
        cur = jnp.concatenate([left, right], axis=1).reshape((2, 2) + share_q.shape)
        q_sum = fold(fold(cur, Z_NEAR), Z_FAR, 0, False)
        d_sum = jnp.concatenate([d_sum[:, :tall], d_sum[:, tall:]], axis=0).T
    else:

        def scatter_whole(whole):
            cols = whole.shape[2]
            pieces = whole.reshape(fsdp_size, dp_size, -1, cols).transpose(1, 0, 2, 3)
            pieces = pieces.reshape(-1, cols)
            return lax.psum_scatter(pieces, both, scatter_dimension=0, tiled=True).astype(F32)

        q_sum, u_sum = scatter_whole(q_blocks), scatter_whole(up_blocks)
        pieces = down_blocks.reshape(fsdp_size, slim, dp_size, tall).transpose(2, 0, 1, 3)
        pieces = pieces.reshape(device_count * slim, tall)
        d_sum = lax.psum_scatter(pieces, both, scatter_dimension=0, tiled=True).astype(F32).T

    vector_grad = jnp.concatenate(
        [
            sums_one[:2],
            sums_value[:1],
            sums_two[:3],
            up_sums.reshape(-1, model_width),
            sums_two[3:4],
            mask_grad[None],
        ],
        axis=0,
    )
    parts = vector_grad.reshape(fsdp_size, vec_rows, dp_size, vec_cols).transpose(2, 0, 1, 3)
    parts = parts.reshape(device_count, vec_rows, vec_cols)
    parts = lax.all_to_all(parts, both, split_axis=0, concat_axis=0, tiled=True)
    shares = (q_sum[:, :wide], q_sum[:, wide:], u_sum, d_sum, jnp.sum(parts, axis=0))
    squares = jnp.sum(q_sum * q_sum) + jnp.sum(u_sum * u_sum) + jnp.sum(d_sum * d_sum)
    squares = squares + jnp.sum(shares[4] * shares[4])
    square_parts = jnp.broadcast_to(squares, (device_count, 1))
    grad_total = jnp.sum(lax.all_to_all(square_parts, both, split_axis=0, concat_axis=0, tiled=True))
    grad_norm = jnp.sqrt(grad_total)
    tokens_all = device_count * chip_count * seq_len
    threshold = 0.05 * model_width * math.sqrt(tokens_all)
    clip = jnp.minimum(1.0, threshold / grad_norm)
    rate = 0.6 / math.sqrt(model_width)
    out_rate = 0.6 / math.sqrt(model_width // 32)
    down_rate = 0.6 / math.sqrt(ff_width)
    qkv_out = adam_step(qkv_weight, shares[0], qkv_first, qkv_second, clip, rate, 0.05)
    out_out = adam_step(out_weight, shares[1], out_first, out_second, clip, out_rate, 0.05)
    up_out = adam_step(up_weight, shares[2], up_first, up_second, clip, rate, 0.05)
    down_out = adam_step(down_weight, shares[3], down_first, down_second, clip, down_rate, 0.05)
    vec_out = adam_step(vectors, shares[4], vector_first, vector_second, clip, 0.45, 0.0)
    return (
        full_layout,
        tokens_grad[None],
        *qkv_out,
        qkv_out[2].astype(BF16),
        *out_out,
        out_out[2].astype(BF16),
        *up_out,
        up_out[2].astype(BF16),
        *down_out,
        down_out[2].astype(BF16),
        *vec_out,
        grad_norm,
    )


def solution(mesh):
    grid = P("dp", "fsdp")
    table = P("fsdp", "dp")
    weights = (grid, grid, grid, grid, table)
    in_specs = (
        P("fsdp", "dp", None, None),
        P("fsdp", None, None),
        P("fsdp", None, "dp", None),
        *weights,
        *weights,
        *weights,
    )
    out_specs = (
        P("fsdp", None, "dp", None),
        P("fsdp", "dp", None, None),
        *(grid,) * 16,
        *(table,) * 3,
        P(),
    )
    return jax.shard_map(
        on_device, mesh=mesh, in_specs=in_specs, out_specs=out_specs, check_vma=False
    )
```

```python
import functools
import math

import jax
import jax.numpy as jnp
from jax import lax
from jax.experimental import pallas as pl
from jax.experimental.pallas import tpu as pltpu
from jax.sharding import PartitionSpec as P

HD = 64
STEP = 10
F32 = jnp.float32
BF16 = jnp.bfloat16
VMEM_BYTES = 60 * 1024 * 1024


def params_for(**more):
    return pltpu.CompilerParams(vmem_limit_bytes=VMEM_BYTES, **more)


def busy_for(micros):
    return pl.CostEstimate(flops=micros * 10**9, bytes_accessed=micros * 3 * 10**6, transcendentals=0)


def dot_nn(left, right):
    return lax.dot_general(left, right, (((1,), (0,)), ((), ())), preferred_element_type=F32)


def dot_nt(left, right):
    return lax.dot_general(left, right, (((1,), (1,)), ((), ())), preferred_element_type=F32)


def dot_tn(left, right):
    return lax.dot_general(left, right, (((0,), (0,)), ((), ())), preferred_element_type=F32)


def norm_parts(values):
    center = values - jnp.mean(values, axis=-1, keepdims=True)
    spread = jnp.mean(center * center, axis=-1, keepdims=True)
    factor = lax.rsqrt(spread + 1e-05)
    return center * factor, factor


def norm_back(grad, hat, factor, gain):
    scaled = grad * gain
    inner = jnp.mean(scaled * hat, axis=-1, keepdims=True)
    return factor * (scaled - jnp.mean(scaled, axis=-1, keepdims=True) - hat * inner)


def gelu_pair(gate):
    cdf = 0.5 + 0.5 * lax.erf(gate * 0.5**0.5)
    bell = jnp.exp2(gate * gate * (-0.5 * math.log2(math.e))) * (0.5 / math.pi) ** 0.5
    return gate * cdf, cdf + gate * bell


def load_grid(table, refs, me_ref, dest, sems, rows, first=0):
    copies = []
    for ref, places in zip(refs, table):
        for pos, (rel_d, rel_f, off, turned) in enumerate(places):
            d = rel_d ^ me_ref[0] if turned else rel_d
            f = rel_f ^ me_ref[1] if turned else rel_f
            height = min(ref.shape[1], rows)
            start = pl.multiple_of(d * rows + off, 16)
            copy = pltpu.make_async_copy(
                ref.at[pos, pl.ds(0, height)], dest.at[f, pl.ds(start, height)], sems.at[first + len(copies)]
            )
            copy.start()
            copies.append(copy)
    return copies


def load_down(table, refs, me_ref, dest, sems, share, first=0):
    copies = []
    for ref, places in zip(refs, table):
        for pos, (rel_d, rel_f, off, turned) in enumerate(places):
            if share is None:
                pairs = [(ref.at[pos], dest)]
            else:
                half, wide = share
                d = rel_d ^ me_ref[0] if turned else rel_d
                f = rel_f ^ me_ref[1] if turned else rel_f
                lane = pl.multiple_of(d * wide, 128)
                pairs = []
                for k in range(2):
                    row = pl.multiple_of(f * (2 * half) + k * half + off, 16)
                    pairs.append(
                        (
                            ref.at[pos, :, pl.ds(k * wide, wide)],
                            dest.at[pl.ds(row, ref.shape[1]), pl.ds(lane, wide)],
                        )
                    )
            for src, dst in pairs:
                copy = pltpu.make_async_copy(src, dst, sems.at[first + len(copies)])
                copy.start()
                copies.append(copy)
    return copies


def any_specs(count):
    return [pl.BlockSpec(memory_space=pl.ANY)] * count


SMEM_SPEC = pl.BlockSpec(memory_space=pltpu.SMEM)


def full_spec(shape):
    return pl.BlockSpec(shape, lambda i: (0,) * len(shape))


def picked(places, length):
    lanes = places.shape[1]
    rows = lax.broadcasted_iota(jnp.int32, (length, lanes), 0)
    return (rows == places).astype(F32)


def seen_body(seen, cot_ref, places_ref, out_ref, sum_ref):
    count, length, _ = cot_ref.shape

    @pl.when(pl.program_id(0) == 0)
    def _():
        sum_ref[...] = jnp.zeros_like(sum_ref)

    for k in range(count):
        pick = picked(places_ref[k], length)
        gaps = 1.0 - jnp.sum(pick, axis=-1, keepdims=True)
        lane = lax.broadcasted_iota(jnp.int32, pick.shape, 1)
        rows = dot_tn(jnp.where(lane == seen, gaps, pick).astype(BF16), cot_ref[k])
        out_ref[k] = rows[:seen].astype(BF16)
        sum_ref[...] += rows[seen : seen + 1]


def seen_rows(cot, places, seen):
    chips, length, model = cot.shape
    step = 4
    return pl.pallas_call(
        functools.partial(seen_body, seen),
        grid=(chips // step,),
        in_specs=[
            pl.BlockSpec((step, length, model), lambda i: (i, 0, 0)),
            pl.BlockSpec((step, 1, places.shape[2]), lambda i: (i, 0, 0)),
        ],
        out_specs=[pl.BlockSpec((step, seen, model), lambda i: (i, 0, 0)), full_spec((1, model))],
        out_shape=[
            jax.ShapeDtypeStruct((chips, seen, model), BF16),
            jax.ShapeDtypeStruct((1, model), F32),
        ],
        compiler_params=params_for(),
        cost_estimate=busy_for(8),
        name="seen_rows",
    )(cot, places)


def lane_sides(seq):
    lane = lax.broadcasted_iota(jnp.int32, (seq, 2 * HD), 1)
    return lane, (lane < HD, lane >= HD)


def attend_body(table, rows, heads, wide, *refs):
    n = len(table)
    me_ref, x_ref, vec_ref = refs[:3]
    w_refs = refs[3 : 3 + n]
    normed_ref, mixed_ref, expo_ref, share_ref, context_ref, qkv_ref, out_ref, weight, sems = refs[3 + n :]
    shares, model, cols = weight.shape
    slim = cols - wide

    @pl.when(pl.program_id(0) == 0)
    def _():
        for copy in load_grid(table, w_refs, me_ref, weight, sems, rows):
            copy.wait()
        for f in range(shares):
            qkv_ref[:, f * wide : (f + 1) * wide] = weight[f, :, :wide]
            out_ref[:, f * slim : (f + 1) * slim] = weight[f, :, wide:]

    hat, _ = norm_parts(x_ref[0].astype(F32))
    normed = (hat * vec_ref[0:1, :] + vec_ref[1:2, :]).astype(BF16)
    normed_ref[0] = normed
    for part in range(3):
        lanes = slice(part * model, (part + 1) * model)
        mixed = dot_nn(normed, qkv_ref[:, lanes])
        if part == 2:
            mixed = mixed + vec_ref[2:3, :]
        mixed_ref[0, :, lanes] = mixed.astype(BF16)
    seq = normed.shape[0]
    _, sides = lane_sides(seq)
    one = jnp.ones((), BF16)
    for pair in range(heads // 2):
        query, key, value = (
            mixed_ref[0, :, part * model + 2 * HD * pair : part * model + 2 * HD * (pair + 1)]
            for part in range(3)
        )
        query = query * jnp.asarray(HD ** (-0.5), BF16)
        context = None
        for side in range(2):
            mine = sides[side]
            scores = dot_nt(key, jnp.where(mine, query, jnp.zeros_like(query)))
            expo = jnp.exp(scores - jnp.max(scores, axis=0, keepdims=True)).astype(BF16)
            expo_ref[0, 2 * pair + side] = expo
            rich = dot_tn(expo, jnp.where(mine, value, one))
            spot = HD * (1 - side)
            share = 1.0 / rich[:, spot : spot + 1]
            share_ref[0, :, 2 * pair + side : 2 * pair + side + 1] = share
            rich = rich * share
            context = rich if context is None else jnp.where(mine, rich, context)
        context_ref[0, :, 2 * HD * pair : 2 * HD * (pair + 1)] = context.astype(BF16)


def attend_forward(me, x, vec, table, arrays, rows, wide):
    chips, seq, model = x.shape
    heads = model // HD
    cols = arrays[0].shape[-1]
    shares = 3 * model // wide
    count = sum(len(t) for t in table)
    tile = lambda w: pl.BlockSpec((1, seq, w), lambda i: (i, 0, 0))
    return pl.pallas_call(
        functools.partial(attend_body, table, rows, heads, wide),
        grid=(chips,),
        in_specs=[SMEM_SPEC, tile(model), full_spec(vec.shape)] + any_specs(len(arrays)),
        out_specs=[
            tile(model),
            tile(3 * model),
            pl.BlockSpec((1, heads, seq, seq), lambda i: (i, 0, 0, 0)),
            tile(heads),
            tile(model),
            full_spec((model, 3 * model)),
            full_spec((model, model)),
        ],
        out_shape=[
            jax.ShapeDtypeStruct((chips, seq, model), BF16),
            jax.ShapeDtypeStruct((chips, seq, 3 * model), BF16),
            jax.ShapeDtypeStruct((chips, heads, seq, seq), BF16),
            jax.ShapeDtypeStruct((chips, seq, heads), F32),
            jax.ShapeDtypeStruct((chips, seq, model), BF16),
            jax.ShapeDtypeStruct((model, 3 * model), BF16),
            jax.ShapeDtypeStruct((model, model), BF16),
        ],
        scratch_shapes=[
            pltpu.VMEM((shares, model, cols), BF16),
            pltpu.SemaphoreType.DMA((count,)),
        ],
        compiler_params=params_for(),
        cost_estimate=busy_for(20),
        name="attend_forward",
    )(me, x, vec, *arrays)


def feed_up_body(table, rows, *refs):
    n = len(table)
    me_ref, x_ref, context_ref, vec_ref, bias_ref, out_ref = refs[:6]
    u_refs = refs[6 : 6 + n]
    middle_ref, normed_ref, active_ref, slope_ref, up, sems = refs[6 + n :]
    shares, _, span = up.shape

    @pl.when(pl.program_id(0) == 0)
    def _():
        for copy in load_grid(table, u_refs, me_ref, up, sems, rows):
            copy.wait()

    branch = dot_nn(context_ref[0], out_ref[...])
    middle = x_ref[0].astype(F32) + branch + vec_ref[3:4, :]
    middle_ref[0] = middle
    hat, _ = norm_parts(middle)
    normed = (hat * vec_ref[4:5, :] + vec_ref[5:6, :]).astype(BF16)
    normed_ref[0] = normed
    for f in range(shares):
        gate = dot_nn(normed, up[f]) + bias_ref[:, f * span : (f + 1) * span]
        active, slope = gelu_pair(gate)
        active_ref[0, :, f * span : (f + 1) * span] = active.astype(BF16)
        slope_ref[0, :, f * span : (f + 1) * span] = slope.astype(BF16)


def feed_up(me, x, context, vec, bias, out_whole, table, arrays, rows):
    chips, seq, model = x.shape
    ff = bias.shape[1]
    span = arrays[0].shape[-1]
    shares = ff // span
    count = sum(len(t) for t in table)
    tile = lambda w: pl.BlockSpec((1, seq, w), lambda i: (i, 0, 0))
    return pl.pallas_call(
        functools.partial(feed_up_body, table, rows),
        grid=(chips,),
        in_specs=[
            SMEM_SPEC,
            tile(model),
            tile(model),
            full_spec(vec.shape),
            full_spec(bias.shape),
            full_spec(out_whole.shape),
        ]
        + any_specs(len(arrays)),
        out_specs=[tile(model), tile(model), tile(ff), tile(ff)],
        out_shape=[
            jax.ShapeDtypeStruct((chips, seq, model), F32),
            jax.ShapeDtypeStruct((chips, seq, model), BF16),
            jax.ShapeDtypeStruct((chips, seq, ff), BF16),
            jax.ShapeDtypeStruct((chips, seq, ff), BF16),
        ],
        scratch_shapes=[
            pltpu.VMEM((shares, model, span), BF16),
            pltpu.SemaphoreType.DMA((count,)),
        ],
        compiler_params=params_for(),
        cost_estimate=busy_for(17),
        name="feed_up",
    )(me, x, context, vec, bias, out_whole, *arrays)


def feed_down_body(u_table, d_table, rows, share, *refs):
    nu, nd = len(u_table), len(d_table)
    me_ref, grad_ref, middle_ref, active_ref, slope_ref, vec_ref, out_ref = refs[:7]
    u_refs = refs[7 : 7 + nu]
    d_refs = refs[7 + nu : 7 + nu + nd]
    (
        result_ref,
        gate_grad_ref,
        middle_grad_ref,
        branch_grad_ref,
        context_grad_ref,
        sums_ref,
        bias_sums_ref,
        up,
        down,
        sems,
    ) = refs[7 + nu + nd :]
    count = sum(len(t) for t in u_table)
    shares, model, span = up.shape
    step = pl.program_id(0)

    @pl.when(step == 0)
    def _():
        first = load_grid(u_table, u_refs, me_ref, up, sems, rows)
        second = load_down(d_table, d_refs, me_ref, down, sems, share, first=count)
        sums_ref[...] = jnp.zeros_like(sums_ref)
        bias_sums_ref[...] = jnp.zeros_like(bias_sums_ref)
        for copy in first + second:
            copy.wait()

    seq = middle_ref.shape[1]
    middle = middle_ref[0]
    feed_grad = grad_ref[:, 0].reshape(seq, model)
    result = middle + dot_nt(active_ref[0], down[...]) + vec_ref[10:11, :]
    result_ref[:, 0] = result.astype(BF16).reshape(result_ref.shape[0], -1, model)
    normed_grad = jnp.zeros((seq, model), F32)
    for f in range(shares):
        lanes = slice(f * span, (f + 1) * span)
        active_grad = dot_nn(feed_grad, down[:, lanes])
        gate_grad = (active_grad * slope_ref[0, :, lanes].astype(F32)).astype(BF16)
        gate_grad_ref[0, :, lanes] = gate_grad
        bias_sums_ref[:, lanes] += jnp.sum(gate_grad.astype(F32), axis=0, keepdims=True)
        normed_grad += dot_nt(gate_grad, up[f])
    hat, factor = norm_parts(middle)
    gain = vec_ref[4:5, :]
    grad_full = feed_grad.astype(F32)
    middle_grad = grad_full + norm_back(normed_grad, hat, factor, gain)
    middle_grad_ref[0] = middle_grad
    branch_grad = middle_grad.astype(BF16)
    branch_grad_ref[0] = branch_grad
    context_grad_ref[0] = dot_nt(branch_grad, out_ref[...]).astype(BF16)
    sums_ref[0:1, :] += jnp.sum(branch_grad.astype(F32), axis=0, keepdims=True)
    sums_ref[1:2, :] += jnp.sum(normed_grad * hat, axis=0, keepdims=True)
    sums_ref[2:3, :] += jnp.sum(normed_grad, axis=0, keepdims=True)
    sums_ref[3:4, :] += jnp.sum(grad_full, axis=0, keepdims=True)


def feed_down(
    me, grad, middle, active, slope, vec, out_whole, u_table, u_arrays, d_table, d_arrays, rows, share
):
    chips, seq, model = middle.shape
    ff = active.shape[2]
    blocks, _, seen, _ = grad.shape
    span = u_arrays[0].shape[-1]
    shares = ff // span
    count = sum(len(t) for t in u_table) + 2 * sum(len(t) for t in d_table)
    tile = lambda w: pl.BlockSpec((1, seq, w), lambda i: (i, 0, 0))
    spread = pl.BlockSpec((blocks, 1, seen, model), lambda i: (0, i, 0, 0))
    return pl.pallas_call(
        functools.partial(feed_down_body, u_table, d_table, rows, share),
        grid=(chips,),
        in_specs=[
            SMEM_SPEC,
            spread,
            tile(model),
            tile(ff),
            tile(ff),
            full_spec(vec.shape),
            full_spec(out_whole.shape),
        ]
        + any_specs(len(u_arrays) + len(d_arrays)),
        out_specs=[
            spread,
            tile(ff),
            tile(model),
            tile(model),
            tile(model),
            full_spec((8, model)),
            full_spec((1, ff)),
        ],
        out_shape=[
            jax.ShapeDtypeStruct(grad.shape, BF16),
            jax.ShapeDtypeStruct((chips, seq, ff), BF16),
            jax.ShapeDtypeStruct((chips, seq, model), F32),
            jax.ShapeDtypeStruct((chips, seq, model), BF16),
            jax.ShapeDtypeStruct((chips, seq, model), BF16),
            jax.ShapeDtypeStruct((8, model), F32),
            jax.ShapeDtypeStruct((1, ff), F32),
        ],
        scratch_shapes=[
            pltpu.VMEM((shares, model, span), BF16),
            pltpu.VMEM((model, ff), BF16),
            pltpu.SemaphoreType.DMA((count,)),
        ],
        compiler_params=params_for(),
        cost_estimate=busy_for(20),
        name="feed_down",
    )(me, grad, middle, active, slope, vec, out_whole, *u_arrays, *d_arrays)


def attend_back_body(heads, mixed_ref, expo_ref, share_ref, context_ref, grad_ref, mixed_grad_ref, sums_ref):
    seq, model = context_ref.shape[1:]

    @pl.when(pl.program_id(0) == 0)
    def _():
        sums_ref[...] = jnp.zeros_like(sums_ref)

    lane, sides = lane_sides(seq)
    scale = jnp.asarray(HD ** (-0.5), BF16)
    for pair in range(heads // 2):
        spots = [
            slice(part * model + 2 * HD * pair, part * model + 2 * HD * (pair + 1)) for part in range(3)
        ]
        query, key, value = (mixed_ref[0, :, spot] for spot in spots)
        query, key = query * scale, key * scale
        nothing, one = jnp.zeros_like(query), jnp.ones((), BF16)
        out_grad = grad_ref[0, :, spots[0]].astype(F32)
        inner_parts = out_grad * context_ref[0, :, spots[0]].astype(F32)
        grads = [0.0, 0.0, 0.0]
        for side in range(2):
            mine, other = sides[side], HD * (1 - side)
            share = share_ref[0, :, 2 * pair + side : 2 * pair + side + 1]
            inner = -share * jnp.sum(jnp.where(mine, inner_parts, 0.0), axis=-1, keepdims=True)
            inner_high = inner.astype(BF16)
            inner_low = (inner - inner_high.astype(F32)).astype(BF16)
            scaled = jnp.where(mine, out_grad * share, 0.0).astype(BF16)
            rich = jnp.where(lane == other, inner_high, jnp.where(lane == other + 1, inner_low, scaled))
            prob_grad = dot_nt(jnp.where(mine, value, one), rich)
            expo = expo_ref[0, 2 * pair + side]
            score_grad = (expo.astype(F32) * prob_grad).astype(BF16)
            grads[0] += dot_tn(score_grad, jnp.where(mine, key, nothing))
            grads[1] += dot_nn(score_grad, jnp.where(mine, query, nothing))
            grads[2] += dot_nn(expo, scaled)
        for part in range(3):
            mixed_grad_ref[0, :, spots[part]] = grads[part].astype(BF16)
        sums_ref[0:1, spots[0]] += jnp.sum(grads[2].astype(BF16).astype(F32), axis=0, keepdims=True)


def attend_back(mixed, expo, share, context, context_grad):
    chips, seq, model = context.shape
    heads = model // HD
    tile = lambda w: pl.BlockSpec((1, seq, w), lambda i: (i, 0, 0))
    return pl.pallas_call(
        functools.partial(attend_back_body, heads),
        grid=(chips,),
        in_specs=[
            tile(3 * model),
            pl.BlockSpec((1, heads, seq, seq), lambda i: (i, 0, 0, 0)),
            tile(heads),
            tile(model),
            tile(model),
        ],
        out_specs=[tile(3 * model), full_spec((8, model))],
        out_shape=[
            jax.ShapeDtypeStruct(mixed.shape, BF16),
            jax.ShapeDtypeStruct((8, model), F32),
        ],
        compiler_params=params_for(),
        cost_estimate=busy_for(15),
        name="attend_back",
    )(mixed, expo, share, context, context_grad)


def tokens_back_body(x_ref, grad_ref, mixed_grad_ref, vec_ref, qkv_ref, tokens_ref, sums_ref):
    @pl.when(pl.program_id(0) == 0)
    def _():
        sums_ref[...] = jnp.zeros_like(sums_ref)

    normed_grad = dot_nt(mixed_grad_ref[0], qkv_ref[...])
    hat, factor = norm_parts(x_ref[0].astype(F32))
    tokens_ref[0] = grad_ref[0] + norm_back(normed_grad, hat, factor, vec_ref[0:1, :])
    sums_ref[0:1, :] += jnp.sum(normed_grad * hat, axis=0, keepdims=True)
    sums_ref[1:2, :] += jnp.sum(normed_grad, axis=0, keepdims=True)


def tokens_back(x, middle_grad, mixed_grad, vec, qkv_whole):
    chips, seq, model = x.shape
    tile = lambda w: pl.BlockSpec((1, seq, w), lambda i: (i, 0, 0))
    return pl.pallas_call(
        tokens_back_body,
        grid=(chips,),
        in_specs=[
            tile(model),
            tile(model),
            tile(3 * model),
            full_spec(vec.shape),
            full_spec(qkv_whole.shape),
        ],
        out_specs=[tile(model), full_spec((8, model))],
        out_shape=[
            jax.ShapeDtypeStruct((chips, seq, model), F32),
            jax.ShapeDtypeStruct((8, model), F32),
        ],
        compiler_params=params_for(),
        cost_estimate=busy_for(8),
        name="tokens_back",
    )(x, middle_grad, mixed_grad, vec, qkv_whole)


def store_block(order, refs, me_ref, d, f, *lanes_and_blocks):
    rel_d, rel_f = d ^ me_ref[0], f ^ me_ref[1]
    bits = [((rel_d if is_dp else rel_f) // value) % 2 for is_dp, value in order]
    pos = 0
    for bit in bits[1:]:
        pos = pos * 2 + bit
    for side, ref in enumerate(refs):

        @pl.when(bits[0] == side)
        def _():
            for lanes, block in lanes_and_blocks:
                ref[pos, :, lanes] = block


def up_grad_body(split, rows, left_ref, right_ref, out_ref):
    grad = dot_tn(left_ref[...], right_ref[...]).astype(BF16)
    if split:
        for d in range(grad.shape[0] // rows):
            out_ref[d, 0] = grad[d * rows : (d + 1) * rows]
    else:
        out_ref[0] = grad


def block_outs(order, whole, blocks):
    shapes = [whole] if order is None else [blocks, blocks]
    return [full_spec(s) for s in shapes], [jax.ShapeDtypeStruct(s, BF16) for s in shapes]


def up_grad_blocks(left, right, split, rows, shares):
    tokens, model = left.shape
    span = right.shape[1] // shares
    if split:
        shape = (model // rows, shares, rows, span)
        out_spec = pl.BlockSpec((model // rows, 1, rows, span), lambda i: (0, i, 0, 0))
    else:
        shape = (shares, model, span)
        out_spec = pl.BlockSpec((1, model, span), lambda i: (i, 0, 0))
    return pl.pallas_call(
        functools.partial(up_grad_body, split, rows),
        grid=(shares,),
        in_specs=[full_spec(left.shape), pl.BlockSpec((tokens, span), lambda i: (0, i))],
        out_specs=out_spec,
        out_shape=jax.ShapeDtypeStruct(shape, BF16),
        compiler_params=params_for(),
        cost_estimate=busy_for(8),
        name="up_grad",
    )(left, right)


def down_grad_body(order, half, me_ref, grad_ref, active_ref, *refs):
    d = pl.program_id(0)
    whole = dot_tn(grad_ref[...], active_ref[...]).astype(BF16)
    if order is None:
        refs[0][...] = whole
    else:
        wide = whole.shape[1]
        for f in range(whole.shape[0] // (2 * half)):
            parts = []
            for k in range(2):
                start = (2 * f + k) * half
                parts.append((slice(k * wide, (k + 1) * wide), whole[start : start + half]))
            store_block(order, refs, me_ref, d, f, *parts)


def down_grad_blocks(me, grad, active, order, half, wide):
    tokens, model = grad.shape
    ff = active.shape[1]
    steps, width = (4, ff // 4) if order is None else (ff // wide, wide)
    out_specs, out_shape = block_outs(order, (model, ff), (steps * model // (4 * half), half, 2 * wide))
    if order is None:
        out_specs = [pl.BlockSpec((model, width), lambda i: (0, i))]
    return pl.pallas_call(
        functools.partial(down_grad_body, order, half),
        grid=(steps,),
        in_specs=[
            SMEM_SPEC,
            full_spec(grad.shape),
            pl.BlockSpec((tokens, width), lambda i: (0, i)),
        ],
        out_specs=out_specs,
        out_shape=out_shape,
        compiler_params=params_for(),
        cost_estimate=busy_for(10),
        name="down_grad",
    )(me, grad, active)


def qkv_grad_body(order, rows, wide, me_ref, normed_ref, mixed_grad_ref, context_ref, branch_ref, *refs):
    step = pl.program_id(0)
    qkv, out = refs[-2:]
    parts, model, _ = qkv.shape
    shares = 3 * model // wide
    slim = model // shares

    qkv[step] = dot_tn(normed_ref[...], mixed_grad_ref[...]).astype(BF16)

    @pl.when(step == parts - 1)
    def _():
        out[...] = dot_tn(context_ref[...], branch_ref[...]).astype(BF16)

        def qkv_part(spot, f):
            pieces = []
            first, last = f * wide, (f + 1) * wide
            for part in range(parts):
                low, high = max(first, part * model), min(last, (part + 1) * model)
                if low < high:
                    pieces.append(
                        (slice(low - first, high - first), qkv[part, spot, low - part * model : high - part * model])
                    )
            return pieces + [(slice(wide, wide + slim), out[spot, f * slim : (f + 1) * slim])]

        for f in range(shares):
            if order is None:
                for lanes, block in qkv_part(slice(None), f):
                    refs[0][f, :, lanes] = block
            else:
                for d in range(model // rows):
                    store_block(order, refs[:-2], me_ref, d, f, *qkv_part(slice(d * rows, (d + 1) * rows), f))


def qkv_grad_blocks(me, normed, mixed_grad, context, branch_grad, order, rows, wide):
    tokens, model = normed.shape
    shares = 3 * model // wide
    cols = wide + model // shares
    out_specs, out_shape = block_outs(
        order, (shares, model, cols), (shares * model // rows // 2, rows, cols)
    )
    return pl.pallas_call(
        functools.partial(qkv_grad_body, order, rows, wide),
        grid=(3,),
        in_specs=[
            SMEM_SPEC,
            full_spec(normed.shape),
            pl.BlockSpec((tokens, model), lambda i: (0, i)),
            full_spec(context.shape),
            full_spec(branch_grad.shape),
        ],
        out_specs=out_specs,
        out_shape=out_shape,
        scratch_shapes=[pltpu.VMEM((3, model, model), BF16), pltpu.VMEM((model, model), BF16)],
        compiler_params=params_for(),
        cost_estimate=busy_for(10),
        name="qkv_grad",
    )(me, normed, mixed_grad, context, branch_grad)


DP, FSDP = "dp", "fsdp"


def swap(value, axis, bit):
    size = lax.axis_size(axis)
    return lax.ppermute(value, axis, [(i, i ^ bit) for i in range(size)])


def after(value, *others):
    return lax.optimization_barrier((value,) + others)[0]


def grow(value, step, *others):
    arrived = swap(value, *step)
    if others:
        arrived = after(arrived, *others)
    return jnp.concatenate([value, arrived], axis=0)


def fold_body(plan, count, *refs):
    sums = []
    for k in range(count):
        sums.append(refs[2 * k][...].astype(F32) + refs[2 * k + 1][...].astype(F32))
    for out_ref, takes in zip(refs[2 * count :], plan):
        start = 0
        for pair, spot in takes:
            part = sums[pair][spot].astype(out_ref.dtype)
            rows = part.shape[-2]
            out_ref[..., start : start + rows, :] = part
            start += rows


def fold_call(pairs, plan, in_blocks, out_blocks, out_shapes, steps, dtype=BF16):
    def spec(block, along):
        return pl.BlockSpec(block, lambda i: tuple(i if k == along else 0 for k in range(len(block))))

    arrays = [array for pair in pairs for array in pair]
    return pl.pallas_call(
        functools.partial(fold_body, plan, len(pairs)),
        grid=(steps,),
        in_specs=[spec(*in_blocks[k // 2]) for k in range(len(arrays))],
        out_specs=[spec(*b) for b in out_blocks],
        out_shape=[jax.ShapeDtypeStruct(shape, dtype) for shape in out_shapes],
        compiler_params=params_for(),
        cost_estimate=busy_for(2),
        name="fold_sums",
    )(*arrays)


class Fold:
    def __init__(self, keep, send):
        self.rows, self.cols = keep.shape[1:]
        self.keep, self.arrived = keep, swap(send, *CORE)
        self.stage = 0

    def step(self, *others):
        rows, cols = self.rows, self.cols
        cut, sizes = rows // 2, (2, 2, 4, rows, cols)
        upper, lower = slice(0, cut), slice(cut, rows)
        everything = slice(None)
        keep = after(self.keep, *others)
        if self.stage == 0:
            outs = fold_call(
                [(keep.reshape(sizes), self.arrived.reshape(sizes))],
                [
                    [(0, (0, everything, everything, upper))],
                    [(0, (1, everything, everything, upper))],
                    [(0, (everything, 0, everything, lower))],
                    [(0, (everything, 1, everything, lower))],
                ],
                [((2, 2, 1, rows, cols), 2)],
                [((2, 1, cut, cols), 1)] * 4,
                [(2, 4, cut, cols)] * 4,
                4,
            )
            self.keep, sent = (outs[0], outs[2]), (outs[1], outs[3])
            self.arrived = swap(sent[0], *XS), swap(sent[1], *YS)
        elif self.stage == 1:
            outs = fold_call(
                list(zip(keep, self.arrived)),
                [[(0, 0)], [(0, 1)], [(1, 0)], [(1, 1)]],
                [((2, 4, cut, cols), None)] * 2,
                [((4, cut, cols), None)] * 4,
                [(4, cut, cols)] * 4,
                1,
            )
            self.keep, sent = (outs[0], outs[2]), (outs[1], outs[3])
            self.arrived = swap(sent[0], *YS), swap(sent[1], *XS)
        elif self.stage == 2:
            near, far = slice(0, 2), slice(2, 4)
            self.keep, sent = fold_call(
                list(zip(keep, self.arrived)),
                [[(0, near), (1, near)], [(0, far), (1, far)]],
                [((4, cut, cols), None)] * 2,
                [((2, rows, cols), None)] * 2,
                [(2, rows, cols)] * 2,
                1,
            )
            self.arrived = swap(sent, *Z_NEAR)
        elif self.stage == 3:
            self.keep, sent = fold_call(
                [(keep, self.arrived)],
                [[(0, 0)], [(0, 1)]],
                [((2, rows, cols), None)],
                [((rows, cols), None)] * 2,
                [(rows, cols)] * 2,
                1,
            )
            self.arrived = swap(sent, *Z_FAR)
        else:
            return keep.astype(F32) + self.arrived.astype(F32)
        self.stage += 1
        return sent


def rel_table(steps, last, off):
    places = []
    for pos in range(2 ** len(steps)):
        rel = {DP: 0, FSDP: 0}
        for k, (axis, bit) in enumerate(steps):
            if (pos >> k) & 1:
                rel[axis] ^= bit
        if last is not None:
            rel[last[0]] ^= last[1]
        places.append((rel[DP], rel[FSDP], off, True))
    return tuple(places)


CORE, XS, YS, Z_NEAR, Z_FAR = (FSDP, 1), (FSDP, 2), (DP, 1), (DP, 2), (DP, 4)
XY = [Z_FAR, Z_NEAR, XS, YS]
YX = [Z_FAR, Z_NEAR, YS, XS]


def grow_end(value, second, *others):
    value = grow(value, second[0], *others)
    value = grow(value, second[1])
    return value, swap(value, *CORE)


def order_of(steps):
    return [(axis == DP, bit) for axis, bit in steps]


def adam_step(weight, gradient, first_mom, second, clip_factor, step_rate, decay_rate):
    scaled = gradient * clip_factor
    first_new = 0.5 * first_mom + 0.5 * scaled
    second_new = 0.5 * second + 0.5 * scaled * scaled
    correction = 1.0 - 0.5**STEP
    update = first_new / correction / (jnp.sqrt(second_new / correction) + 1e-08)
    return (first_new, second_new, weight - step_rate * (update + decay_rate * weight))


def on_device(
    tokens,
    visible_index,
    cotangent,
    qkv_weight,
    out_weight,
    up_weight,
    down_weight,
    vectors,
    qkv_first,
    out_first,
    up_first,
    down_first,
    vector_first,
    qkv_second,
    out_second,
    up_second,
    down_second,
    vector_second,
):
    _, chip_count, seq_len, model_width = tokens.shape
    dp_size, fsdp_size = lax.axis_size(DP), lax.axis_size(FSDP)
    device_count = dp_size * fsdp_size
    both = (DP, FSDP)
    block_count = dp_size
    block_seen = seq_len // block_count
    block_len = cotangent.shape[2]
    chips_group = chip_count * block_count
    rows, wide = qkv_weight.shape
    slim = out_weight.shape[1]
    span = up_weight.shape[1]
    ff_width = span * fsdp_size
    half = slim // 2
    tall = down_weight.shape[0]
    folded = (dp_size, fsdp_size) == (8, 4)

    share_q = jnp.concatenate([qkv_weight, out_weight], axis=1).astype(BF16)
    share_u = up_weight.astype(BF16)
    down_turned = down_weight.astype(BF16).T

    vec_rows, vec_cols = vectors.shape
    vector_copies = jnp.broadcast_to(vectors.astype(BF16), (device_count, vec_rows, vec_cols))
    vec_shares = lax.all_to_all(vector_copies, both, split_axis=0, concat_axis=0, tiled=True)
    vec = vec_shares.reshape(dp_size, fsdp_size, vec_rows, vec_cols).transpose(1, 2, 0, 3)
    vec = vec.reshape(fsdp_size * vec_rows, model_width).astype(F32)

    my_block = lax.axis_index(DP)
    places = visible_index[0].reshape(chips_group, block_count, block_seen)
    places = lax.dynamic_index_in_dim(places, my_block, 1, keepdims=False) - my_block * block_len
    seen_places = places
    cot = cotangent[0]
    whole_tiles = block_seen % 16 == 0
    if whole_tiles:
        places = jnp.pad(places, ((0, 0), (0, 128 - block_seen)), constant_values=-1)[:, None]
        cot_seen, mask_grad = seen_rows(cot, places, block_seen)
    else:
        slot_ids = lax.broadcasted_iota(jnp.int32, (chips_group, block_len, block_seen), 1)
        pick = (places[:, None, :] == slot_ids).astype(BF16)
        gaps = 1.0 - jnp.sum(pick.astype(F32), axis=-1)
        cot_seen = jnp.einsum("cpv,cpd->cvd", pick, cot, preferred_element_type=F32).astype(BF16)
        mask_grad = jnp.einsum("cp,cpd->d", gaps.astype(BF16), cot, preferred_element_type=F32)[None]
    if folded:
        me = jnp.stack([lax.axis_index(DP), lax.axis_index(FSDP)]).astype(jnp.int32)
        share_d = jnp.concatenate([down_turned[:half], down_turned[half:]], axis=1)
        cut = rows // 2
        cur = grow(grow(share_q[None], Z_FAR, vec_shares), Z_NEAR, cot_seen)
        d_cur = after(share_d[None], cur)
        q_upper, q_lower = grow(cur[:, :cut], XS), grow(cur[:, cut:], YS)
        d_cur = grow(d_cur, Z_FAR, q_upper, q_lower)
        q_upper, q_lower = grow(q_upper, YS), grow(q_lower, XS)
        q_arrays = (q_upper, swap(q_upper, *CORE), q_lower, swap(q_lower, *CORE))
        cot_seen = after(cot_seen, q_upper, q_lower)
        q_table = d_table = (
            rel_table(XY, None, 0),
            rel_table(XY, CORE, 0),
            rel_table(YX, None, cut),
            rel_table(YX, CORE, cut),
        )
        u_arrays = (lax.all_gather(share_u, both, axis=0, tiled=False),)
        u_table = (tuple((d, f, 0, False) for d in range(dp_size) for f in range(fsdp_size)),)
        q_order = d_order = order_of([CORE, XS, YS, Z_NEAR, Z_FAR])
        down_share = (half, tall)
        load_rows = rows
    else:
        me = jnp.zeros((2,), jnp.int32)

        def gather_whole(share):
            whole = lax.all_gather(share, both, axis=0, tiled=False)
            whole = whole.reshape((dp_size, fsdp_size) + share.shape).transpose(1, 0, 2, 3)
            return whole.reshape(fsdp_size, dp_size * share.shape[0], share.shape[1])

        q_arrays = (gather_whole(share_q),)
        u_arrays = (gather_whole(share_u),)
        down_whole = lax.all_gather(down_turned, both, axis=0, tiled=False)
        down_whole = down_whole.reshape(dp_size, fsdp_size, slim, tall).transpose(1, 2, 0, 3)
        d_arrays = (down_whole.reshape(1, model_width, ff_width),)
        q_table = u_table = (tuple((0, f, 0, False) for f in range(fsdp_size)),)
        d_table = (((0, 0, 0, False),),)
        q_order = d_order = None
        down_share = None
        load_rows = model_width

    cot_seen = cot_seen.reshape(block_count, chip_count, block_seen, model_width)
    grad = lax.all_to_all(cot_seen, DP, split_axis=0, concat_axis=0, tiled=True)
    if not whole_tiles:
        grad = grad.transpose(1, 0, 2, 3).reshape(1, chip_count, seq_len, model_width)

    x = tokens[0]
    up_bias = vec[6:10].reshape(1, ff_width)
    normed, mixed, expo, share, context, qkv_whole, out_whole = attend_forward(
        me, x, vec, q_table, q_arrays, load_rows, wide
    )
    if folded:
        d_cur = grow(d_cur, Z_NEAR, context)
        d_halves = d_cur[:, :cut], d_cur[:, cut:]
        context = after(context, *d_halves)
    middle, normed_two, active, slope = feed_up(
        me, x, context, vec, up_bias, out_whole, u_table, u_arrays, load_rows
    )
    if folded:
        d_halves = grow(d_halves[0], XS, active), grow(d_halves[1], YS, active)
        grad = after(grad, *d_halves)
    token_count = chip_count * seq_len
    flat = lambda v: v.reshape(token_count, v.shape[-1])
    grad_rows = flat(grad.transpose(1, 0, 2, 3).reshape(chip_count, seq_len, model_width))
    d_blocks = down_grad_blocks(me, grad_rows, flat(active), d_order, half, tall)
    if folded:
        upper, lower = grow(d_halves[0], YS, *d_blocks), grow(d_halves[1], XS, *d_blocks)
        d_arrays = (upper, swap(upper, *CORE), lower, swap(lower, *CORE))
    if folded:
        d_fold = Fold(*d_blocks)
        middle = after(middle, *d_blocks)
    result, gate_grad, middle_grad, branch_grad, context_grad, sums_two, up_sums = feed_down(
        me, grad, middle, active, slope, vec, out_whole, u_table, u_arrays, d_table, d_arrays, load_rows, down_share
    )
    if folded:
        normed_two = after(normed_two, d_fold.step(gate_grad))
    u_blocks = up_grad_blocks(flat(normed_two), flat(gate_grad), folded, rows, fsdp_size)
    if folded:
        u_sum = lax.psum_scatter(u_blocks.reshape(-1, span), both, scatter_dimension=0, tiled=True)
        context_grad = after(context_grad, d_fold.step(u_blocks), u_blocks)
        result = after(result, u_blocks)
    if not whole_tiles:
        result = result.reshape(chip_count, block_count, block_seen, model_width).transpose(1, 0, 2, 3)
    arrived = lax.all_to_all(result, DP, split_axis=0, concat_axis=0, tiled=True)
    arrived = arrived.reshape(chips_group, block_seen, model_width)
    mixed_grad, sums_value = attend_back(mixed, expo, share, context, context_grad)
    if folded:
        normed = after(normed, d_fold.step(mixed_grad))
    q_blocks = qkv_grad_blocks(
        me,
        flat(normed),
        flat(mixed_grad),
        flat(context),
        flat(branch_grad),
        q_order,
        rows,
        wide,
    )
    if folded:
        q_fold = Fold(*q_blocks)
        x = after(x, q_blocks, arrived)
    tokens_grad, sums_one = tokens_back(x, middle_grad, mixed_grad, vec, qkv_whole)

    slot_ids = lax.broadcasted_iota(jnp.int32, (chips_group, block_len, block_seen), 1)
    pick = (seen_places[:, None, :] == slot_ids).astype(BF16)
    gaps = 1.0 - jnp.sum(pick.astype(F32), axis=-1)
    filled = jnp.einsum("cpv,cvd->cpd", pick, arrived, preferred_element_type=F32)
    filled = filled + gaps[..., None] * vec[11]
    full_layout = filled.astype(BF16).reshape(1, chips_group, block_len, model_width)

    if folded:
        d_fold.step(tokens_grad)
        d_sum = d_fold.step()
        q_fold.step(tokens_grad)
        q_fold.step()
        q_fold.step()
        q_fold.step()
        q_sum = q_fold.step()
        u_sum = u_sum.astype(F32)
        d_sum = jnp.concatenate([d_sum[:, :tall], d_sum[:, tall:]], axis=0).T.astype(F32)
    else:

        def scatter_whole(whole):
            cols = whole.shape[2]
            pieces = whole.reshape(fsdp_size, dp_size, -1, cols).transpose(1, 0, 2, 3)
            pieces = pieces.reshape(-1, cols)
            return lax.psum_scatter(pieces, both, scatter_dimension=0, tiled=True).astype(F32)

        q_sum, u_sum = scatter_whole(q_blocks[0]), scatter_whole(u_blocks)
        pieces = d_blocks[0].reshape(fsdp_size, slim, dp_size, tall).transpose(2, 0, 1, 3)
        pieces = pieces.reshape(device_count * slim, tall)
        d_sum = lax.psum_scatter(pieces, both, scatter_dimension=0, tiled=True).astype(F32).T

    vector_grad = jnp.concatenate(
        [
            sums_one[:2],
            sums_value[:1],
            sums_two[:3],
            up_sums.reshape(-1, model_width),
            sums_two[3:4],
            mask_grad,
        ],
        axis=0,
    )
    parts = vector_grad.reshape(fsdp_size, vec_rows, dp_size, vec_cols).transpose(2, 0, 1, 3)
    parts = parts.reshape(device_count, vec_rows, vec_cols)
    parts = lax.all_to_all(parts, both, split_axis=0, concat_axis=0, tiled=True)
    shares = (q_sum[:, :wide], q_sum[:, wide:], u_sum, d_sum, jnp.sum(parts, axis=0))
    squares = jnp.sum(q_sum * q_sum) + jnp.sum(u_sum * u_sum) + jnp.sum(d_sum * d_sum)
    squares = squares + jnp.sum(shares[4] * shares[4])
    square_parts = jnp.broadcast_to(squares, (device_count, 1))
    grad_total = jnp.sum(lax.all_to_all(square_parts, both, split_axis=0, concat_axis=0, tiled=True))
    grad_norm = jnp.sqrt(grad_total)
    tokens_all = device_count * chip_count * seq_len
    threshold = 0.05 * model_width * math.sqrt(tokens_all)
    clip = jnp.minimum(1.0, threshold / grad_norm)
    rate = 0.6 / math.sqrt(model_width)
    out_rate = 0.6 / math.sqrt(model_width // 32)
    down_rate = 0.6 / math.sqrt(ff_width)
    qkv_out = adam_step(qkv_weight, shares[0], qkv_first, qkv_second, clip, rate, 0.05)
    out_out = adam_step(out_weight, shares[1], out_first, out_second, clip, out_rate, 0.05)
    up_out = adam_step(up_weight, shares[2], up_first, up_second, clip, rate, 0.05)
    down_out = adam_step(down_weight, shares[3], down_first, down_second, clip, down_rate, 0.05)
    vec_out = adam_step(vectors, shares[4], vector_first, vector_second, clip, 0.45, 0.0)
    return (
        full_layout,
        tokens_grad[None],
        *qkv_out,
        qkv_out[2].astype(BF16),
        *out_out,
        out_out[2].astype(BF16),
        *up_out,
        up_out[2].astype(BF16),
        *down_out,
        down_out[2].astype(BF16),
        *vec_out,
        grad_norm,
    )


def solution(mesh):
    grid = P("dp", "fsdp")
    table = P("fsdp", "dp")
    weights = (grid, grid, grid, grid, table)
    in_specs = (
        P("fsdp", "dp", None, None),
        P("fsdp", None, None),
        P("fsdp", None, "dp", None),
        *weights,
        *weights,
        *weights,
    )
    out_specs = (
        P("fsdp", None, "dp", None),
        P("fsdp", "dp", None, None),
        *(grid,) * 16,
        *(table,) * 3,
        P(),
    )
    return jax.shard_map(
        on_device, mesh=mesh, in_specs=in_specs, out_specs=out_specs, check_vma=False
    )
```

```python
import functools
import math

import jax
import jax.numpy as jnp
from jax import lax
from jax.experimental import pallas as pl
from jax.experimental.pallas import tpu as pltpu
from jax.sharding import PartitionSpec as P

HD = 64
HEAD_GROUP = 6
STEP = 10
F32 = jnp.float32
BF16 = jnp.bfloat16
VMEM_BYTES = 66_900_000


def params_for(**more):
    return pltpu.CompilerParams(vmem_limit_bytes=VMEM_BYTES, **more)


def busy_for(micros):
    return pl.CostEstimate(flops=micros * 10**9, bytes_accessed=micros * 3 * 10**6, transcendentals=0)


def dot_nn(left, right):
    return lax.dot_general(left, right, (((1,), (0,)), ((), ())), preferred_element_type=F32)


def dot_nt(left, right):
    return lax.dot_general(left, right, (((1,), (1,)), ((), ())), preferred_element_type=F32)


def dot_tn(left, right):
    return lax.dot_general(left, right, (((0,), (0,)), ((), ())), preferred_element_type=F32)


def norm_parts(values):
    center = values - jnp.mean(values, axis=-1, keepdims=True)
    spread = jnp.mean(center * center, axis=-1, keepdims=True)
    factor = lax.rsqrt(spread + 1e-05)
    return center * factor, factor


def norm_back(grad, hat, factor, gain):
    scaled = grad * gain
    inner = jnp.mean(scaled * hat, axis=-1, keepdims=True)
    return factor * (scaled - jnp.mean(scaled, axis=-1, keepdims=True) - hat * inner)


def gelu_pair(gate):
    cdf = 0.5 + 0.5 * lax.erf(gate * 0.5**0.5)
    bell = jnp.exp2(gate * gate * (-0.5 * math.log2(math.e))) * (0.5 / math.pi) ** 0.5
    return gate * cdf, cdf + gate * bell


def load_grid(table, refs, me_ref, dest, sems, rows, first=0, start=True):
    copies = []
    for ref, places in zip(refs, table):
        for pos, (rel_d, rel_f, off, turned) in enumerate(places):
            d = rel_d ^ me_ref[0] if turned else rel_d
            f = rel_f ^ me_ref[1] if turned else rel_f
            height = min(ref.shape[1], rows)
            row = pl.multiple_of(d * rows + off, 16)
            copy = pltpu.make_async_copy(
                ref.at[pos, pl.ds(0, height)], dest.at[f, pl.ds(row, height)], sems.at[first + len(copies)]
            )
            if start:
                copy.start()
            copies.append(copy)
    return copies


def load_down(table, refs, me_ref, dest, sems, share, first=0, start=True):
    copies = []
    for ref, places in zip(refs, table):
        for pos, (rel_d, rel_f, off, turned) in enumerate(places):
            if share is None:
                pairs = [(ref.at[pos], dest)]
            else:
                half, wide = share
                d = rel_d ^ me_ref[0] if turned else rel_d
                f = rel_f ^ me_ref[1] if turned else rel_f
                lane = pl.multiple_of(d * wide, 128)
                pairs = []
                for k in range(2):
                    row = pl.multiple_of(f * (2 * half) + k * half + off, 16)
                    pairs.append(
                        (
                            ref.at[pos, pl.ds(ref.shape[1] - half, half), pl.ds(k * wide, wide)],
                            dest.at[pl.ds(row, half), pl.ds(lane, wide)],
                        )
                    )
            for src, dst in pairs:
                copy = pltpu.make_async_copy(src, dst, sems.at[first + len(copies)])
                if start:
                    copy.start()
                copies.append(copy)
    return copies


def any_specs(count):
    return [pl.BlockSpec(memory_space=pl.ANY)] * count


SMEM_SPEC = pl.BlockSpec(memory_space=pltpu.SMEM)


def full_spec(shape):
    return pl.BlockSpec(shape, lambda i: (0,) * len(shape))


def picked(places, length):
    lanes = places.shape[1]
    rows = lax.broadcasted_iota(jnp.int32, (length, lanes), 0)
    return (rows == places).astype(F32)


def seen_body(seen, cot_ref, places_ref, out_ref, sum_ref):
    count, length, _ = cot_ref.shape

    @pl.when(pl.program_id(0) == 0)
    def _():
        sum_ref[...] = jnp.zeros_like(sum_ref)

    for k in range(count):
        pick = picked(places_ref[k], length)
        gaps = 1.0 - jnp.sum(pick, axis=-1, keepdims=True)
        lane = lax.broadcasted_iota(jnp.int32, pick.shape, 1)
        rows = dot_tn(jnp.where(lane == seen, gaps, pick).astype(BF16), cot_ref[k])
        out_ref[k] = rows[:seen].astype(BF16)
        sum_ref[...] += rows[seen : seen + 1]


def seen_rows(cot, places, seen):
    chips, length, model = cot.shape
    step = 4
    return pl.pallas_call(
        functools.partial(seen_body, seen),
        grid=(chips // step,),
        in_specs=[
            pl.BlockSpec((step, length, model), lambda i: (i, 0, 0)),
            pl.BlockSpec((step, 1, places.shape[2]), lambda i: (i, 0, 0)),
        ],
        out_specs=[pl.BlockSpec((step, seen, model), lambda i: (i, 0, 0)), full_spec((1, model))],
        out_shape=[
            jax.ShapeDtypeStruct((chips, seen, model), BF16),
            jax.ShapeDtypeStruct((1, model), F32),
        ],
        compiler_params=params_for(),
        cost_estimate=busy_for(8),
        name="seen_rows",
    )(cot, places)


def attend_body(table, rows, heads, wide, *refs):
    n = len(table)
    me_ref, x_ref, vec_ref, bias_ref = refs[:4]
    w_refs = refs[4 : 4 + n]
    normed_ref, mixed_ref, expo_ref, share_ref, context_ref, qkv_out, out_out = refs[4 + n : 11 + n]
    qkv_ref, out_ref, weight, sems = refs[11 + n :]
    shares, model, cols = weight.shape
    slim = cols - wide
    step, last = pl.program_id(0), pl.num_programs(0) - 1
    count = sum(len(t) for t in table)
    saves = [
        pltpu.make_async_copy(qkv_ref, qkv_out, sems.at[count]),
        pltpu.make_async_copy(out_ref, out_out, sems.at[count + 1]),
    ]

    @pl.when(step == 0)
    def _():
        load_grid(table, w_refs, me_ref, weight, sems, rows)

    hat, _ = norm_parts(x_ref[0].astype(F32))
    normed = (hat * vec_ref[0:1, :] + vec_ref[1:2, :]).astype(BF16)
    normed_ref[...] = normed.T

    @pl.when(step == 0)
    def _():
        for copy in load_grid(table, w_refs, me_ref, weight, sems, rows, start=False):
            copy.wait()
        up_to = -(-wide // 128) * 128
        for f in range(shares):
            qkv_ref[f * wide : (f + 1) * wide, :] = weight[f, :, :up_to].T[:wide]
            out_ref[:, f * slim : (f + 1) * slim] = weight[f, :, wide:]
        for copy in saves:
            copy.start()

    for part in range(3):
        spot = slice(part * model, (part + 1) * model)
        mixed = dot_nt(qkv_ref[spot, :], normed)
        if part == 2:
            mixed = mixed + bias_ref[...]
        mixed_ref[spot, :] = mixed.astype(BF16)
    for first in range(0, heads, HEAD_GROUP):
        group = range(first, first + HEAD_GROUP)
        part = lambda which, head: mixed_ref[which * model + HD * head : which * model + HD * (head + 1), :]
        scores = [dot_tn(part(1, head), part(0, head) * jnp.asarray(HD ** (-0.5), BF16)) for head in group]
        expos = [jnp.exp(score - jnp.max(score, axis=0, keepdims=True)) for score in scores]
        shares = [1.0 / jnp.sum(expo, axis=0, keepdims=True) for expo in expos]
        expos = [expo.astype(BF16) for expo in expos]
        contexts = [dot_nn(part(2, head), expo) for head, expo in zip(group, expos)]
        for head, expo, share, context in zip(group, expos, shares, contexts):
            share_ref[head : head + 1, :] = share
            expo_ref[0, head] = expo
            context_ref[HD * head : HD * (head + 1), :] = (context * share).astype(BF16)

    @pl.when(step == last)
    def _():
        for copy in saves:
            copy.wait()


def attend_forward(me, x, vec, bias, table, arrays, rows, wide):
    chips, seq, model = x.shape
    heads = model // HD
    cols = arrays[0].shape[-1]
    shares = 3 * model // wide
    count = sum(len(t) for t in table)
    tall = lambda h: pl.BlockSpec((h, seq), lambda i: (0, i))
    tokens = chips * seq
    return pl.pallas_call(
        functools.partial(attend_body, table, rows, heads, wide),
        grid=(chips,),
        in_specs=[
            SMEM_SPEC,
            pl.BlockSpec((1, seq, model), lambda i: (i, 0, 0)),
            full_spec(vec.shape),
            full_spec(bias.shape),
        ]
        + any_specs(len(arrays)),
        out_specs=[
            tall(model),
            tall(3 * model),
            pl.BlockSpec((1, heads, seq, seq), lambda i: (i, 0, 0, 0)),
            tall(heads),
            tall(model),
        ]
        + any_specs(2),
        out_shape=[
            jax.ShapeDtypeStruct((model, tokens), BF16),
            jax.ShapeDtypeStruct((3 * model, tokens), BF16),
            jax.ShapeDtypeStruct((chips, heads, seq, seq), BF16),
            jax.ShapeDtypeStruct((heads, tokens), F32),
            jax.ShapeDtypeStruct((model, tokens), BF16),
            jax.ShapeDtypeStruct((3 * model, model), BF16),
            jax.ShapeDtypeStruct((model, model), BF16),
        ],
        scratch_shapes=[
            pltpu.VMEM((3 * model, model), BF16),
            pltpu.VMEM((model, model), BF16),
            pltpu.VMEM((shares, model, cols), BF16),
            pltpu.SemaphoreType.DMA((count + 2,)),
        ],
        compiler_params=params_for(),
        cost_estimate=busy_for(1),
        name="attend_forward",
    )(me, x, vec, bias, *arrays)


def feed_body(u_table, d_table, rows, share, *refs):
    nu, nd = len(u_table), len(d_table)
    me_ref, grad_ref, x_ref, context_ref, vec_ref, bias_ref, out_ref = refs[:7]
    u_refs = refs[7 : 7 + nu]
    d_refs = refs[7 + nu : 7 + nu + nd]
    (
        result_ref,
        normed_ref,
        active_ref,
        gate_grad_ref,
        feed_grad_ref,
        middle_grad_ref,
        branch_grad_ref,
        context_grad_ref,
        sums_ref,
        bias_sums_ref,
        up,
        down,
        sems,
    ) = refs[7 + nu + nd :]
    count = sum(len(t) for t in u_table)
    shares, model, span = up.shape
    seq = x_ref.shape[1]
    first_step = pl.program_id(0) == 0

    @pl.when(first_step)
    def _():
        load_grid(u_table, u_refs, me_ref, up, sems, rows)
        load_down(d_table, d_refs, me_ref, down, sems, share, first=count)
        sums_ref[...] = jnp.zeros_like(sums_ref)
        bias_sums_ref[...] = jnp.zeros_like(bias_sums_ref)

    feed_grad = grad_ref[:, 0].reshape(seq, model)
    feed_grad_ref[...] = feed_grad
    middle = x_ref[0].astype(F32) + dot_tn(context_ref[...], out_ref[...]) + vec_ref[3:4, :]
    hat, factor = norm_parts(middle)
    gain = vec_ref[4:5, :]
    normed = (hat * gain + vec_ref[5:6, :]).astype(BF16)
    normed_ref[...] = normed

    @pl.when(first_step)
    def _():
        copies = load_grid(u_table, u_refs, me_ref, up, sems, rows, start=False)
        copies += load_down(d_table, d_refs, me_ref, down, sems, share, first=count, start=False)
        for copy in copies:
            copy.wait()

    def fore(f):
        lanes = slice(f * span, (f + 1) * span)
        return dot_nn(normed, up[f]) + bias_ref[:, lanes], dot_nn(feed_grad, down[:, lanes])

    normed_grad = jnp.zeros((seq, model), F32)
    result = middle + vec_ref[10:11, :]
    ready = fore(0)
    for f in range(shares):
        lanes = slice(f * span, (f + 1) * span)
        gate, active_grad = ready
        if f + 1 < shares:
            ready = fore(f + 1)
        active, slope = gelu_pair(gate)
        active = active.astype(BF16)
        gate_grad = (active_grad * slope).astype(BF16)
        active_ref[:, lanes] = active
        gate_grad_ref[:, lanes] = gate_grad
        result += dot_nt(active, down[:, lanes])
        normed_grad += dot_nt(gate_grad, up[f])
        bias_sums_ref[:, lanes] += jnp.sum(gate_grad.astype(F32), axis=0, keepdims=True)
    result_ref[:, 0] = result.astype(BF16).reshape(result_ref.shape[0], -1, model)
    grad_full = feed_grad.astype(F32)
    middle_grad = grad_full + norm_back(normed_grad, hat, factor, gain)
    middle_grad_ref[0] = middle_grad
    branch_grad = middle_grad.astype(BF16)
    branch_grad_ref[...] = branch_grad
    context_grad_ref[...] = dot_nt(out_ref[...], branch_grad).astype(BF16)
    sums_ref[0:1, :] += jnp.sum(branch_grad.astype(F32), axis=0, keepdims=True)
    sums_ref[1:2, :] += jnp.sum(normed_grad * hat, axis=0, keepdims=True)
    sums_ref[2:3, :] += jnp.sum(normed_grad, axis=0, keepdims=True)
    sums_ref[3:4, :] += jnp.sum(grad_full, axis=0, keepdims=True)


def feed_forward_back(
    me, grad, x, context, vec, bias, out_whole, u_table, u_arrays, d_table, d_arrays, rows, share
):
    chips, seq, model = x.shape
    ff = bias.shape[1]
    blocks, _, seen, _ = grad.shape
    span = u_arrays[0].shape[-1]
    shares = ff // span
    tokens = chips * seq
    count = sum(len(t) for t in u_table) + 2 * sum(len(t) for t in d_table)
    tile = pl.BlockSpec((1, seq, model), lambda i: (i, 0, 0))
    flat = lambda w: pl.BlockSpec((seq, w), lambda i: (i, 0))
    tall = pl.BlockSpec((model, seq), lambda i: (0, i))
    spread = pl.BlockSpec((blocks, 1, seen, model), lambda i: (0, i, 0, 0))
    rows_of = lambda w: jax.ShapeDtypeStruct((tokens, w), BF16)
    return pl.pallas_call(
        functools.partial(feed_body, u_table, d_table, rows, share),
        grid=(chips,),
        in_specs=[
            SMEM_SPEC,
            spread,
            tile,
            tall,
            full_spec(vec.shape),
            full_spec(bias.shape),
            full_spec(out_whole.shape),
        ]
        + any_specs(len(u_arrays) + len(d_arrays)),
        out_specs=[
            spread,
            flat(model),
            flat(ff),
            flat(ff),
            flat(model),
            tile,
            flat(model),
            tall,
            full_spec((8, model)),
            full_spec((1, ff)),
        ],
        out_shape=[
            jax.ShapeDtypeStruct(grad.shape, BF16),
            rows_of(model),
            rows_of(ff),
            rows_of(ff),
            rows_of(model),
            jax.ShapeDtypeStruct((chips, seq, model), F32),
            rows_of(model),
            jax.ShapeDtypeStruct((model, tokens), BF16),
            jax.ShapeDtypeStruct((8, model), F32),
            jax.ShapeDtypeStruct((1, ff), F32),
        ],
        scratch_shapes=[
            pltpu.VMEM((shares, model, span), BF16),
            pltpu.VMEM((model, ff), BF16),
            pltpu.SemaphoreType.DMA((count,)),
        ],
        compiler_params=params_for(),
        cost_estimate=busy_for(10),
        name="feed_forward_back",
    )(me, grad, x, context, vec, bias, out_whole, *u_arrays, *d_arrays)


def attend_back_body(heads, mixed_ref, expo_ref, share_ref, grad_ref, mixed_grad_ref, sums_ref):
    model, seq = grad_ref.shape

    @pl.when(pl.program_id(0) == 0)
    def _():
        sums_ref[...] = jnp.zeros_like(sums_ref)

    scale = jnp.asarray(HD ** (-0.5), BF16)
    for first in range(0, heads, HEAD_GROUP):
        group = range(first, first + HEAD_GROUP)
        spot = lambda which, head: slice(which * model + HD * head, which * model + HD * (head + 1))
        shares = [share_ref[head : head + 1, :] for head in group]
        out_grads = [
            (grad_ref[spot(0, head), :].astype(F32) * share).astype(BF16) for head, share in zip(group, shares)
        ]
        prob_grads = [dot_tn(mixed_ref[spot(2, head), :], grad) for head, grad in zip(group, out_grads)]
        value_grads = [dot_nt(grad, expo_ref[0, head]) for head, grad in zip(group, out_grads)]
        score_grads = []
        for head, share, prob_grad in zip(group, shares, prob_grads):
            expo = expo_ref[0, head].astype(F32)
            weighted = expo * prob_grad
            inner = jnp.sum(weighted, axis=0, keepdims=True) * share
            score_grads.append((weighted - expo * inner).astype(BF16))
        query_grads = [dot_nn(mixed_ref[spot(1, head), :] * scale, grad) for head, grad in zip(group, score_grads)]
        key_grads = [dot_nt(mixed_ref[spot(0, head), :] * scale, grad) for head, grad in zip(group, score_grads)]
        for head, *grads in zip(group, query_grads, key_grads, value_grads):
            for which in range(3):
                mixed_grad_ref[spot(which, head), :] = grads[which].astype(BF16)
    sums_ref[...] += dot_nt(jnp.ones((8, seq), BF16), mixed_grad_ref[2 * model :, :])


def attend_back(mixed, expo, share, context_grad):
    model, tokens = context_grad.shape
    chips, heads, seq, _ = expo.shape
    tall = lambda h: pl.BlockSpec((h, seq), lambda i: (0, i))
    return pl.pallas_call(
        functools.partial(attend_back_body, heads),
        grid=(chips,),
        in_specs=[
            tall(3 * model),
            pl.BlockSpec((1, heads, seq, seq), lambda i: (i, 0, 0, 0)),
            tall(heads),
            tall(model),
        ],
        out_specs=[tall(3 * model), full_spec((8, model))],
        out_shape=[
            jax.ShapeDtypeStruct((3 * model, tokens), BF16),
            jax.ShapeDtypeStruct((8, model), F32),
        ],
        compiler_params=params_for(),
        cost_estimate=busy_for(30),
        name="attend_back",
    )(mixed, expo, share, context_grad)


def tokens_back_body(x_ref, grad_ref, mixed_grad_ref, vec_ref, qkv_ref, tokens_ref, sums_ref):
    @pl.when(pl.program_id(0) == 0)
    def _():
        sums_ref[...] = jnp.zeros_like(sums_ref)

    normed_grad = dot_tn(mixed_grad_ref[...], qkv_ref[...])
    hat, factor = norm_parts(x_ref[0].astype(F32))
    tokens_ref[0] = grad_ref[0] + norm_back(normed_grad, hat, factor, vec_ref[0:1, :])
    sums_ref[0:1, :] += jnp.sum(normed_grad * hat, axis=0, keepdims=True)
    sums_ref[1:2, :] += jnp.sum(normed_grad, axis=0, keepdims=True)


def tokens_back(x, middle_grad, mixed_grad, vec, qkv_whole):
    chips, seq, model = x.shape
    tile = pl.BlockSpec((1, seq, model), lambda i: (i, 0, 0))
    return pl.pallas_call(
        tokens_back_body,
        grid=(chips,),
        in_specs=[
            tile,
            tile,
            pl.BlockSpec((3 * model, seq), lambda i: (0, i)),
            full_spec(vec.shape),
            full_spec(qkv_whole.shape),
        ],
        out_specs=[tile, full_spec((8, model))],
        out_shape=[
            jax.ShapeDtypeStruct((chips, seq, model), F32),
            jax.ShapeDtypeStruct((8, model), F32),
        ],
        compiler_params=params_for(),
        cost_estimate=busy_for(40),
        name="tokens_back",
    )(x, middle_grad, mixed_grad, vec, qkv_whole)


def start_block(order, me_ref, d, f, sides, sem, source, *window):
    rel_d, rel_f = d ^ me_ref[0], f ^ me_ref[1]
    bits = [((rel_d if is_dp else rel_f) // value) % 2 for is_dp, value in order]
    pos = 0
    for bit in bits[1:]:
        pos = pos * 2 + bit
    for side, ref in enumerate(sides):

        @pl.when(bits[0] == side)
        def _():
            pltpu.make_async_copy(source, ref.at[(pos,) + window], sem).start()


def feed_grad_body(order, rows, half, wide, me_ref, normed_ref, gate_grad_ref, feed_grad_ref, active_ref, *refs):
    step = pl.program_id(0)
    if order is None:
        refs[0][0] = dot_tn(normed_ref[...], gate_grad_ref[...]).astype(BF16)
        refs[1][...] = dot_tn(feed_grad_ref[...], active_ref[...]).astype(BF16)
        return
    keep_ref, send_ref, up, down, sems = refs
    shares, model, span = up.shape
    count, fit = model // rows, span // wide
    sides = keep_ref, send_ref
    base = step * count * 2
    up[step] = dot_tn(normed_ref[...], gate_grad_ref[...]).astype(BF16)
    for d in range(count):
        source = up.at[step, pl.ds(d * rows, rows)]
        start_block(order, me_ref, d, step, sides, sems.at[step, d], source, pl.ds(0, rows))
    down[step] = dot_tn(feed_grad_ref[...], active_ref[...]).astype(BF16)
    sem = count
    for j in range(fit):
        for f in range(shares):
            for k in range(2):
                source = down.at[step, pl.ds((2 * f + k) * half, half), pl.ds(j * wide, wide)]
                window = pl.ds(rows, half), pl.ds(k * wide, wide)
                start_block(order, me_ref, step * fit + j, f, sides, sems.at[step, sem], source, *window)
                sem += 1

    @pl.when(step == shares - 1)
    def _():
        for s in range(shares):
            for d in range(count):
                pltpu.make_async_copy(
                    up.at[s, pl.ds(0, rows)], keep_ref.at[0, pl.ds(0, rows)], sems.at[s, d]
                ).wait()
            for k in range(count, sem):
                pltpu.make_async_copy(
                    down.at[s, pl.ds(0, half), pl.ds(0, wide)],
                    keep_ref.at[0, pl.ds(rows, half), pl.ds(0, wide)],
                    sems.at[s, k],
                ).wait()


def feed_grads(me, normed, gate_grad, feed_grad, active, order, rows, half, wide, shares):
    tokens, model = normed.shape
    ff = active.shape[1]
    span = ff // shares
    chunk = pl.BlockSpec((tokens, span), lambda i: (0, i))
    if order is None:
        out_specs = [
            pl.BlockSpec((1, model, span), lambda i: (i, 0, 0)),
            pl.BlockSpec((model, span), lambda i: (0, i)),
        ]
        shapes = [(shares, model, span), (model, ff)]
        scratch = []
    else:
        out_specs = any_specs(2)
        shapes = [(shares * model // rows // 2, rows + half, span)] * 2
        copies = model // rows + 2 * shares * (span // wide)
        scratch = [
            pltpu.VMEM((shares, model, span), BF16),
            pltpu.VMEM((shares, model, span), BF16),
            pltpu.SemaphoreType.DMA((shares, copies)),
        ]
    return pl.pallas_call(
        functools.partial(feed_grad_body, order, rows, half, wide),
        grid=(shares,),
        in_specs=[SMEM_SPEC, full_spec(normed.shape), chunk, full_spec(feed_grad.shape), chunk],
        out_specs=out_specs,
        out_shape=[jax.ShapeDtypeStruct(shape, BF16) for shape in shapes],
        scratch_shapes=scratch,
        compiler_params=params_for(),
        cost_estimate=busy_for(1),
        name="feed_grads",
    )(me, normed, gate_grad, feed_grad, active)


def qkv_grad_body(order, rows, me_ref, normed_ref, mixed_grad_ref, context_ref, branch_ref, *refs):
    f = pl.program_id(0)
    slots, packed = refs[-3:-1] if order is not None else refs[-2:]
    shares, model, slim = slots.shape
    wide = mixed_grad_ref.shape[0]

    @pl.when(f == 0)
    def _():
        whole = dot_nn(context_ref[...], branch_ref[...]).astype(BF16)
        for k in range(shares):
            slots[k] = whole[:, k * slim : (k + 1) * slim]

    packed[f, :, :wide] = dot_nt(normed_ref[...], mixed_grad_ref[...]).astype(BF16)
    packed[f, :, wide:] = slots[f]
    if order is None:
        refs[0][...] = packed[f]
        return
    sems = refs[-1]
    count = model // rows
    for d in range(count):
        source = packed.at[f, pl.ds(d * rows, rows)]
        start_block(order, me_ref, d, f, refs[:2], sems.at[f, d], source)

    @pl.when(f == shares - 1)
    def _():
        for s in range(shares):
            for d in range(count):
                pltpu.make_async_copy(packed.at[s, pl.ds(0, rows)], refs[0].at[0], sems.at[s, d]).wait()


def qkv_grads(me, normed, mixed_grad, context, branch_grad, order, rows, wide):
    model, tokens = normed.shape
    shares = 3 * model // wide
    slim = model // shares
    cols = wide + slim
    if order is None:
        out_specs = [pl.BlockSpec((model, cols), lambda i: (i, 0))]
        shapes = [(shares * model, cols)]
        sems = []
    else:
        out_specs = any_specs(2)
        shapes = [(shares * model // rows // 2, rows, cols)] * 2
        sems = [pltpu.SemaphoreType.DMA((shares, model // rows))]
    return pl.pallas_call(
        functools.partial(qkv_grad_body, order, rows),
        grid=(shares,),
        in_specs=[
            SMEM_SPEC,
            full_spec(normed.shape),
            pl.BlockSpec((wide, tokens), lambda i: (i, 0)),
            full_spec(context.shape),
            full_spec(branch_grad.shape),
        ],
        out_specs=out_specs,
        out_shape=[jax.ShapeDtypeStruct(shape, BF16) for shape in shapes],
        scratch_shapes=[pltpu.VMEM((shares, model, slim), BF16), pltpu.VMEM((shares, model, cols), BF16)] + sems,
        compiler_params=params_for(),
        cost_estimate=busy_for(30),
        name="qkv_grads",
    )(me, normed, mixed_grad, context, branch_grad)


DP, FSDP = "dp", "fsdp"


def swap(value, axis, bit):
    size = lax.axis_size(axis)
    return lax.ppermute(value, axis, [(i, i ^ bit) for i in range(size)])


def after(value, *others):
    return lax.optimization_barrier((value,) + others)[0]


def grow(value, step, *others):
    arrived = swap(value, *step)
    if others:
        arrived = after(arrived, *others)
    return jnp.concatenate([value, arrived], axis=0)


def fold_body(plan, count, *refs):
    sums = []
    for k in range(count):
        sums.append(refs[2 * k][...].astype(F32) + refs[2 * k + 1][...].astype(F32))
    for out_ref, takes in zip(refs[2 * count :], plan):
        start = 0
        for pair, spot in takes:
            part = sums[pair][spot].astype(out_ref.dtype)
            rows = part.shape[-2]
            out_ref[..., start : start + rows, :] = part
            start += rows


def fold_call(pairs, plan, in_blocks, out_blocks, out_shapes, steps, dtype=BF16):
    def spec(block, along):
        return pl.BlockSpec(block, lambda i: tuple(i if k == along else 0 for k in range(len(block))))

    arrays = [array for pair in pairs for array in pair]
    return pl.pallas_call(
        functools.partial(fold_body, plan, len(pairs)),
        grid=(steps,),
        in_specs=[spec(*in_blocks[k // 2]) for k in range(len(arrays))],
        out_specs=[spec(*b) for b in out_blocks],
        out_shape=[jax.ShapeDtypeStruct(shape, dtype) for shape in out_shapes],
        compiler_params=params_for(),
        cost_estimate=busy_for(2),
        name="fold_sums",
    )(*arrays)


class Fold:
    def __init__(self, keep, send):
        self.rows, self.cols = keep.shape[1:]
        self.keep, self.arrived = keep, swap(send, *CORE)
        self.stage = 0

    def step(self, *others):
        rows, cols = self.rows, self.cols
        cut, sizes = rows // 2, (2, 2, 4, rows, cols)
        upper, lower = slice(0, cut), slice(cut, rows)
        everything = slice(None)
        keep = after(self.keep, *others)
        if self.stage == 0:
            outs = fold_call(
                [(keep.reshape(sizes), self.arrived.reshape(sizes))],
                [
                    [(0, (0, everything, everything, upper))],
                    [(0, (1, everything, everything, upper))],
                    [(0, (everything, 0, everything, lower))],
                    [(0, (everything, 1, everything, lower))],
                ],
                [((2, 2, 1, rows, cols), 2)],
                [((2, 1, cut, cols), 1)] * 4,
                [(2, 4, cut, cols)] * 4,
                4,
            )
            self.keep, sent = (outs[0], outs[2]), (outs[1], outs[3])
            self.arrived = swap(sent[0], *XS), swap(sent[1], *YS)
        elif self.stage == 1:
            outs = fold_call(
                list(zip(keep, self.arrived)),
                [[(0, 0)], [(0, 1)], [(1, 0)], [(1, 1)]],
                [((2, 4, cut, cols), None)] * 2,
                [((4, cut, cols), None)] * 4,
                [(4, cut, cols)] * 4,
                1,
            )
            self.keep, sent = (outs[0], outs[2]), (outs[1], outs[3])
            self.arrived = swap(sent[0], *YS), swap(sent[1], *XS)
        elif self.stage == 2:
            near, far = slice(0, 2), slice(2, 4)
            self.keep, sent = fold_call(
                list(zip(keep, self.arrived)),
                [[(0, near), (1, near)], [(0, far), (1, far)]],
                [((4, cut, cols), None)] * 2,
                [((2, rows, cols), None)] * 2,
                [(2, rows, cols)] * 2,
                1,
            )
            self.arrived = swap(sent, *Z_NEAR)
        elif self.stage == 3:
            self.keep, sent = fold_call(
                [(keep, self.arrived)],
                [[(0, 0)], [(0, 1)]],
                [((2, rows, cols), None)],
                [((rows, cols), None)] * 2,
                [(rows, cols)] * 2,
                1,
            )
            self.arrived = swap(sent, *Z_FAR)
        else:
            return keep.astype(F32) + self.arrived.astype(F32)
        self.stage += 1
        return sent


def rel_table(steps, last, off):
    places = []
    for pos in range(2 ** len(steps)):
        rel = {DP: 0, FSDP: 0}
        for k, (axis, bit) in enumerate(steps):
            if (pos >> k) & 1:
                rel[axis] ^= bit
        if last is not None:
            rel[last[0]] ^= last[1]
        places.append((rel[DP], rel[FSDP], off, True))
    return tuple(places)


CORE, XS, YS, Z_NEAR, Z_FAR = (FSDP, 1), (FSDP, 2), (DP, 1), (DP, 2), (DP, 4)
XY = [Z_FAR, Z_NEAR, XS, YS]
YX = [Z_FAR, Z_NEAR, YS, XS]


def grow_end(value, second, *others):
    value = grow(value, second[0], *others)
    value = grow(value, second[1])
    return value, swap(value, *CORE)


def order_of(steps):
    return [(axis == DP, bit) for axis, bit in steps]


def adam_step(weight, gradient, first_mom, second, clip_factor, step_rate, decay_rate):
    scaled = gradient * clip_factor
    first_new = 0.5 * first_mom + 0.5 * scaled
    second_new = 0.5 * second + 0.5 * scaled * scaled
    correction = 1.0 - 0.5**STEP
    update = first_new / correction / (jnp.sqrt(second_new / correction) + 1e-08)
    return (first_new, second_new, weight - step_rate * (update + decay_rate * weight))


def on_device(
    tokens,
    visible_index,
    cotangent,
    qkv_weight,
    out_weight,
    up_weight,
    down_weight,
    vectors,
    qkv_first,
    out_first,
    up_first,
    down_first,
    vector_first,
    qkv_second,
    out_second,
    up_second,
    down_second,
    vector_second,
):
    _, chip_count, seq_len, model_width = tokens.shape
    dp_size, fsdp_size = lax.axis_size(DP), lax.axis_size(FSDP)
    device_count = dp_size * fsdp_size
    both = (DP, FSDP)
    block_count = dp_size
    block_seen = seq_len // block_count
    block_len = cotangent.shape[2]
    chips_group = chip_count * block_count
    rows, wide = qkv_weight.shape
    slim = out_weight.shape[1]
    span = up_weight.shape[1]
    ff_width = span * fsdp_size
    half = slim // 2
    tall = down_weight.shape[0]
    folded = (dp_size, fsdp_size) == (8, 4)

    share_q = jnp.concatenate([qkv_weight, out_weight], axis=1).astype(BF16)
    share_u = up_weight.astype(BF16)
    down_turned = down_weight.astype(BF16).T

    vec_rows, vec_cols = vectors.shape
    vector_copies = jnp.broadcast_to(vectors.astype(BF16), (device_count, vec_rows, vec_cols))
    vec_shares = lax.all_to_all(vector_copies, both, split_axis=0, concat_axis=0, tiled=True)
    vec = vec_shares.reshape(dp_size, fsdp_size, vec_rows, vec_cols).transpose(1, 2, 0, 3)
    vec = vec.reshape(fsdp_size * vec_rows, model_width).astype(F32)

    my_block = lax.axis_index(DP)
    places = visible_index[0].reshape(chips_group, block_count, block_seen)
    places = lax.dynamic_index_in_dim(places, my_block, 1, keepdims=False) - my_block * block_len
    seen_places = places
    cot = cotangent[0]
    whole_tiles = block_seen % 16 == 0
    if whole_tiles:
        places = jnp.pad(places, ((0, 0), (0, 128 - block_seen)), constant_values=-1)[:, None]
        cot_seen, mask_grad = seen_rows(cot, places, block_seen)
    else:
        slot_ids = lax.broadcasted_iota(jnp.int32, (chips_group, block_len, block_seen), 1)
        pick = (places[:, None, :] == slot_ids).astype(BF16)
        gaps = 1.0 - jnp.sum(pick.astype(F32), axis=-1)
        cot_seen = jnp.einsum("cpv,cpd->cvd", pick, cot, preferred_element_type=F32).astype(BF16)
        mask_grad = jnp.einsum("cp,cpd->d", gaps.astype(BF16), cot, preferred_element_type=F32)[None]
    if folded:
        me = jnp.stack([lax.axis_index(DP), lax.axis_index(FSDP)]).astype(jnp.int32)
        share_d = jnp.concatenate([down_turned[:half], down_turned[half:]], axis=1)
        cut = rows // 2
        cur = grow(grow(share_q[None], Z_FAR, cot_seen), Z_NEAR)
        q_upper, q_lower = grow(cur[:, :cut], XS, vec_shares), grow(cur[:, cut:], YS, vec_shares)
        q_upper, q_lower = grow(q_upper, YS), grow(q_lower, XS)
        q_arrays = (q_upper, swap(q_upper, *CORE), q_lower, swap(q_lower, *CORE))
        q_table = (
            rel_table(XY, None, 0),
            rel_table(XY, CORE, 0),
            rel_table(YX, None, cut),
            rel_table(YX, CORE, cut),
        )
        gathered = lax.all_gather(jnp.concatenate([share_u, share_d]), both, axis=0, tiled=False)
        u_arrays = d_arrays = (gathered,)
        u_table = d_table = (tuple((d, f, 0, False) for d in range(dp_size) for f in range(fsdp_size)),)
        order = order_of([CORE, XS, YS, Z_NEAR, Z_FAR])
        down_share = (half, tall)
        load_rows = rows
    else:
        me = jnp.zeros((2,), jnp.int32)

        def gather_whole(share):
            whole = lax.all_gather(share, both, axis=0, tiled=False)
            whole = whole.reshape((dp_size, fsdp_size) + share.shape).transpose(1, 0, 2, 3)
            return whole.reshape(fsdp_size, dp_size * share.shape[0], share.shape[1])

        q_arrays = (gather_whole(share_q),)
        u_arrays = (gather_whole(share_u),)
        down_whole = lax.all_gather(down_turned, both, axis=0, tiled=False)
        down_whole = down_whole.reshape(dp_size, fsdp_size, slim, tall).transpose(1, 2, 0, 3)
        d_arrays = (down_whole.reshape(1, model_width, ff_width),)
        q_table = u_table = (tuple((0, f, 0, False) for f in range(fsdp_size)),)
        d_table = (((0, 0, 0, False),),)
        order = None
        down_share = None
        load_rows = model_width

    cot_seen = cot_seen.reshape(block_count, chip_count, block_seen, model_width)
    grad = lax.all_to_all(cot_seen, DP, split_axis=0, concat_axis=0, tiled=True)
    if not whole_tiles:
        grad = grad.transpose(1, 0, 2, 3).reshape(1, chip_count, seq_len, model_width)

    x = tokens[0]
    up_bias = vec[6:10].reshape(1, ff_width)
    value_bias = vec[2].reshape(model_width, 1)
    normed, mixed, expo, share, context, qkv_whole, out_whole = attend_forward(
        me, x, vec, value_bias, q_table, q_arrays, load_rows, wide
    )
    if folded:
        context = after(context, grad)
    result, normed_two, active, gate_grad, feed_grad, middle_grad, branch_grad, context_grad, sums_two, up_sums = (
        feed_forward_back(
            me, grad, x, context, vec, up_bias, out_whole, u_table, u_arrays, d_table, d_arrays, load_rows, down_share
        )
    )
    feed_blocks = feed_grads(me, normed_two, gate_grad, feed_grad, active, order, rows, half, tall, fsdp_size)
    if folded:
        feed_fold = Fold(*feed_blocks)
        context_grad = after(context_grad, *feed_blocks)
    mixed_grad, sums_value = attend_back(mixed, expo, share, context_grad)
    if folded:
        normed = after(normed, feed_fold.step(mixed_grad))
    q_blocks = qkv_grads(me, normed, mixed_grad, context, branch_grad, order, rows, wide)
    if folded:
        result = after(result, *q_blocks)
    if not whole_tiles:
        result = result.reshape(chip_count, block_count, block_seen, model_width).transpose(1, 0, 2, 3)
    arrived = lax.all_to_all(result, DP, split_axis=0, concat_axis=0, tiled=True)
    arrived = arrived.reshape(chips_group, block_seen, model_width)
    if folded:
        q_fold = Fold(*q_blocks)
        x = after(x, *q_blocks)
    tokens_grad, sums_one = tokens_back(x, middle_grad, mixed_grad, vec, qkv_whole)

    slot_ids = lax.broadcasted_iota(jnp.int32, (chips_group, block_len, block_seen), 1)
    pick = (seen_places[:, None, :] == slot_ids).astype(BF16)
    gaps = 1.0 - jnp.sum(pick.astype(F32), axis=-1)
    filled = jnp.einsum("cpv,cvd->cpd", pick, arrived, preferred_element_type=F32)
    filled = filled + gaps[..., None] * vec[11]
    full_layout = filled.astype(BF16).reshape(1, chips_group, block_len, model_width)

    if folded:
        feed_fold.step(tokens_grad)
        q_fold.step(tokens_grad)
        feed_fold.step()
        q_fold.step(arrived)
        feed_fold.step()
        q_fold.step()
        feed_sum = feed_fold.step()
        u_sum, d_sum = feed_sum[:rows], feed_sum[rows:]
        q_fold.step()
        q_sum = q_fold.step()
        d_sum = jnp.concatenate([d_sum[:, :tall], d_sum[:, tall:]], axis=0).T
    else:

        def scatter_whole(whole):
            cols = whole.shape[2]
            pieces = whole.reshape(fsdp_size, dp_size, -1, cols).transpose(1, 0, 2, 3)
            pieces = pieces.reshape(-1, cols)
            return lax.psum_scatter(pieces, both, scatter_dimension=0, tiled=True).astype(F32)

        q_sum, u_sum = scatter_whole(q_blocks[0].reshape(fsdp_size, model_width, -1)), scatter_whole(feed_blocks[0])
        pieces = feed_blocks[1].reshape(fsdp_size, slim, dp_size, tall).transpose(2, 0, 1, 3)
        pieces = pieces.reshape(device_count * slim, tall)
        d_sum = lax.psum_scatter(pieces, both, scatter_dimension=0, tiled=True).astype(F32).T

    vector_grad = jnp.concatenate(
        [
            sums_one[:2],
            sums_value[:1],
            sums_two[:3],
            up_sums.reshape(-1, model_width),
            sums_two[3:4],
            mask_grad,
        ],
        axis=0,
    )
    parts = vector_grad.reshape(fsdp_size, vec_rows, dp_size, vec_cols).transpose(2, 0, 1, 3)
    parts = parts.reshape(device_count, vec_rows, vec_cols)
    parts = lax.all_to_all(parts, both, split_axis=0, concat_axis=0, tiled=True)
    shares = (q_sum[:, :wide], q_sum[:, wide:], u_sum, d_sum, jnp.sum(parts, axis=0))
    squares = jnp.sum(q_sum * q_sum) + jnp.sum(u_sum * u_sum) + jnp.sum(d_sum * d_sum)
    squares = squares + jnp.sum(shares[4] * shares[4])
    square_parts = jnp.broadcast_to(squares, (device_count, 1))
    grad_total = jnp.sum(lax.all_to_all(square_parts, both, split_axis=0, concat_axis=0, tiled=True))
    grad_norm = jnp.sqrt(grad_total)
    tokens_all = device_count * chip_count * seq_len
    threshold = 0.05 * model_width * math.sqrt(tokens_all)
    clip = jnp.minimum(1.0, threshold / grad_norm)
    rate = 0.6 / math.sqrt(model_width)
    out_rate = 0.6 / math.sqrt(model_width // 32)
    down_rate = 0.6 / math.sqrt(ff_width)
    qkv_out = adam_step(qkv_weight, shares[0], qkv_first, qkv_second, clip, rate, 0.05)
    out_out = adam_step(out_weight, shares[1], out_first, out_second, clip, out_rate, 0.05)
    up_out = adam_step(up_weight, shares[2], up_first, up_second, clip, rate, 0.05)
    down_out = adam_step(down_weight, shares[3], down_first, down_second, clip, down_rate, 0.05)
    vec_out = adam_step(vectors, shares[4], vector_first, vector_second, clip, 0.45, 0.0)
    return (
        full_layout,
        tokens_grad[None],
        *qkv_out,
        qkv_out[2].astype(BF16),
        *out_out,
        out_out[2].astype(BF16),
        *up_out,
        up_out[2].astype(BF16),
        *down_out,
        down_out[2].astype(BF16),
        *vec_out,
        grad_norm,
    )


def solution(mesh):
    grid = P("dp", "fsdp")
    table = P("fsdp", "dp")
    weights = (grid, grid, grid, grid, table)
    in_specs = (
        P("fsdp", "dp", None, None),
        P("fsdp", None, None),
        P("fsdp", None, "dp", None),
        *weights,
        *weights,
        *weights,
    )
    out_specs = (
        P("fsdp", None, "dp", None),
        P("fsdp", "dp", None, None),
        *(grid,) * 16,
        *(table,) * 3,
        P(),
    )
    return jax.shard_map(
        on_device, mesh=mesh, in_specs=in_specs, out_specs=out_specs, check_vma=False
    )
```

```python
import functools
import math

import jax
import jax.numpy as jnp
from jax import lax
from jax.experimental import pallas as pl
from jax.experimental.pallas import tpu as pltpu
from jax.sharding import PartitionSpec as P

HD = 64
HEAD_GROUP = 6
STEP = 10
F32 = jnp.float32
BF16 = jnp.bfloat16
VMEM_BYTES = 66_900_000


def params_for(**more):
    return pltpu.CompilerParams(vmem_limit_bytes=VMEM_BYTES, **more)


def busy_for(micros):
    return pl.CostEstimate(flops=micros * 10**9, bytes_accessed=micros * 3 * 10**6, transcendentals=0)


def dot_nn(left, right):
    return lax.dot_general(left, right, (((1,), (0,)), ((), ())), preferred_element_type=F32)


def dot_nt(left, right):
    return lax.dot_general(left, right, (((1,), (1,)), ((), ())), preferred_element_type=F32)


def dot_tn(left, right):
    return lax.dot_general(left, right, (((0,), (0,)), ((), ())), preferred_element_type=F32)


def norm_parts(values):
    center = values - jnp.mean(values, axis=-1, keepdims=True)
    spread = jnp.mean(center * center, axis=-1, keepdims=True)
    factor = lax.rsqrt(spread + 1e-05)
    return center * factor, factor


def norm_back(grad, hat, factor, gain):
    scaled = grad * gain
    inner = jnp.mean(scaled * hat, axis=-1, keepdims=True)
    return factor * (scaled - jnp.mean(scaled, axis=-1, keepdims=True) - hat * inner)


def gelu_pair(gate):
    cdf = 0.5 + 0.5 * lax.erf(gate * 0.5**0.5)
    bell = jnp.exp2(gate * gate * (-0.5 * math.log2(math.e))) * (0.5 / math.pi) ** 0.5
    return gate * cdf, cdf + gate * bell


def load_grid(table, refs, me_ref, dest, sems, rows, first=0, start=True):
    copies = []
    for ref, places in zip(refs, table):
        for pos, (rel_d, rel_f, off, turned) in enumerate(places):
            d = rel_d ^ me_ref[0] if turned else rel_d
            f = rel_f ^ me_ref[1] if turned else rel_f
            height = min(ref.shape[1], rows)
            row = pl.multiple_of(d * rows + off, 16)
            copy = pltpu.make_async_copy(
                ref.at[pos, pl.ds(0, height)], dest.at[f, pl.ds(row, height)], sems.at[first + len(copies)]
            )
            if start:
                copy.start()
            copies.append(copy)
    return copies


def load_down(table, refs, me_ref, dest, sems, share, first=0, start=True):
    copies = []
    for ref, places in zip(refs, table):
        for pos, (rel_d, rel_f, off, turned) in enumerate(places):
            if share is None:
                pairs = [(ref.at[pos], dest)]
            else:
                half, wide = share
                d = rel_d ^ me_ref[0] if turned else rel_d
                f = rel_f ^ me_ref[1] if turned else rel_f
                lane = pl.multiple_of(d * wide, 128)
                pairs = []
                for k in range(2):
                    row = pl.multiple_of(f * (2 * half) + k * half + off, 16)
                    pairs.append(
                        (
                            ref.at[pos, pl.ds(ref.shape[1] - half, half), pl.ds(k * wide, wide)],
                            dest.at[pl.ds(row, half), pl.ds(lane, wide)],
                        )
                    )
            for src, dst in pairs:
                copy = pltpu.make_async_copy(src, dst, sems.at[first + len(copies)])
                if start:
                    copy.start()
                copies.append(copy)
    return copies


def any_specs(count):
    return [pl.BlockSpec(memory_space=pl.ANY)] * count


SMEM_SPEC = pl.BlockSpec(memory_space=pltpu.SMEM)


def full_spec(shape):
    return pl.BlockSpec(shape, lambda i: (0,) * len(shape))


def seen_body(seen, *refs):
    cot_refs, (places_ref, out_ref, sum_ref) = refs[:-3], refs[-3:]
    count, length, _ = cot_refs[0].shape
    depth = places_ref.shape[1]

    @pl.when(pl.program_id(0) == 0)
    def _():
        sum_ref[...] = jnp.zeros_like(sum_ref)

    lane = lax.broadcasted_iota(jnp.int32, (depth, length), 1)
    row = lax.broadcasted_iota(jnp.int32, (depth, length), 0)
    for k in range(count * len(cot_refs)):
        pick = jnp.where((lane == places_ref[k]) | (row == seen), 1.0, 0.0).astype(BF16)
        rows = dot_nn(pick, cot_refs[k // count][k % count])
        out_ref[k] = rows[:seen].astype(BF16)
        sum_ref[...] += rows[seen : seen + 1] - jnp.sum(rows[:seen], axis=0, keepdims=True)


def seen_rows(cot, places, seen):
    chips, length, model = cot.shape
    streams, step = 4, 8

    def stream(k):
        return pl.BlockSpec((step // streams, length, model), lambda i: (i * streams + k, 0, 0))

    return pl.pallas_call(
        functools.partial(seen_body, seen),
        grid=(chips // step,),
        in_specs=[stream(k) for k in range(streams)]
        + [pl.BlockSpec((step,) + places.shape[1:], lambda i: (i, 0, 0))],
        out_specs=[pl.BlockSpec((step, seen, model), lambda i: (i, 0, 0)), full_spec((1, model))],
        out_shape=[
            jax.ShapeDtypeStruct((chips, seen, model), BF16),
            jax.ShapeDtypeStruct((1, model), F32),
        ],
        compiler_params=params_for(),
        cost_estimate=busy_for(8),
        name="seen_rows",
    )(*[cot] * streams, places)


def attend_body(table, rows, heads, wide, *refs):
    n = len(table)
    me_ref, x_ref, vec_ref, bias_ref = refs[:4]
    w_refs = refs[4 : 4 + n]
    normed_ref, mixed_ref, expo_ref, share_ref, context_ref, qkv_out, out_out = refs[4 + n : 11 + n]
    qkv_ref, out_ref, weight, sems = refs[11 + n :]
    shares, model, cols = weight.shape
    slim = cols - wide
    step, last = pl.program_id(0), pl.num_programs(0) - 1
    count = sum(len(t) for t in table)
    saves = [
        pltpu.make_async_copy(qkv_ref, qkv_out, sems.at[count]),
        pltpu.make_async_copy(out_ref, out_out, sems.at[count + 1]),
    ]

    @pl.when(step == 0)
    def _():
        load_grid(table, w_refs, me_ref, weight, sems, rows)

    hat, _ = norm_parts(x_ref[0].astype(F32))
    normed = (hat * vec_ref[0:1, :] + vec_ref[1:2, :]).astype(BF16)
    normed_ref[...] = normed.T

    @pl.when(step == 0)
    def _():
        for copy in load_grid(table, w_refs, me_ref, weight, sems, rows, start=False):
            copy.wait()
        up_to = -(-wide // 128) * 128
        for f in range(shares):
            qkv_ref[f * wide : (f + 1) * wide, :] = weight[f, :, :up_to].T[:wide]
            out_ref[:, f * slim : (f + 1) * slim] = weight[f, :, wide:]
        for copy in saves:
            copy.start()

    for part in range(3):
        spot = slice(part * model, (part + 1) * model)
        mixed = dot_nt(qkv_ref[spot, :], normed)
        if part == 2:
            mixed = mixed + bias_ref[...]
        mixed_ref[spot, :] = mixed.astype(BF16)
    for first in range(0, heads, HEAD_GROUP):
        group = range(first, first + HEAD_GROUP)
        part = lambda which, head: mixed_ref[which * model + HD * head : which * model + HD * (head + 1), :]
        scores = [dot_tn(part(1, head), part(0, head) * jnp.asarray(HD ** (-0.5), BF16)) for head in group]
        expos = [jnp.exp(score - jnp.max(score, axis=0, keepdims=True)) for score in scores]
        shares = [1.0 / jnp.sum(expo, axis=0, keepdims=True) for expo in expos]
        expos = [expo.astype(BF16) for expo in expos]
        contexts = [dot_nn(part(2, head), expo) for head, expo in zip(group, expos)]
        for head, expo, share, context in zip(group, expos, shares, contexts):
            share_ref[head : head + 1, :] = share
            expo_ref[0, head] = expo
            context_ref[HD * head : HD * (head + 1), :] = (context * share).astype(BF16)

    @pl.when(step == last)
    def _():
        for copy in saves:
            copy.wait()


def attend_forward(me, x, vec, bias, table, arrays, rows, wide):
    chips, seq, model = x.shape
    heads = model // HD
    cols = arrays[0].shape[-1]
    shares = 3 * model // wide
    count = sum(len(t) for t in table)
    tall = lambda h: pl.BlockSpec((h, seq), lambda i: (0, i))
    tokens = chips * seq
    return pl.pallas_call(
        functools.partial(attend_body, table, rows, heads, wide),
        grid=(chips,),
        in_specs=[
            SMEM_SPEC,
            pl.BlockSpec((1, seq, model), lambda i: (i, 0, 0)),
            full_spec(vec.shape),
            full_spec(bias.shape),
        ]
        + any_specs(len(arrays)),
        out_specs=[
            tall(model),
            tall(3 * model),
            pl.BlockSpec((1, heads, seq, seq), lambda i: (i, 0, 0, 0)),
            tall(heads),
            tall(model),
        ]
        + any_specs(2),
        out_shape=[
            jax.ShapeDtypeStruct((model, tokens), BF16),
            jax.ShapeDtypeStruct((3 * model, tokens), BF16),
            jax.ShapeDtypeStruct((chips, heads, seq, seq), BF16),
            jax.ShapeDtypeStruct((heads, tokens), F32),
            jax.ShapeDtypeStruct((model, tokens), BF16),
            jax.ShapeDtypeStruct((3 * model, model), BF16),
            jax.ShapeDtypeStruct((model, model), BF16),
        ],
        scratch_shapes=[
            pltpu.VMEM((3 * model, model), BF16),
            pltpu.VMEM((model, model), BF16),
            pltpu.VMEM((shares, model, cols), BF16),
            pltpu.SemaphoreType.DMA((count + 2,)),
        ],
        compiler_params=params_for(),
        cost_estimate=busy_for(1),
        name="attend_forward",
    )(me, x, vec, bias, *arrays)


def feed_body(u_table, d_table, rows, share, *refs):
    nu, nd = len(u_table), len(d_table)
    me_ref, grad_ref, x_ref, context_ref, vec_ref, bias_ref, out_ref = refs[:7]
    u_refs = refs[7 : 7 + nu]
    d_refs = refs[7 + nu : 7 + nu + nd]
    (
        result_ref,
        normed_ref,
        active_ref,
        gate_grad_ref,
        feed_grad_ref,
        middle_grad_ref,
        branch_grad_ref,
        context_grad_ref,
        sums_ref,
        bias_sums_ref,
        up,
        down,
        sems,
    ) = refs[7 + nu + nd :]
    count = sum(len(t) for t in u_table)
    shares, model, span = up.shape
    seq = x_ref.shape[1]
    first_step = pl.program_id(0) == 0

    @pl.when(first_step)
    def _():
        load_grid(u_table, u_refs, me_ref, up, sems, rows)
        load_down(d_table, d_refs, me_ref, down, sems, share, first=count)
        sums_ref[...] = jnp.zeros_like(sums_ref)
        bias_sums_ref[...] = jnp.zeros_like(bias_sums_ref)

    feed_grad = grad_ref[:, 0].reshape(seq, model)
    feed_grad_ref[...] = feed_grad
    middle = x_ref[0].astype(F32) + dot_tn(context_ref[...], out_ref[...]) + vec_ref[3:4, :]
    hat, factor = norm_parts(middle)
    gain = vec_ref[4:5, :]
    normed = (hat * gain + vec_ref[5:6, :]).astype(BF16)
    normed_ref[...] = normed

    @pl.when(first_step)
    def _():
        for copy in load_grid(u_table, u_refs, me_ref, up, sems, rows, start=False):
            copy.wait()

    def gate_of(f):
        return dot_nn(normed, up[f]) + bias_ref[:, f * span : (f + 1) * span]

    gate = gate_of(0)

    @pl.when(first_step)
    def _():
        for copy in load_down(d_table, d_refs, me_ref, down, sems, share, first=count, start=False):
            copy.wait()

    def active_grad_of(f):
        return dot_nn(feed_grad, down[:, f * span : (f + 1) * span])

    normed_grad = jnp.zeros((seq, model), F32)
    result = middle + vec_ref[10:11, :]
    ready = gate, active_grad_of(0)
    for f in range(shares):
        lanes = slice(f * span, (f + 1) * span)
        gate, active_grad = ready
        if f + 1 < shares:
            ready = gate_of(f + 1), active_grad_of(f + 1)
        active, slope = gelu_pair(gate)
        active = active.astype(BF16)
        gate_grad = (active_grad * slope).astype(BF16)
        active_ref[:, lanes] = active
        gate_grad_ref[:, lanes] = gate_grad
        result += dot_nt(active, down[:, lanes])
        normed_grad += dot_nt(gate_grad, up[f])
        bias_sums_ref[:, lanes] += jnp.sum(gate_grad.astype(F32), axis=0, keepdims=True)
    result_ref[:, 0] = result.astype(BF16).reshape(result_ref.shape[0], -1, model)
    grad_full = feed_grad.astype(F32)
    middle_grad = grad_full + norm_back(normed_grad, hat, factor, gain)
    middle_grad_ref[0] = middle_grad
    branch_grad = middle_grad.astype(BF16)
    branch_grad_ref[...] = branch_grad
    context_grad_ref[...] = dot_nt(out_ref[...], branch_grad).astype(BF16)
    sums_ref[0:1, :] += jnp.sum(branch_grad.astype(F32), axis=0, keepdims=True)
    sums_ref[1:2, :] += jnp.sum(normed_grad * hat, axis=0, keepdims=True)
    sums_ref[2:3, :] += jnp.sum(normed_grad, axis=0, keepdims=True)
    sums_ref[3:4, :] += jnp.sum(grad_full, axis=0, keepdims=True)


def feed_forward_back(
    me, grad, x, context, vec, bias, out_whole, u_table, u_arrays, d_table, d_arrays, rows, share
):
    chips, seq, model = x.shape
    ff = bias.shape[1]
    blocks, _, seen, _ = grad.shape
    span = u_arrays[0].shape[-1]
    shares = ff // span
    tokens = chips * seq
    count = sum(len(t) for t in u_table) + 2 * sum(len(t) for t in d_table)
    tile = pl.BlockSpec((1, seq, model), lambda i: (i, 0, 0))
    flat = lambda w: pl.BlockSpec((seq, w), lambda i: (i, 0))
    tall = pl.BlockSpec((model, seq), lambda i: (0, i))
    spread = pl.BlockSpec((blocks, 1, seen, model), lambda i: (0, i, 0, 0))
    rows_of = lambda w: jax.ShapeDtypeStruct((tokens, w), BF16)
    return pl.pallas_call(
        functools.partial(feed_body, u_table, d_table, rows, share),
        grid=(chips,),
        in_specs=[
            SMEM_SPEC,
            spread,
            tile,
            tall,
            full_spec(vec.shape),
            full_spec(bias.shape),
            full_spec(out_whole.shape),
        ]
        + any_specs(len(u_arrays) + len(d_arrays)),
        out_specs=[
            spread,
            flat(model),
            flat(ff),
            flat(ff),
            flat(model),
            tile,
            flat(model),
            tall,
            full_spec((8, model)),
            full_spec((1, ff)),
        ],
        out_shape=[
            jax.ShapeDtypeStruct(grad.shape, BF16),
            rows_of(model),
            rows_of(ff),
            rows_of(ff),
            rows_of(model),
            jax.ShapeDtypeStruct((chips, seq, model), F32),
            rows_of(model),
            jax.ShapeDtypeStruct((model, tokens), BF16),
            jax.ShapeDtypeStruct((8, model), F32),
            jax.ShapeDtypeStruct((1, ff), F32),
        ],
        scratch_shapes=[
            pltpu.VMEM((shares, model, span), BF16),
            pltpu.VMEM((model, ff), BF16),
            pltpu.SemaphoreType.DMA((count,)),
        ],
        compiler_params=params_for(),
        cost_estimate=busy_for(10),
        name="feed_forward_back",
    )(me, grad, x, context, vec, bias, out_whole, *u_arrays, *d_arrays)


def attend_back_body(heads, mixed_ref, expo_ref, share_ref, grad_ref, mixed_grad_ref, sums_ref):
    model, seq = grad_ref.shape

    @pl.when(pl.program_id(0) == 0)
    def _():
        sums_ref[...] = jnp.zeros_like(sums_ref)

    scale = jnp.asarray(HD ** (-0.5), BF16)
    for first in range(0, heads, HEAD_GROUP):
        group = range(first, first + HEAD_GROUP)
        spot = lambda which, head: slice(which * model + HD * head, which * model + HD * (head + 1))
        shares = [share_ref[head : head + 1, :] for head in group]
        out_grads = [
            (grad_ref[spot(0, head), :].astype(F32) * share).astype(BF16) for head, share in zip(group, shares)
        ]
        prob_grads = [dot_tn(mixed_ref[spot(2, head), :], grad) for head, grad in zip(group, out_grads)]
        value_grads = [dot_nt(grad, expo_ref[0, head]) for head, grad in zip(group, out_grads)]
        score_grads = []
        for head, share, prob_grad in zip(group, shares, prob_grads):
            expo = expo_ref[0, head].astype(F32)
            weighted = expo * prob_grad
            inner = jnp.sum(weighted, axis=0, keepdims=True) * share
            score_grads.append((weighted - expo * inner).astype(BF16))
        query_grads = [dot_nn(mixed_ref[spot(1, head), :] * scale, grad) for head, grad in zip(group, score_grads)]
        key_grads = [dot_nt(mixed_ref[spot(0, head), :] * scale, grad) for head, grad in zip(group, score_grads)]
        for head, *grads in zip(group, query_grads, key_grads, value_grads):
            for which in range(3):
                mixed_grad_ref[spot(which, head), :] = grads[which].astype(BF16)
    sums_ref[...] += dot_nt(jnp.ones((8, seq), BF16), mixed_grad_ref[2 * model :, :])


def attend_back(mixed, expo, share, context_grad):
    model, tokens = context_grad.shape
    chips, heads, seq, _ = expo.shape
    tall = lambda h: pl.BlockSpec((h, seq), lambda i: (0, i))
    return pl.pallas_call(
        functools.partial(attend_back_body, heads),
        grid=(chips,),
        in_specs=[
            tall(3 * model),
            pl.BlockSpec((1, heads, seq, seq), lambda i: (i, 0, 0, 0)),
            tall(heads),
            tall(model),
        ],
        out_specs=[tall(3 * model), full_spec((8, model))],
        out_shape=[
            jax.ShapeDtypeStruct((3 * model, tokens), BF16),
            jax.ShapeDtypeStruct((8, model), F32),
        ],
        compiler_params=params_for(),
        cost_estimate=busy_for(1),
        name="attend_back",
    )(mixed, expo, share, context_grad)


def tokens_back_body(x_ref, grad_ref, mixed_grad_ref, vec_ref, qkv_ref, tokens_ref, sums_ref):
    @pl.when(pl.program_id(0) == 0)
    def _():
        sums_ref[...] = jnp.zeros_like(sums_ref)

    normed_grad = dot_tn(mixed_grad_ref[...], qkv_ref[...])
    hat, factor = norm_parts(x_ref[0].astype(F32))
    tokens_ref[0] = grad_ref[0] + norm_back(normed_grad, hat, factor, vec_ref[0:1, :])
    sums_ref[0:1, :] += jnp.sum(normed_grad * hat, axis=0, keepdims=True)
    sums_ref[1:2, :] += jnp.sum(normed_grad, axis=0, keepdims=True)


def tokens_back(x, middle_grad, mixed_grad, vec, qkv_whole):
    chips, seq, model = x.shape
    tile = pl.BlockSpec((1, seq, model), lambda i: (i, 0, 0))
    return pl.pallas_call(
        tokens_back_body,
        grid=(chips,),
        in_specs=[
            tile,
            tile,
            pl.BlockSpec((3 * model, seq), lambda i: (0, i)),
            full_spec(vec.shape),
            full_spec(qkv_whole.shape),
        ],
        out_specs=[tile, full_spec((8, model))],
        out_shape=[
            jax.ShapeDtypeStruct((chips, seq, model), F32),
            jax.ShapeDtypeStruct((8, model), F32),
        ],
        compiler_params=params_for(),
        cost_estimate=busy_for(25),
        name="tokens_back",
    )(x, middle_grad, mixed_grad, vec, qkv_whole)


def start_block(order, me_ref, d, f, sides, sem, source, *window):
    rel_d, rel_f = d ^ me_ref[0], f ^ me_ref[1]
    bits = [((rel_d if is_dp else rel_f) // value) % 2 for is_dp, value in order]
    pos = 0
    for bit in bits[1:]:
        pos = pos * 2 + bit
    for side, ref in enumerate(sides):

        @pl.when(bits[0] == side)
        def _():
            pltpu.make_async_copy(source, ref.at[(pos,) + window], sem).start()


def feed_grad_body(order, rows, half, wide, me_ref, normed_ref, gate_grad_ref, feed_grad_ref, active_ref, *refs):
    step = pl.program_id(0)
    if order is None:
        refs[0][0] = dot_tn(normed_ref[...], gate_grad_ref[...]).astype(BF16)
        refs[1][...] = dot_tn(feed_grad_ref[...], active_ref[...]).astype(BF16)
        return
    keep_ref, send_ref, up, down, sems = refs
    shares, model, span = up.shape
    count, fit = model // rows, span // wide
    sides = keep_ref, send_ref
    base = step * count * 2
    up[step] = dot_tn(normed_ref[...], gate_grad_ref[...]).astype(BF16)
    for d in range(count):
        source = up.at[step, pl.ds(d * rows, rows)]
        start_block(order, me_ref, d, step, sides, sems.at[step, d], source, pl.ds(0, rows))
    down[step] = dot_tn(feed_grad_ref[...], active_ref[...]).astype(BF16)
    sem = count
    for j in range(fit):
        for f in range(shares):
            for k in range(2):
                source = down.at[step, pl.ds((2 * f + k) * half, half), pl.ds(j * wide, wide)]
                window = pl.ds(rows, half), pl.ds(k * wide, wide)
                start_block(order, me_ref, step * fit + j, f, sides, sems.at[step, sem], source, *window)
                sem += 1

    @pl.when(step == shares - 1)
    def _():
        for s in range(shares):
            for d in range(count):
                pltpu.make_async_copy(
                    up.at[s, pl.ds(0, rows)], keep_ref.at[0, pl.ds(0, rows)], sems.at[s, d]
                ).wait()
            for k in range(count, sem):
                pltpu.make_async_copy(
                    down.at[s, pl.ds(0, half), pl.ds(0, wide)],
                    keep_ref.at[0, pl.ds(rows, half), pl.ds(0, wide)],
                    sems.at[s, k],
                ).wait()


def feed_grads(me, normed, gate_grad, feed_grad, active, order, rows, half, wide, shares):
    tokens, model = normed.shape
    ff = active.shape[1]
    span = ff // shares
    chunk = pl.BlockSpec((tokens, span), lambda i: (0, i))
    if order is None:
        out_specs = [
            pl.BlockSpec((1, model, span), lambda i: (i, 0, 0)),
            pl.BlockSpec((model, span), lambda i: (0, i)),
        ]
        shapes = [(shares, model, span), (model, ff)]
        scratch = []
    else:
        out_specs = any_specs(2)
        shapes = [(shares * model // rows // 2, rows + half, span)] * 2
        copies = model // rows + 2 * shares * (span // wide)
        scratch = [
            pltpu.VMEM((shares, model, span), BF16),
            pltpu.VMEM((shares, model, span), BF16),
            pltpu.SemaphoreType.DMA((shares, copies)),
        ]
    return pl.pallas_call(
        functools.partial(feed_grad_body, order, rows, half, wide),
        grid=(shares,),
        in_specs=[SMEM_SPEC, full_spec(normed.shape), chunk, full_spec(feed_grad.shape), chunk],
        out_specs=out_specs,
        out_shape=[jax.ShapeDtypeStruct(shape, BF16) for shape in shapes],
        scratch_shapes=scratch,
        compiler_params=params_for(),
        cost_estimate=busy_for(1),
        name="feed_grads",
    )(me, normed, gate_grad, feed_grad, active)


def qkv_grad_body(order, rows, me_ref, normed_ref, mixed_grad_ref, context_ref, branch_ref, *refs):
    f = pl.program_id(0)
    slots, packed = refs[-3:-1] if order is not None else refs[-2:]
    shares, model, slim = slots.shape
    wide = mixed_grad_ref.shape[0]

    @pl.when(f == 0)
    def _():
        whole = dot_nn(context_ref[...], branch_ref[...]).astype(BF16)
        for k in range(shares):
            slots[k] = whole[:, k * slim : (k + 1) * slim]

    packed[f, :, :wide] = dot_nt(normed_ref[...], mixed_grad_ref[...]).astype(BF16)
    packed[f, :, wide:] = slots[f]
    if order is None:
        refs[0][...] = packed[f]
        return
    sems = refs[-1]
    count = model // rows
    for d in range(count):
        source = packed.at[f, pl.ds(d * rows, rows)]
        start_block(order, me_ref, d, f, refs[:2], sems.at[f, d], source)

    @pl.when(f == shares - 1)
    def _():
        for s in range(shares):
            for d in range(count):
                pltpu.make_async_copy(packed.at[s, pl.ds(0, rows)], refs[0].at[0], sems.at[s, d]).wait()


def qkv_grads(me, normed, mixed_grad, context, branch_grad, order, rows, wide):
    model, tokens = normed.shape
    shares = 3 * model // wide
    slim = model // shares
    cols = wide + slim
    if order is None:
        out_specs = [pl.BlockSpec((model, cols), lambda i: (i, 0))]
        shapes = [(shares * model, cols)]
        sems = []
    else:
        out_specs = any_specs(2)
        shapes = [(shares * model // rows // 2, rows, cols)] * 2
        sems = [pltpu.SemaphoreType.DMA((shares, model // rows))]
    return pl.pallas_call(
        functools.partial(qkv_grad_body, order, rows),
        grid=(shares,),
        in_specs=[
            SMEM_SPEC,
            full_spec(normed.shape),
            pl.BlockSpec((wide, tokens), lambda i: (i, 0)),
            full_spec(context.shape),
            full_spec(branch_grad.shape),
        ],
        out_specs=out_specs,
        out_shape=[jax.ShapeDtypeStruct(shape, BF16) for shape in shapes],
        scratch_shapes=[pltpu.VMEM((shares, model, slim), BF16), pltpu.VMEM((shares, model, cols), BF16)] + sems,
        compiler_params=params_for(),
        cost_estimate=busy_for(1),
        name="qkv_grads",
    )(me, normed, mixed_grad, context, branch_grad)


DP, FSDP = "dp", "fsdp"


def swap(value, axis, bit):
    size = lax.axis_size(axis)
    return lax.ppermute(value, axis, [(i, i ^ bit) for i in range(size)])


def after(value, *others):
    return lax.optimization_barrier((value,) + others)[0]


def grow(value, step, *others):
    arrived = swap(value, *step)
    if others:
        arrived = after(arrived, *others)
    return jnp.concatenate([value, arrived], axis=0)


def fold_body(plan, count, *refs):
    sums = []
    for k in range(count):
        sums.append(refs[2 * k][...].astype(F32) + refs[2 * k + 1][...].astype(F32))
    for out_ref, takes in zip(refs[2 * count :], plan):
        start = 0
        for pair, spot in takes:
            part = sums[pair][spot].astype(out_ref.dtype)
            rows = part.shape[-2]
            out_ref[..., start : start + rows, :] = part
            start += rows


def fold_call(pairs, plan, in_blocks, out_blocks, out_shapes, steps, dtype=BF16):
    def spec(block, along):
        return pl.BlockSpec(block, lambda i: tuple(i if k in along else 0 for k in range(len(block))))

    arrays = [array for pair in pairs for array in pair]
    return pl.pallas_call(
        functools.partial(fold_body, plan, len(pairs)),
        grid=(steps,),
        in_specs=[spec(*in_blocks[k // 2]) for k in range(len(arrays))],
        out_specs=[spec(*b) for b in out_blocks],
        out_shape=[jax.ShapeDtypeStruct(shape, dtype) for shape in out_shapes],
        compiler_params=params_for(),
        cost_estimate=busy_for(2),
        name="fold_sums",
    )(*arrays)


class Fold:
    def __init__(self, keep, send):
        self.rows, self.cols = keep.shape[1:]
        self.keep, self.arrived = keep, swap(send, *CORE)
        self.stage = 0

    def step(self, *others):
        rows, cols = self.rows, self.cols
        cut, sizes = rows // 2, (2, 2, 4, rows, cols)
        upper, lower = slice(0, cut), slice(cut, rows)
        everything = slice(None)
        keep = after(self.keep, *others)
        if self.stage == 0:
            outs = fold_call(
                [(keep.reshape(sizes), self.arrived.reshape(sizes))],
                [
                    [(0, (0, everything, everything, upper))],
                    [(0, (1, everything, everything, upper))],
                    [(0, (everything, 0, everything, lower))],
                    [(0, (everything, 1, everything, lower))],
                ],
                [((2, 2, 1, rows, cols), (2,))],
                [((2, 1, cut, cols), (1,))] * 4,
                [(2, 4, cut, cols)] * 4,
                4,
            )
            self.keep, sent = (outs[0], outs[2]), (outs[1], outs[3])
            self.arrived = swap(sent[0], *XS), swap(sent[1], *YS)
        elif self.stage == 1:
            outs = fold_call(
                list(zip(keep, self.arrived)),
                [[(0, 0)], [(0, 1)], [(1, 0)], [(1, 1)]],
                [((2, 4, cut, cols), ())] * 2,
                [((4, cut, cols), ())] * 4,
                [(4, cut, cols)] * 4,
                1,
            )
            self.keep, sent = (outs[0], outs[2]), (outs[1], outs[3])
            self.arrived = swap(sent[0], *YS), swap(sent[1], *XS)
        elif self.stage == 2:
            self.keep, sent = fold_call(
                [[v.reshape(2, 2, cut, cols) for v in pair] for pair in zip(keep, self.arrived)],
                [[(0, 0), (1, 0)], [(0, 1), (1, 1)]],
                [((2, 2, cut, cols), ())] * 2,
                [((2, rows, cols), ())] * 2,
                [(2, rows, cols)] * 2,
                1,
            )
            self.arrived = swap(sent, *Z_NEAR)
        elif self.stage == 3:
            self.keep, sent = fold_call(
                [(keep, self.arrived)],
                [[(0, 0)], [(0, 1)]],
                [((2, rows, cols), ())],
                [((rows, cols), ())] * 2,
                [(rows, cols)] * 2,
                1,
            )
            self.arrived = swap(sent, *Z_FAR)
        else:
            return keep, self.arrived
        self.stage += 1
        return sent


def lane_sums(values):
    rows = jnp.sum(values, axis=0, keepdims=True)
    total = rows[:, :128]
    for k in range(1, values.shape[1] // 128):
        total += rows[:, 128 * k : 128 * (k + 1)]
    return total


def last_body(keep_ref, arrived_ref, squares_ref, small_ref, sum_ref, parts_ref):
    total = keep_ref[...].astype(F32) + arrived_ref[...].astype(F32)
    sum_ref[...] = total
    small = small_ref[...]
    lane = lax.broadcasted_iota(jnp.int32, (1, 128), 1)
    squares = squares_ref[...] + lane_sums(total * total) + jnp.where(lane == 0, jnp.sum(small * small), 0.0)
    parts_ref[...] = jnp.broadcast_to(squares[None], parts_ref.shape)


def last_sum(keep, arrived, squares, small, copies):
    whole = lambda shape: pl.BlockSpec(shape, lambda: (0,) * len(shape))
    out = (copies, 1, 128)
    return pl.pallas_call(
        last_body,
        in_specs=[whole(v.shape) for v in (keep, arrived, squares, small)],
        out_specs=[whole(keep.shape), whole(out)],
        out_shape=[jax.ShapeDtypeStruct(keep.shape, F32), jax.ShapeDtypeStruct(out, F32)],
        compiler_params=params_for(),
        cost_estimate=busy_for(2),
        name="last_sum",
    )(keep, arrived, squares, small)


def adam_body(threshold, plan, *refs):
    ins, outs = refs[: 4 + 3 * len(plan)], refs[4 + 3 * len(plan) :]
    parts_ref, q_ref, feed_ref, small_ref = ins[:4]
    norm = jnp.sqrt(jnp.sum(jnp.sum(parts_ref[...], axis=0), axis=-1, keepdims=True))
    outs[-1][...] = norm
    clip = jnp.minimum(1.0, threshold / norm)
    spot = 0
    for k, (which, windows, step_rate, decay_rate, low) in enumerate(plan):
        source = (q_ref, feed_ref, small_ref)[which]
        weight, first, second = (ref[...] for ref in ins[4 + 3 * k : 7 + 3 * k])
        gradient = jnp.concatenate([source[rows, lanes] for rows, lanes in windows], axis=0)
        results = adam_step(weight, gradient, first, second, clip, step_rate, decay_rate)
        for value in results:
            outs[spot][...] = value
            spot += 1
        if low:
            outs[spot][...] = results[2].astype(BF16)
            spot += 1


def adam_all(threshold, plan, parts, q_sum, feed_sum, small, states):
    whole = lambda shape: pl.BlockSpec(shape, lambda: (0,) * len(shape))
    arrays = [parts, q_sum, feed_sum, small] + [v for state in states for v in state]
    shapes = []
    for (_, _, _, _, low), (weight, _, _) in zip(plan, states):
        shapes += [jax.ShapeDtypeStruct(weight.shape, F32)] * 3
        shapes += [jax.ShapeDtypeStruct(weight.shape, BF16)] if low else []
    shapes.append(jax.ShapeDtypeStruct((1, 1), F32))
    return pl.pallas_call(
        functools.partial(adam_body, threshold, plan),
        in_specs=[whole(v.shape) for v in arrays],
        out_specs=[whole(v.shape) for v in shapes],
        out_shape=shapes,
        compiler_params=params_for(),
        cost_estimate=busy_for(4),
        name="adam_all",
    )(*arrays)


def rel_table(steps, last, off):
    places = []
    for pos in range(2 ** len(steps)):
        rel = {DP: 0, FSDP: 0}
        for k, (axis, bit) in enumerate(steps):
            if (pos >> k) & 1:
                rel[axis] ^= bit
        if last is not None:
            rel[last[0]] ^= last[1]
        places.append((rel[DP], rel[FSDP], off, True))
    return tuple(places)


CORE, XS, YS, Z_NEAR, Z_FAR = (FSDP, 1), (FSDP, 2), (DP, 1), (DP, 2), (DP, 4)
XY = [Z_FAR, Z_NEAR, XS, YS]
YX = [Z_FAR, Z_NEAR, YS, XS]


def grow_end(value, second, *others):
    value = grow(value, second[0], *others)
    value = grow(value, second[1])
    return value, swap(value, *CORE)


def order_of(steps):
    return [(axis == DP, bit) for axis, bit in steps]


def adam_step(weight, gradient, first_mom, second, clip_factor, step_rate, decay_rate):
    scaled = gradient * clip_factor
    first_new = 0.5 * first_mom + 0.5 * scaled
    second_new = 0.5 * second + 0.5 * scaled * scaled
    correction = 1.0 - 0.5**STEP
    update = first_new / correction / (jnp.sqrt(second_new / correction) + 1e-08)
    return (first_new, second_new, weight - step_rate * (update + decay_rate * weight))


def on_device(
    tokens,
    visible_index,
    cotangent,
    qkv_weight,
    out_weight,
    up_weight,
    down_weight,
    vectors,
    qkv_first,
    out_first,
    up_first,
    down_first,
    vector_first,
    qkv_second,
    out_second,
    up_second,
    down_second,
    vector_second,
):
    _, chip_count, seq_len, model_width = tokens.shape
    dp_size, fsdp_size = lax.axis_size(DP), lax.axis_size(FSDP)
    device_count = dp_size * fsdp_size
    both = (DP, FSDP)
    block_count = dp_size
    block_seen = seq_len // block_count
    block_len = cotangent.shape[2]
    chips_group = chip_count * block_count
    rows, wide = qkv_weight.shape
    slim = out_weight.shape[1]
    span = up_weight.shape[1]
    ff_width = span * fsdp_size
    half = slim // 2
    tall = down_weight.shape[0]
    folded = (dp_size, fsdp_size) == (8, 4)

    share_q = jnp.concatenate([qkv_weight, out_weight], axis=1).astype(BF16)
    share_u = up_weight.astype(BF16)
    down_turned = down_weight.astype(BF16).T

    vec_rows, vec_cols = vectors.shape
    vector_copies = jnp.broadcast_to(vectors.astype(BF16), (device_count, vec_rows, vec_cols))
    vec_shares = lax.all_to_all(vector_copies, both, split_axis=0, concat_axis=0, tiled=True)
    vec = vec_shares.reshape(dp_size, fsdp_size, vec_rows, vec_cols).transpose(1, 2, 0, 3)
    vec = vec.reshape(fsdp_size * vec_rows, model_width).astype(F32)

    my_block = lax.axis_index(DP)
    places = visible_index[0].reshape(chips_group, block_count, block_seen)
    places = lax.dynamic_index_in_dim(places, my_block, 1, keepdims=False) - my_block * block_len
    seen_places = places
    cot = cotangent[0]
    whole_tiles = block_seen % 16 == 0
    if whole_tiles:
        places = jnp.pad(places, ((0, 0), (0, 16)), constant_values=-1)[:, :, None]
        cot_seen, mask_grad = seen_rows(cot, places, block_seen)
    else:
        slot_ids = lax.broadcasted_iota(jnp.int32, (chips_group, block_len, block_seen), 1)
        pick = (places[:, None, :] == slot_ids).astype(BF16)
        gaps = 1.0 - jnp.sum(pick.astype(F32), axis=-1)
        cot_seen = jnp.einsum("cpv,cpd->cvd", pick, cot, preferred_element_type=F32).astype(BF16)
        mask_grad = jnp.einsum("cp,cpd->d", gaps.astype(BF16), cot, preferred_element_type=F32)[None]
    if folded:
        me = jnp.stack([lax.axis_index(DP), lax.axis_index(FSDP)]).astype(jnp.int32)
        share_d = jnp.concatenate([down_turned[:half], down_turned[half:]], axis=1)
        cut = rows // 2
        cur = grow(grow(share_q[None], Z_FAR, cot_seen), Z_NEAR)
        q_upper, q_lower = grow(cur[:, :cut], XS, vec_shares), grow(cur[:, cut:], YS, vec_shares)
        q_upper, q_lower = grow(q_upper, YS), grow(q_lower, XS)
        q_arrays = (q_upper, swap(q_upper, *CORE), q_lower, swap(q_lower, *CORE))
        q_table = (
            rel_table(XY, None, 0),
            rel_table(XY, CORE, 0),
            rel_table(YX, None, cut),
            rel_table(YX, CORE, cut),
        )
        gathered = lax.all_gather(jnp.concatenate([share_u, share_d]), both, axis=0, tiled=False)
        u_arrays = d_arrays = (gathered,)
        u_table = d_table = (tuple((d, f, 0, False) for d in range(dp_size) for f in range(fsdp_size)),)
        order = order_of([CORE, XS, YS, Z_NEAR, Z_FAR])
        down_share = (half, tall)
        load_rows = rows
    else:
        me = jnp.zeros((2,), jnp.int32)

        def gather_whole(share):
            whole = lax.all_gather(share, both, axis=0, tiled=False)
            whole = whole.reshape((dp_size, fsdp_size) + share.shape).transpose(1, 0, 2, 3)
            return whole.reshape(fsdp_size, dp_size * share.shape[0], share.shape[1])

        q_arrays = (gather_whole(share_q),)
        u_arrays = (gather_whole(share_u),)
        down_whole = lax.all_gather(down_turned, both, axis=0, tiled=False)
        down_whole = down_whole.reshape(dp_size, fsdp_size, slim, tall).transpose(1, 2, 0, 3)
        d_arrays = (down_whole.reshape(1, model_width, ff_width),)
        q_table = u_table = (tuple((0, f, 0, False) for f in range(fsdp_size)),)
        d_table = (((0, 0, 0, False),),)
        order = None
        down_share = None
        load_rows = model_width

    cot_seen = cot_seen.reshape(block_count, chip_count, block_seen, model_width)
    grad = lax.all_to_all(cot_seen, DP, split_axis=0, concat_axis=0, tiled=True)
    if not whole_tiles:
        grad = grad.transpose(1, 0, 2, 3).reshape(1, chip_count, seq_len, model_width)

    x = tokens[0]
    up_bias = vec[6:10].reshape(1, ff_width)
    value_bias = vec[2].reshape(model_width, 1)
    normed, mixed, expo, share, context, qkv_whole, out_whole = attend_forward(
        me, x, vec, value_bias, q_table, q_arrays, load_rows, wide
    )
    if folded:
        context = after(context, grad)
    result, normed_two, active, gate_grad, feed_grad, middle_grad, branch_grad, context_grad, sums_two, up_sums = (
        feed_forward_back(
            me, grad, x, context, vec, up_bias, out_whole, u_table, u_arrays, d_table, d_arrays, load_rows, down_share
        )
    )
    feed_blocks = feed_grads(me, normed_two, gate_grad, feed_grad, active, order, rows, half, tall, fsdp_size)
    if folded:
        feed_fold = Fold(*feed_blocks)
        context_grad = after(context_grad, *feed_blocks)
    mixed_grad, sums_value = attend_back(mixed, expo, share, context_grad)
    if folded:
        normed = after(normed, feed_fold.step(mixed_grad))
    q_blocks = qkv_grads(me, normed, mixed_grad, context, branch_grad, order, rows, wide)
    if not whole_tiles:
        result = result.reshape(chip_count, block_count, block_seen, model_width).transpose(1, 0, 2, 3)
    arrived = lax.all_to_all(result, DP, split_axis=0, concat_axis=0, tiled=True)
    arrived = arrived.reshape(chips_group, block_seen, model_width)
    if folded:
        q_fold = Fold(*q_blocks)
        x = after(x, *q_blocks)
    tokens_grad, sums_one = tokens_back(x, middle_grad, mixed_grad, vec, qkv_whole)

    vector_grad = jnp.concatenate(
        [
            sums_one[:2],
            sums_value[:1],
            sums_two[:3],
            up_sums.reshape(-1, model_width),
            sums_two[3:4],
            mask_grad,
        ],
        axis=0,
    )
    parts = vector_grad.reshape(fsdp_size, vec_rows, dp_size, vec_cols).transpose(2, 0, 1, 3)
    parts = parts.reshape(device_count, vec_rows, vec_cols)
    small = jnp.sum(lax.all_to_all(parts, both, split_axis=0, concat_axis=0, tiled=True), axis=0)

    slot_ids = lax.broadcasted_iota(jnp.int32, (chips_group, block_len, block_seen), 1)
    pick = (seen_places[:, None, :] == slot_ids).astype(BF16)
    gaps = 1.0 - jnp.sum(pick.astype(F32), axis=-1)
    filled = jnp.einsum("cpv,cvd->cpd", pick, arrived, preferred_element_type=F32)
    filled = filled + gaps[..., None] * vec[11]
    full_layout = filled.astype(BF16).reshape(1, chips_group, block_len, model_width)

    if folded:
        feed_fold.step(tokens_grad, arrived)
        q_fold.step(tokens_grad)
        feed_fold.step()
        q_fold.step()
        feed_fold.step()
        q_fold.step()
        feed_sum, squares = last_sum(*feed_fold.step(), jnp.zeros((1, 128), F32), small, 1)
        q_fold.step()
        q_sum, squares = last_sum(*q_fold.step(), squares[0], jnp.zeros_like(small), device_count)
    else:

        def scatter_whole(whole):
            cols = whole.shape[2]
            pieces = whole.reshape(fsdp_size, dp_size, -1, cols).transpose(1, 0, 2, 3)
            pieces = pieces.reshape(-1, cols)
            return lax.psum_scatter(pieces, both, scatter_dimension=0, tiled=True).astype(F32)

        q_sum, u_sum = scatter_whole(q_blocks[0].reshape(fsdp_size, model_width, -1)), scatter_whole(feed_blocks[0])
        pieces = feed_blocks[1].reshape(fsdp_size, slim, dp_size, tall).transpose(2, 0, 1, 3)
        pieces = pieces.reshape(device_count * slim, tall)
        d_sum = lax.psum_scatter(pieces, both, scatter_dimension=0, tiled=True).astype(F32).T

    tokens_all = device_count * chip_count * seq_len
    threshold = 0.05 * model_width * math.sqrt(tokens_all)
    rate = 0.6 / math.sqrt(model_width)
    out_rate = 0.6 / math.sqrt(model_width // 32)
    down_rate = 0.6 / math.sqrt(ff_width)
    if folded:
        squares = lax.all_to_all(squares, both, split_axis=0, concat_axis=0, tiled=True)
        everything = slice(None)
        plan = (
            (0, ((everything, slice(0, wide)),), rate, 0.05, True),
            (0, ((everything, slice(wide, wide + slim)),), out_rate, 0.05, True),
            (1, ((slice(0, rows), everything),), rate, 0.05, True),
            (1, ((slice(rows, rows + half), slice(0, tall)), (slice(rows, rows + half), slice(tall, 2 * tall))), down_rate, 0.05, True),
            (2, ((everything, everything),), 0.45, 0.0, False),
        )
        states = (
            (qkv_weight, qkv_first, qkv_second),
            (out_weight, out_first, out_second),
            (up_weight, up_first, up_second),
            (down_weight.T, down_first.T, down_second.T),
            (vectors, vector_first, vector_second),
        )
        news = adam_all(threshold, plan, squares, q_sum, feed_sum, small, states)
        qkv_out, out_out, up_out = news[0:4], news[4:8], news[8:12]
        down_out = [v.T for v in news[12:16]]
        vec_out, grad_norm = news[16:19], news[19][0, 0]
    else:
        grads = (q_sum[:, :wide], q_sum[:, wide:], u_sum, d_sum, small)
        squares = sum(jnp.sum(grad * grad) for grad in grads)
        squares = jnp.broadcast_to(squares, (device_count, 1))
        grad_total = jnp.sum(lax.all_to_all(squares, both, split_axis=0, concat_axis=0, tiled=True))
        grad_norm = jnp.sqrt(grad_total)
        clip = jnp.minimum(1.0, threshold / grad_norm)

        def stepped(*state):
            news = adam_step(*state)
            return news + (news[2].astype(BF16),)

        qkv_out = stepped(qkv_weight, grads[0], qkv_first, qkv_second, clip, rate, 0.05)
        out_out = stepped(out_weight, grads[1], out_first, out_second, clip, out_rate, 0.05)
        up_out = stepped(up_weight, grads[2], up_first, up_second, clip, rate, 0.05)
        down_out = stepped(down_weight, grads[3], down_first, down_second, clip, down_rate, 0.05)
        vec_out = adam_step(vectors, grads[4], vector_first, vector_second, clip, 0.45, 0.0)
    return (
        full_layout,
        tokens_grad[None],
        *qkv_out,
        *out_out,
        *up_out,
        *down_out,
        *vec_out,
        grad_norm,
    )


def solution(mesh):
    grid = P("dp", "fsdp")
    table = P("fsdp", "dp")
    weights = (grid, grid, grid, grid, table)
    in_specs = (
        P("fsdp", "dp", None, None),
        P("fsdp", None, None),
        P("fsdp", None, "dp", None),
        *weights,
        *weights,
        *weights,
    )
    out_specs = (
        P("fsdp", None, "dp", None),
        P("fsdp", "dp", None, None),
        *(grid,) * 16,
        *(table,) * 3,
        P(),
    )
    return jax.shard_map(
        on_device, mesh=mesh, in_specs=in_specs, out_specs=out_specs, check_vma=False
    )
```

```python
import functools
import math

import jax
import jax.numpy as jnp
from jax import lax
from jax.experimental import pallas as pl
from jax.experimental.pallas import tpu as pltpu
from jax.sharding import PartitionSpec as P

HD = 64
HEAD_GROUP = 6
STEP = 10
F32 = jnp.float32
BF16 = jnp.bfloat16
VMEM_BYTES = 66_900_000


def params_for(**more):
    return pltpu.CompilerParams(vmem_limit_bytes=VMEM_BYTES, **more)


def busy_for(micros):
    return pl.CostEstimate(flops=micros * 10**9, bytes_accessed=micros * 3 * 10**6, transcendentals=0)


def dot_nn(left, right):
    return lax.dot_general(left, right, (((1,), (0,)), ((), ())), preferred_element_type=F32)


def dot_nt(left, right):
    return lax.dot_general(left, right, (((1,), (1,)), ((), ())), preferred_element_type=F32)


def dot_tn(left, right):
    return lax.dot_general(left, right, (((0,), (0,)), ((), ())), preferred_element_type=F32)


def norm_parts(values):
    center = values - jnp.mean(values, axis=-1, keepdims=True)
    spread = jnp.mean(center * center, axis=-1, keepdims=True)
    factor = lax.rsqrt(spread + 1e-05)
    return center * factor, factor


def norm_back(grad, hat, factor, gain):
    scaled = grad * gain
    inner = jnp.mean(scaled * hat, axis=-1, keepdims=True)
    return factor * (scaled - jnp.mean(scaled, axis=-1, keepdims=True) - hat * inner)


def gelu_pair(gate):
    cdf = 0.5 + 0.5 * lax.erf(gate * 0.5**0.5)
    bell = jnp.exp2(gate * gate * (-0.5 * math.log2(math.e))) * (0.5 / math.pi) ** 0.5
    return gate * cdf, cdf + gate * bell


def load_grid(table, refs, me_ref, dest, sems, rows, first=0, start=True):
    copies = []
    for ref, places in zip(refs, table):
        for pos, (rel_d, rel_f, off, turned) in enumerate(places):
            d = rel_d ^ me_ref[0] if turned else rel_d
            f = rel_f ^ me_ref[1] if turned else rel_f
            height = min(ref.shape[1], rows)
            row = pl.multiple_of(d * rows + off, 16)
            copy = pltpu.make_async_copy(
                ref.at[pos, pl.ds(0, height)], dest.at[f, pl.ds(row, height)], sems.at[first + len(copies)]
            )
            if start:
                copy.start()
            copies.append(copy)
    return copies


def load_down(table, refs, me_ref, dest, sems, share, first=0, start=True):
    copies = []
    for ref, places in zip(refs, table):
        for pos, (rel_d, rel_f, off, turned) in enumerate(places):
            if share is None:
                pairs = [(ref.at[pos], dest)]
            else:
                half, wide = share
                d = rel_d ^ me_ref[0] if turned else rel_d
                f = rel_f ^ me_ref[1] if turned else rel_f
                lane = pl.multiple_of(d * wide, 128)
                pairs = []
                for k in range(2):
                    row = pl.multiple_of(f * (2 * half) + k * half + off, 16)
                    pairs.append(
                        (
                            ref.at[pos, pl.ds(ref.shape[1] - half, half), pl.ds(k * wide, wide)],
                            dest.at[pl.ds(row, half), pl.ds(lane, wide)],
                        )
                    )
            for src, dst in pairs:
                copy = pltpu.make_async_copy(src, dst, sems.at[first + len(copies)])
                if start:
                    copy.start()
                copies.append(copy)
    return copies


def any_specs(count):
    return [pl.BlockSpec(memory_space=pl.ANY)] * count


SMEM_SPEC = pl.BlockSpec(memory_space=pltpu.SMEM)


def full_spec(shape):
    return pl.BlockSpec(shape, lambda i: (0,) * len(shape))


def seen_body(seen, *refs):
    cot_refs, (places_ref, out_ref, sum_ref) = refs[:-3], refs[-3:]
    count, length, _ = cot_refs[0].shape
    depth = places_ref.shape[1]

    @pl.when(pl.program_id(0) == 0)
    def _():
        sum_ref[...] = jnp.zeros_like(sum_ref)

    lane = lax.broadcasted_iota(jnp.int32, (depth, length), 1)
    row = lax.broadcasted_iota(jnp.int32, (depth, length), 0)
    for k in range(count * len(cot_refs)):
        pick = jnp.where((lane == places_ref[k]) | (row == seen), 1.0, 0.0).astype(BF16)
        rows = dot_nn(pick, cot_refs[k // count][k % count])
        out_ref[k] = rows[:seen].astype(BF16)
        sum_ref[...] += rows[seen : seen + 1] - jnp.sum(rows[:seen], axis=0, keepdims=True)


def seen_rows(cot, places, seen):
    chips, length, model = cot.shape
    streams, step = 4, 8

    def stream(k):
        return pl.BlockSpec((step // streams, length, model), lambda i: (i * streams + k, 0, 0))

    return pl.pallas_call(
        functools.partial(seen_body, seen),
        grid=(chips // step,),
        in_specs=[stream(k) for k in range(streams)]
        + [pl.BlockSpec((step,) + places.shape[1:], lambda i: (i, 0, 0))],
        out_specs=[pl.BlockSpec((step, seen, model), lambda i: (i, 0, 0)), full_spec((1, model))],
        out_shape=[
            jax.ShapeDtypeStruct((chips, seen, model), BF16),
            jax.ShapeDtypeStruct((1, model), F32),
        ],
        compiler_params=params_for(),
        cost_estimate=busy_for(8),
        name="seen_rows",
    )(*[cot] * streams, places)


def attend_body(table, rows, heads, wide, *refs):
    n = len(table)
    me_ref, x_ref, vec_ref, bias_ref = refs[:4]
    w_refs = refs[4 : 4 + n]
    normed_ref, mixed_ref, expo_ref, share_ref, context_ref, qkv_out, out_out = refs[4 + n : 11 + n]
    qkv_ref, out_ref, weight, sems = refs[11 + n :]
    shares, model, cols = weight.shape
    slim = cols - wide
    step, last = pl.program_id(0), pl.num_programs(0) - 1
    count = sum(len(t) for t in table)
    saves = [
        pltpu.make_async_copy(qkv_ref, qkv_out, sems.at[count]),
        pltpu.make_async_copy(out_ref, out_out, sems.at[count + 1]),
    ]

    @pl.when(step == 0)
    def _():
        load_grid(table, w_refs, me_ref, weight, sems, rows)

    hat, _ = norm_parts(x_ref[0].astype(F32))
    normed = (hat * vec_ref[0:1, :] + vec_ref[1:2, :]).astype(BF16)
    normed_ref[...] = normed.T

    @pl.when(step == 0)
    def _():
        for copy in load_grid(table, w_refs, me_ref, weight, sems, rows, start=False):
            copy.wait()
        up_to = -(-wide // 128) * 128
        for f in range(shares):
            qkv_ref[f * wide : (f + 1) * wide, :] = weight[f, :, :up_to].T[:wide]
            out_ref[:, f * slim : (f + 1) * slim] = weight[f, :, wide:]
        for copy in saves:
            copy.start()

    for part in range(3):
        spot = slice(part * model, (part + 1) * model)
        mixed = dot_nt(qkv_ref[spot, :], normed)
        if part == 2:
            mixed = mixed + bias_ref[...]
        mixed_ref[spot, :] = mixed.astype(BF16)
    for first in range(0, heads, HEAD_GROUP):
        group = range(first, first + HEAD_GROUP)
        part = lambda which, head: mixed_ref[which * model + HD * head : which * model + HD * (head + 1), :]
        scores = [dot_tn(part(1, head), part(0, head) * jnp.asarray(HD ** (-0.5), BF16)) for head in group]
        expos = [jnp.exp(score - jnp.max(score, axis=0, keepdims=True)) for score in scores]
        shares = [1.0 / jnp.sum(expo, axis=0, keepdims=True) for expo in expos]
        expos = [expo.astype(BF16) for expo in expos]
        contexts = [dot_nn(part(2, head), expo) for head, expo in zip(group, expos)]
        for head, expo, share, context in zip(group, expos, shares, contexts):
            share_ref[head : head + 1, :] = share
            expo_ref[0, head] = expo
            context_ref[HD * head : HD * (head + 1), :] = (context * share).astype(BF16)

    @pl.when(step == last)
    def _():
        for copy in saves:
            copy.wait()


def attend_forward(me, x, vec, bias, table, arrays, rows, wide):
    chips, seq, model = x.shape
    heads = model // HD
    cols = arrays[0].shape[-1]
    shares = 3 * model // wide
    count = sum(len(t) for t in table)
    tall = lambda h: pl.BlockSpec((h, seq), lambda i: (0, i))
    tokens = chips * seq
    return pl.pallas_call(
        functools.partial(attend_body, table, rows, heads, wide),
        grid=(chips,),
        in_specs=[
            SMEM_SPEC,
            pl.BlockSpec((1, seq, model), lambda i: (i, 0, 0)),
            full_spec(vec.shape),
            full_spec(bias.shape),
        ]
        + any_specs(len(arrays)),
        out_specs=[
            tall(model),
            tall(3 * model),
            pl.BlockSpec((1, heads, seq, seq), lambda i: (i, 0, 0, 0)),
            tall(heads),
            tall(model),
        ]
        + any_specs(2),
        out_shape=[
            jax.ShapeDtypeStruct((model, tokens), BF16),
            jax.ShapeDtypeStruct((3 * model, tokens), BF16),
            jax.ShapeDtypeStruct((chips, heads, seq, seq), BF16),
            jax.ShapeDtypeStruct((heads, tokens), F32),
            jax.ShapeDtypeStruct((model, tokens), BF16),
            jax.ShapeDtypeStruct((3 * model, model), BF16),
            jax.ShapeDtypeStruct((model, model), BF16),
        ],
        scratch_shapes=[
            pltpu.VMEM((3 * model, model), BF16),
            pltpu.VMEM((model, model), BF16),
            pltpu.VMEM((shares, model, cols), BF16),
            pltpu.SemaphoreType.DMA((count + 2,)),
        ],
        compiler_params=params_for(),
        cost_estimate=busy_for(1),
        name="attend_forward",
    )(me, x, vec, bias, *arrays)


def feed_body(u_table, d_table, rows, share, *refs):
    nu, nd = len(u_table), len(d_table)
    me_ref, grad_ref, x_ref, context_ref, vec_ref, bias_ref, out_ref = refs[:7]
    u_refs = refs[7 : 7 + nu]
    d_refs = refs[7 + nu : 7 + nu + nd]
    (
        result_ref,
        normed_ref,
        active_ref,
        gate_grad_ref,
        feed_grad_ref,
        middle_grad_ref,
        branch_grad_ref,
        context_grad_ref,
        sums_ref,
        bias_sums_ref,
        up,
        down,
        sems,
    ) = refs[7 + nu + nd :]
    count = sum(len(t) for t in u_table)
    shares, model, span = up.shape
    seq = x_ref.shape[1]
    first_step = pl.program_id(0) == 0

    @pl.when(first_step)
    def _():
        load_grid(u_table, u_refs, me_ref, up, sems, rows)
        load_down(d_table, d_refs, me_ref, down, sems, share, first=count)
        sums_ref[...] = jnp.zeros_like(sums_ref)
        bias_sums_ref[...] = jnp.zeros_like(bias_sums_ref)

    feed_grad = grad_ref[:, 0].reshape(seq, model)
    feed_grad_ref[...] = feed_grad
    middle = x_ref[0].astype(F32) + dot_tn(context_ref[...], out_ref[...]) + vec_ref[3:4, :]
    hat, factor = norm_parts(middle)
    gain = vec_ref[4:5, :]
    normed = (hat * gain + vec_ref[5:6, :]).astype(BF16)
    normed_ref[...] = normed

    @pl.when(first_step)
    def _():
        for copy in load_grid(u_table, u_refs, me_ref, up, sems, rows, start=False):
            copy.wait()

    def gate_of(f):
        return dot_nn(normed, up[f]) + bias_ref[:, f * span : (f + 1) * span]

    gate = gate_of(0)

    @pl.when(first_step)
    def _():
        for copy in load_down(d_table, d_refs, me_ref, down, sems, share, first=count, start=False):
            copy.wait()

    def active_grad_of(f):
        return dot_nn(feed_grad, down[:, f * span : (f + 1) * span])

    normed_grad = jnp.zeros((seq, model), F32)
    result = middle + vec_ref[10:11, :]
    ready = gate, active_grad_of(0)
    for f in range(shares):
        lanes = slice(f * span, (f + 1) * span)
        gate, active_grad = ready
        if f + 1 < shares:
            ready = gate_of(f + 1), active_grad_of(f + 1)
        active, slope = gelu_pair(gate)
        active = active.astype(BF16)
        gate_grad = (active_grad * slope).astype(BF16)
        active_ref[:, lanes] = active
        gate_grad_ref[:, lanes] = gate_grad
        result += dot_nt(active, down[:, lanes])
        normed_grad += dot_nt(gate_grad, up[f])
        bias_sums_ref[:, lanes] += jnp.sum(gate_grad.astype(F32), axis=0, keepdims=True)
    result_ref[:, 0] = result.astype(BF16).reshape(result_ref.shape[0], -1, model)
    grad_full = feed_grad.astype(F32)
    middle_grad = grad_full + norm_back(normed_grad, hat, factor, gain)
    middle_grad_ref[0] = middle_grad
    branch_grad = middle_grad.astype(BF16)
    branch_grad_ref[...] = branch_grad
    context_grad_ref[...] = dot_nt(out_ref[...], branch_grad).astype(BF16)
    sums_ref[0:1, :] += jnp.sum(branch_grad.astype(F32), axis=0, keepdims=True)
    sums_ref[1:2, :] += jnp.sum(normed_grad * hat, axis=0, keepdims=True)
    sums_ref[2:3, :] += jnp.sum(normed_grad, axis=0, keepdims=True)
    sums_ref[3:4, :] += jnp.sum(grad_full, axis=0, keepdims=True)


def feed_forward_back(
    me, grad, x, context, vec, bias, out_whole, u_table, u_arrays, d_table, d_arrays, rows, share
):
    chips, seq, model = x.shape
    ff = bias.shape[1]
    blocks, _, seen, _ = grad.shape
    span = u_arrays[0].shape[-1]
    shares = ff // span
    tokens = chips * seq
    count = sum(len(t) for t in u_table) + 2 * sum(len(t) for t in d_table)
    tile = pl.BlockSpec((1, seq, model), lambda i: (i, 0, 0))
    flat = lambda w: pl.BlockSpec((seq, w), lambda i: (i, 0))
    tall = pl.BlockSpec((model, seq), lambda i: (0, i))
    spread = pl.BlockSpec((blocks, 1, seen, model), lambda i: (0, i, 0, 0))
    rows_of = lambda w: jax.ShapeDtypeStruct((tokens, w), BF16)
    return pl.pallas_call(
        functools.partial(feed_body, u_table, d_table, rows, share),
        grid=(chips,),
        in_specs=[
            SMEM_SPEC,
            spread,
            tile,
            tall,
            full_spec(vec.shape),
            full_spec(bias.shape),
            full_spec(out_whole.shape),
        ]
        + any_specs(len(u_arrays) + len(d_arrays)),
        out_specs=[
            spread,
            flat(model),
            flat(ff),
            flat(ff),
            flat(model),
            tile,
            flat(model),
            tall,
            full_spec((8, model)),
            full_spec((1, ff)),
        ],
        out_shape=[
            jax.ShapeDtypeStruct(grad.shape, BF16),
            rows_of(model),
            rows_of(ff),
            rows_of(ff),
            rows_of(model),
            jax.ShapeDtypeStruct((chips, seq, model), F32),
            rows_of(model),
            jax.ShapeDtypeStruct((model, tokens), BF16),
            jax.ShapeDtypeStruct((8, model), F32),
            jax.ShapeDtypeStruct((1, ff), F32),
        ],
        scratch_shapes=[
            pltpu.VMEM((shares, model, span), BF16),
            pltpu.VMEM((model, ff), BF16),
            pltpu.SemaphoreType.DMA((count,)),
        ],
        compiler_params=params_for(),
        cost_estimate=busy_for(10),
        name="feed_forward_back",
    )(me, grad, x, context, vec, bias, out_whole, *u_arrays, *d_arrays)


def attend_back_body(heads, mixed_ref, expo_ref, share_ref, grad_ref, mixed_grad_ref, sums_ref):
    model, seq = grad_ref.shape

    @pl.when(pl.program_id(0) == 0)
    def _():
        sums_ref[...] = jnp.zeros_like(sums_ref)

    scale = jnp.asarray(HD ** (-0.5), BF16)
    for first in range(0, heads, HEAD_GROUP):
        group = range(first, first + HEAD_GROUP)
        spot = lambda which, head: slice(which * model + HD * head, which * model + HD * (head + 1))
        shares = [share_ref[head : head + 1, :] for head in group]
        out_grads = [
            (grad_ref[spot(0, head), :].astype(F32) * share).astype(BF16) for head, share in zip(group, shares)
        ]
        prob_grads = [dot_tn(mixed_ref[spot(2, head), :], grad) for head, grad in zip(group, out_grads)]
        value_grads = [dot_nt(grad, expo_ref[0, head]) for head, grad in zip(group, out_grads)]
        score_grads = []
        for head, share, prob_grad in zip(group, shares, prob_grads):
            expo = expo_ref[0, head].astype(F32)
            weighted = expo * prob_grad
            inner = jnp.sum(weighted, axis=0, keepdims=True) * share
            score_grads.append((weighted - expo * inner).astype(BF16))
        query_grads = [dot_nn(mixed_ref[spot(1, head), :] * scale, grad) for head, grad in zip(group, score_grads)]
        key_grads = [dot_nt(mixed_ref[spot(0, head), :] * scale, grad) for head, grad in zip(group, score_grads)]
        for head, *grads in zip(group, query_grads, key_grads, value_grads):
            for which in range(3):
                mixed_grad_ref[spot(which, head), :] = grads[which].astype(BF16)
    sums_ref[...] += dot_nt(jnp.ones((8, seq), BF16), mixed_grad_ref[2 * model :, :])


def attend_back(mixed, expo, share, context_grad):
    model, tokens = context_grad.shape
    chips, heads, seq, _ = expo.shape
    tall = lambda h: pl.BlockSpec((h, seq), lambda i: (0, i))
    return pl.pallas_call(
        functools.partial(attend_back_body, heads),
        grid=(chips,),
        in_specs=[
            tall(3 * model),
            pl.BlockSpec((1, heads, seq, seq), lambda i: (i, 0, 0, 0)),
            tall(heads),
            tall(model),
        ],
        out_specs=[tall(3 * model), full_spec((8, model))],
        out_shape=[
            jax.ShapeDtypeStruct((3 * model, tokens), BF16),
            jax.ShapeDtypeStruct((8, model), F32),
        ],
        compiler_params=params_for(),
        cost_estimate=busy_for(1),
        name="attend_back",
    )(mixed, expo, share, context_grad)


def tokens_back_body(x_ref, grad_ref, mixed_grad_ref, vec_ref, qkv_ref, tokens_ref, sums_ref):
    @pl.when(pl.program_id(0) == 0)
    def _():
        sums_ref[...] = jnp.zeros_like(sums_ref)

    normed_grad = dot_tn(mixed_grad_ref[...], qkv_ref[...])
    hat, factor = norm_parts(x_ref[0].astype(F32))
    tokens_ref[0] = grad_ref[0] + norm_back(normed_grad, hat, factor, vec_ref[0:1, :])
    sums_ref[0:1, :] += jnp.sum(normed_grad * hat, axis=0, keepdims=True)
    sums_ref[1:2, :] += jnp.sum(normed_grad, axis=0, keepdims=True)


def tokens_back(x, middle_grad, mixed_grad, vec, qkv_whole):
    chips, seq, model = x.shape
    tile = pl.BlockSpec((1, seq, model), lambda i: (i, 0, 0))
    return pl.pallas_call(
        tokens_back_body,
        grid=(chips,),
        in_specs=[
            tile,
            tile,
            pl.BlockSpec((3 * model, seq), lambda i: (0, i)),
            full_spec(vec.shape),
            full_spec(qkv_whole.shape),
        ],
        out_specs=[tile, full_spec((8, model))],
        out_shape=[
            jax.ShapeDtypeStruct((chips, seq, model), F32),
            jax.ShapeDtypeStruct((8, model), F32),
        ],
        compiler_params=params_for(),
        cost_estimate=busy_for(25),
        name="tokens_back",
    )(x, middle_grad, mixed_grad, vec, qkv_whole)


def start_block(order, me_ref, d, f, sides, sem, source, *window):
    rel_d, rel_f = d ^ me_ref[0], f ^ me_ref[1]
    bits = [((rel_d if is_dp else rel_f) // value) % 2 for is_dp, value in order]
    pos = 0
    for bit in bits[1:]:
        pos = pos * 2 + bit
    for side, ref in enumerate(sides):

        @pl.when(bits[0] == side)
        def _():
            pltpu.make_async_copy(source, ref.at[(pos,) + window], sem).start()


def feed_grad_body(order, rows, half, wide, me_ref, normed_ref, gate_grad_ref, feed_grad_ref, active_ref, *refs):
    step = pl.program_id(0)
    if order is None:
        refs[0][0] = dot_tn(normed_ref[...], gate_grad_ref[...]).astype(BF16)
        refs[1][...] = dot_tn(feed_grad_ref[...], active_ref[...]).astype(BF16)
        return
    keep_ref, send_ref, up, down, sems = refs
    shares, model, span = up.shape
    count, fit = model // rows, span // wide
    sides = keep_ref, send_ref
    base = step * count * 2
    up[step] = dot_tn(normed_ref[...], gate_grad_ref[...]).astype(BF16)
    for d in range(count):
        source = up.at[step, pl.ds(d * rows, rows)]
        start_block(order, me_ref, d, step, sides, sems.at[step, d], source, pl.ds(0, rows))
    down[step] = dot_tn(feed_grad_ref[...], active_ref[...]).astype(BF16)
    sem = count
    for j in range(fit):
        for f in range(shares):
            for k in range(2):
                source = down.at[step, pl.ds((2 * f + k) * half, half), pl.ds(j * wide, wide)]
                window = pl.ds(rows, half), pl.ds(k * wide, wide)
                start_block(order, me_ref, step * fit + j, f, sides, sems.at[step, sem], source, *window)
                sem += 1

    @pl.when(step == shares - 1)
    def _():
        for s in range(shares):
            for d in range(count):
                pltpu.make_async_copy(
                    up.at[s, pl.ds(0, rows)], keep_ref.at[0, pl.ds(0, rows)], sems.at[s, d]
                ).wait()
            for k in range(count, sem):
                pltpu.make_async_copy(
                    down.at[s, pl.ds(0, half), pl.ds(0, wide)],
                    keep_ref.at[0, pl.ds(rows, half), pl.ds(0, wide)],
                    sems.at[s, k],
                ).wait()


def feed_grads(me, normed, gate_grad, feed_grad, active, order, rows, half, wide, shares):
    tokens, model = normed.shape
    ff = active.shape[1]
    span = ff // shares
    chunk = pl.BlockSpec((tokens, span), lambda i: (0, i))
    if order is None:
        out_specs = [
            pl.BlockSpec((1, model, span), lambda i: (i, 0, 0)),
            pl.BlockSpec((model, span), lambda i: (0, i)),
        ]
        shapes = [(shares, model, span), (model, ff)]
        scratch = []
    else:
        out_specs = any_specs(2)
        shapes = [(shares * model // rows // 2, rows + half, span)] * 2
        copies = model // rows + 2 * shares * (span // wide)
        scratch = [
            pltpu.VMEM((shares, model, span), BF16),
            pltpu.VMEM((shares, model, span), BF16),
            pltpu.SemaphoreType.DMA((shares, copies)),
        ]
    return pl.pallas_call(
        functools.partial(feed_grad_body, order, rows, half, wide),
        grid=(shares,),
        in_specs=[SMEM_SPEC, full_spec(normed.shape), chunk, full_spec(feed_grad.shape), chunk],
        out_specs=out_specs,
        out_shape=[jax.ShapeDtypeStruct(shape, BF16) for shape in shapes],
        scratch_shapes=scratch,
        compiler_params=params_for(),
        cost_estimate=busy_for(1),
        name="feed_grads",
    )(me, normed, gate_grad, feed_grad, active)


def qkv_grad_body(order, rows, me_ref, normed_ref, mixed_grad_ref, context_ref, branch_ref, *refs):
    f = pl.program_id(0)
    slots, packed = refs[-3:-1] if order is not None else refs[-2:]
    shares, model, slim = slots.shape
    wide = mixed_grad_ref.shape[0]

    @pl.when(f == 0)
    def _():
        whole = dot_nn(context_ref[...], branch_ref[...]).astype(BF16)
        for k in range(shares):
            slots[k] = whole[:, k * slim : (k + 1) * slim]

    packed[f, :, :wide] = dot_nt(normed_ref[...], mixed_grad_ref[...]).astype(BF16)
    packed[f, :, wide:] = slots[f]
    if order is None:
        refs[0][...] = packed[f]
        return
    sems = refs[-1]
    count = model // rows
    for d in range(count):
        source = packed.at[f, pl.ds(d * rows, rows)]
        start_block(order, me_ref, d, f, refs[:2], sems.at[f, d], source)

    @pl.when(f == shares - 1)
    def _():
        for s in range(shares):
            for d in range(count):
                pltpu.make_async_copy(packed.at[s, pl.ds(0, rows)], refs[0].at[0], sems.at[s, d]).wait()


def qkv_grads(me, normed, mixed_grad, context, branch_grad, order, rows, wide):
    model, tokens = normed.shape
    shares = 3 * model // wide
    slim = model // shares
    cols = wide + slim
    if order is None:
        out_specs = [pl.BlockSpec((model, cols), lambda i: (i, 0))]
        shapes = [(shares * model, cols)]
        sems = []
    else:
        out_specs = any_specs(2)
        shapes = [(shares * model // rows // 2, rows, cols)] * 2
        sems = [pltpu.SemaphoreType.DMA((shares, model // rows))]
    return pl.pallas_call(
        functools.partial(qkv_grad_body, order, rows),
        grid=(shares,),
        in_specs=[
            SMEM_SPEC,
            full_spec(normed.shape),
            pl.BlockSpec((wide, tokens), lambda i: (i, 0)),
            full_spec(context.shape),
            full_spec(branch_grad.shape),
        ],
        out_specs=out_specs,
        out_shape=[jax.ShapeDtypeStruct(shape, BF16) for shape in shapes],
        scratch_shapes=[pltpu.VMEM((shares, model, slim), BF16), pltpu.VMEM((shares, model, cols), BF16)] + sems,
        compiler_params=params_for(),
        cost_estimate=busy_for(1),
        name="qkv_grads",
    )(me, normed, mixed_grad, context, branch_grad)


DP, FSDP = "dp", "fsdp"


def swap(value, axis, bit):
    size = lax.axis_size(axis)
    return lax.ppermute(value, axis, [(i, i ^ bit) for i in range(size)])


def after(value, *others):
    return lax.optimization_barrier((value,) + others)[0]


def grow(value, step, *others):
    arrived = swap(value, *step)
    if others:
        arrived = after(arrived, *others)
    return jnp.concatenate([value, arrived], axis=0)


def fold_body(plan, count, *refs):
    sums = []
    for k in range(count):
        sums.append(refs[2 * k][...].astype(F32) + refs[2 * k + 1][...].astype(F32))
    for out_ref, takes in zip(refs[2 * count :], plan):
        start = 0
        for pair, spot in takes:
            part = sums[pair][spot].astype(out_ref.dtype)
            rows = part.shape[-2]
            out_ref[..., start : start + rows, :] = part
            start += rows


def fold_call(pairs, plan, in_blocks, out_blocks, out_shapes, steps, dtype=BF16):
    def spec(block, along):
        return pl.BlockSpec(block, lambda i: tuple(i if k in along else 0 for k in range(len(block))))

    arrays = [array for pair in pairs for array in pair]
    return pl.pallas_call(
        functools.partial(fold_body, plan, len(pairs)),
        grid=(steps,),
        in_specs=[spec(*in_blocks[k // 2]) for k in range(len(arrays))],
        out_specs=[spec(*b) for b in out_blocks],
        out_shape=[jax.ShapeDtypeStruct(shape, dtype) for shape in out_shapes],
        compiler_params=params_for(),
        cost_estimate=busy_for(2),
        name="fold_sums",
    )(*arrays)


class Fold:
    def __init__(self, keep, send):
        self.rows, self.cols = keep.shape[1:]
        self.keep, self.arrived = keep, swap(send, *CORE)
        self.stage = 0

    def step(self, *others):
        rows, cols = self.rows, self.cols
        cut, sizes = rows // 2, (2, 2, 4, rows, cols)
        upper, lower = slice(0, cut), slice(cut, rows)
        everything = slice(None)
        keep = after(self.keep, *others)
        if self.stage == 0:
            outs = fold_call(
                [(keep.reshape(sizes), self.arrived.reshape(sizes))],
                [
                    [(0, (0, everything, everything, upper))],
                    [(0, (1, everything, everything, upper))],
                    [(0, (everything, 0, everything, lower))],
                    [(0, (everything, 1, everything, lower))],
                ],
                [((2, 2, 1, rows, cols), (2,))],
                [((2, 1, cut, cols), (1,))] * 4,
                [(2, 4, cut, cols)] * 4,
                4,
            )
            self.keep, sent = (outs[0], outs[2]), (outs[1], outs[3])
            self.arrived = swap(sent[0], *XS), swap(sent[1], *YS)
        elif self.stage == 1:
            outs = fold_call(
                list(zip(keep, self.arrived)),
                [[(0, 0)], [(0, 1)], [(1, 0)], [(1, 1)]],
                [((2, 4, cut, cols), ())] * 2,
                [((4, cut, cols), ())] * 4,
                [(4, cut, cols)] * 4,
                1,
            )
            self.keep, sent = (outs[0], outs[2]), (outs[1], outs[3])
            self.arrived = swap(sent[0], *YS), swap(sent[1], *XS)
        elif self.stage == 2:
            self.keep, sent = fold_call(
                [[v.reshape(2, 2, cut, cols) for v in pair] for pair in zip(keep, self.arrived)],
                [[(0, 0), (1, 0)], [(0, 1), (1, 1)]],
                [((2, 2, cut, cols), ())] * 2,
                [((2, rows, cols), ())] * 2,
                [(2, rows, cols)] * 2,
                1,
            )
            self.arrived = swap(sent, *Z_NEAR)
        elif self.stage == 3:
            self.keep, sent = fold_call(
                [(keep, self.arrived)],
                [[(0, 0)], [(0, 1)]],
                [((2, rows, cols), ())],
                [((rows, cols), ())] * 2,
                [(rows, cols)] * 2,
                1,
            )
            self.arrived = swap(sent, *Z_FAR)
        else:
            return keep, self.arrived
        self.stage += 1
        return sent


def lane_sums(values):
    rows = jnp.sum(values, axis=0, keepdims=True)
    total = rows[:, :128]
    for k in range(1, values.shape[1] // 128):
        total += rows[:, 128 * k : 128 * (k + 1)]
    return total


def last_body(keep_ref, arrived_ref, squares_ref, small_ref, sum_ref, parts_ref):
    total = keep_ref[...].astype(F32) + arrived_ref[...].astype(F32)
    sum_ref[...] = total
    small = small_ref[...]
    lane = lax.broadcasted_iota(jnp.int32, (1, 128), 1)
    squares = squares_ref[...] + lane_sums(total * total) + jnp.where(lane == 0, jnp.sum(small * small), 0.0)
    parts_ref[...] = jnp.broadcast_to(squares[None], parts_ref.shape)


def last_sum(keep, arrived, squares, small, copies):
    whole = lambda shape: pl.BlockSpec(shape, lambda: (0,) * len(shape))
    out = (copies, 1, 128)
    return pl.pallas_call(
        last_body,
        in_specs=[whole(v.shape) for v in (keep, arrived, squares, small)],
        out_specs=[whole(keep.shape), whole(out)],
        out_shape=[jax.ShapeDtypeStruct(keep.shape, F32), jax.ShapeDtypeStruct(out, F32)],
        compiler_params=params_for(),
        cost_estimate=busy_for(2),
        name="last_sum",
    )(keep, arrived, squares, small)


def adam_body(threshold, plan, *refs):
    ins, outs = refs[: 4 + 3 * len(plan)], refs[4 + 3 * len(plan) :]
    parts_ref, q_ref, feed_ref, small_ref = ins[:4]
    norm = jnp.sqrt(jnp.sum(jnp.sum(parts_ref[...], axis=0), axis=-1, keepdims=True))
    outs[-1][...] = norm
    clip = jnp.minimum(1.0, threshold / norm)
    spot = 0
    for k, (which, windows, step_rate, decay_rate, low) in enumerate(plan):
        source = (q_ref, feed_ref, small_ref)[which]
        weight, first, second = (ref[...] for ref in ins[4 + 3 * k : 7 + 3 * k])
        gradient = jnp.concatenate([source[rows, lanes] for rows, lanes in windows], axis=0)
        results = adam_step(weight, gradient, first, second, clip, step_rate, decay_rate)
        for value in results:
            outs[spot][...] = value
            spot += 1
        if low:
            outs[spot][...] = results[2].astype(BF16)
            spot += 1


def adam_all(threshold, plan, parts, q_sum, feed_sum, small, states):
    whole = lambda shape: pl.BlockSpec(shape, lambda: (0,) * len(shape))
    arrays = [parts, q_sum, feed_sum, small] + [v for state in states for v in state]
    shapes = []
    for (_, _, _, _, low), (weight, _, _) in zip(plan, states):
        shapes += [jax.ShapeDtypeStruct(weight.shape, F32)] * 3
        shapes += [jax.ShapeDtypeStruct(weight.shape, BF16)] if low else []
    shapes.append(jax.ShapeDtypeStruct((1, 1), F32))
    return pl.pallas_call(
        functools.partial(adam_body, threshold, plan),
        in_specs=[whole(v.shape) for v in arrays],
        out_specs=[whole(v.shape) for v in shapes],
        out_shape=shapes,
        compiler_params=params_for(),
        cost_estimate=busy_for(4),
        name="adam_all",
    )(*arrays)


def rel_table(steps, last, off):
    places = []
    for pos in range(2 ** len(steps)):
        rel = {DP: 0, FSDP: 0}
        for k, (axis, bit) in enumerate(steps):
            if (pos >> k) & 1:
                rel[axis] ^= bit
        if last is not None:
            rel[last[0]] ^= last[1]
        places.append((rel[DP], rel[FSDP], off, True))
    return tuple(places)


CORE, XS, YS, Z_NEAR, Z_FAR = (FSDP, 1), (FSDP, 2), (DP, 1), (DP, 2), (DP, 4)
XY = [Z_FAR, Z_NEAR, XS, YS]
YX = [Z_FAR, Z_NEAR, YS, XS]


def grow_end(value, second, *others):
    value = grow(value, second[0], *others)
    value = grow(value, second[1])
    return value, swap(value, *CORE)


def order_of(steps):
    return [(axis == DP, bit) for axis, bit in steps]


def adam_step(weight, gradient, first_mom, second, clip_factor, step_rate, decay_rate):
    scaled = gradient * clip_factor
    first_new = 0.5 * first_mom + 0.5 * scaled
    second_new = 0.5 * second + 0.5 * scaled * scaled
    correction = 1.0 - 0.5**STEP
    update = first_new / correction / (jnp.sqrt(second_new / correction) + 1e-08)
    return (first_new, second_new, weight - step_rate * (update + decay_rate * weight))


def on_device(
    tokens,
    visible_index,
    cotangent,
    qkv_weight,
    out_weight,
    up_weight,
    down_weight,
    vectors,
    qkv_first,
    out_first,
    up_first,
    down_first,
    vector_first,
    qkv_second,
    out_second,
    up_second,
    down_second,
    vector_second,
):
    _, chip_count, seq_len, model_width = tokens.shape
    dp_size, fsdp_size = lax.axis_size(DP), lax.axis_size(FSDP)
    device_count = dp_size * fsdp_size
    both = (DP, FSDP)
    block_count = dp_size
    block_seen = seq_len // block_count
    block_len = cotangent.shape[2]
    chips_group = chip_count * block_count
    rows, wide = qkv_weight.shape
    slim = out_weight.shape[1]
    span = up_weight.shape[1]
    ff_width = span * fsdp_size
    half = slim // 2
    tall = down_weight.shape[0]
    folded = (dp_size, fsdp_size) == (8, 4)

    share_q = jnp.concatenate([qkv_weight, out_weight], axis=1).astype(BF16)
    share_u = up_weight.astype(BF16)
    down_turned = down_weight.astype(BF16).T

    vec_rows, vec_cols = vectors.shape
    vector_copies = jnp.broadcast_to(vectors.astype(BF16), (device_count, vec_rows, vec_cols))
    vec_shares = lax.all_to_all(vector_copies, both, split_axis=0, concat_axis=0, tiled=True)
    vec = vec_shares.reshape(dp_size, fsdp_size, vec_rows, vec_cols).transpose(1, 2, 0, 3)
    vec = vec.reshape(fsdp_size * vec_rows, model_width).astype(F32)
    value_bias = vec[2].reshape(model_width, 1)
    up_bias = vec[6:10].reshape(1, ff_width)

    my_block = lax.axis_index(DP)
    places = visible_index[0].reshape(chips_group, block_count, block_seen)
    places = lax.dynamic_index_in_dim(places, my_block, 1, keepdims=False) - my_block * block_len
    seen_places = places
    cot = cotangent[0]
    whole_tiles = block_seen % 16 == 0
    if whole_tiles:
        places = jnp.pad(places, ((0, 0), (0, 16)), constant_values=-1)[:, :, None]
        cot_seen, mask_grad = seen_rows(cot, places, block_seen)
    else:
        slot_ids = lax.broadcasted_iota(jnp.int32, (chips_group, block_len, block_seen), 1)
        pick = (places[:, None, :] == slot_ids).astype(BF16)
        gaps = 1.0 - jnp.sum(pick.astype(F32), axis=-1)
        cot_seen = jnp.einsum("cpv,cpd->cvd", pick, cot, preferred_element_type=F32).astype(BF16)
        mask_grad = jnp.einsum("cp,cpd->d", gaps.astype(BF16), cot, preferred_element_type=F32)[None]
    if folded:
        me = jnp.stack([lax.axis_index(DP), lax.axis_index(FSDP)]).astype(jnp.int32)
        share_d = jnp.concatenate([down_turned[:half], down_turned[half:]], axis=1)
        cut = rows // 2
        cur = grow(grow(share_q[None], Z_FAR, cot_seen), Z_NEAR)
        early = vec, value_bias, up_bias, me
        q_upper, q_lower = grow(cur[:, :cut], XS, *early), grow(cur[:, cut:], YS, *early)
        q_upper, q_lower = grow(q_upper, YS), grow(q_lower, XS)
        q_arrays = (q_upper, swap(q_upper, *CORE), q_lower, swap(q_lower, *CORE))
        q_table = (
            rel_table(XY, None, 0),
            rel_table(XY, CORE, 0),
            rel_table(YX, None, cut),
            rel_table(YX, CORE, cut),
        )
        gathered = lax.all_gather(jnp.concatenate([share_u, share_d]), both, axis=0, tiled=False)
        u_arrays = d_arrays = (gathered,)
        u_table = d_table = (tuple((d, f, 0, False) for d in range(dp_size) for f in range(fsdp_size)),)
        order = order_of([CORE, XS, YS, Z_NEAR, Z_FAR])
        down_share = (half, tall)
        load_rows = rows
    else:
        me = jnp.zeros((2,), jnp.int32)

        def gather_whole(share):
            whole = lax.all_gather(share, both, axis=0, tiled=False)
            whole = whole.reshape((dp_size, fsdp_size) + share.shape).transpose(1, 0, 2, 3)
            return whole.reshape(fsdp_size, dp_size * share.shape[0], share.shape[1])

        q_arrays = (gather_whole(share_q),)
        u_arrays = (gather_whole(share_u),)
        down_whole = lax.all_gather(down_turned, both, axis=0, tiled=False)
        down_whole = down_whole.reshape(dp_size, fsdp_size, slim, tall).transpose(1, 2, 0, 3)
        d_arrays = (down_whole.reshape(1, model_width, ff_width),)
        q_table = u_table = (tuple((0, f, 0, False) for f in range(fsdp_size)),)
        d_table = (((0, 0, 0, False),),)
        order = None
        down_share = None
        load_rows = model_width

    cot_seen = cot_seen.reshape(block_count, chip_count, block_seen, model_width)
    grad = lax.all_to_all(cot_seen, DP, split_axis=0, concat_axis=0, tiled=True)
    if not whole_tiles:
        grad = grad.transpose(1, 0, 2, 3).reshape(1, chip_count, seq_len, model_width)

    x = tokens[0]
    normed, mixed, expo, share, context, qkv_whole, out_whole = attend_forward(
        me, x, vec, value_bias, q_table, q_arrays, load_rows, wide
    )
    if folded:
        context = after(context, grad)
    result, normed_two, active, gate_grad, feed_grad, middle_grad, branch_grad, context_grad, sums_two, up_sums = (
        feed_forward_back(
            me, grad, x, context, vec, up_bias, out_whole, u_table, u_arrays, d_table, d_arrays, load_rows, down_share
        )
    )
    feed_blocks = feed_grads(me, normed_two, gate_grad, feed_grad, active, order, rows, half, tall, fsdp_size)
    if folded:
        feed_fold = Fold(*feed_blocks)
        context_grad = after(context_grad, *feed_blocks)
    mixed_grad, sums_value = attend_back(mixed, expo, share, context_grad)
    if folded:
        normed = after(normed, feed_fold.step(mixed_grad))
    q_blocks = qkv_grads(me, normed, mixed_grad, context, branch_grad, order, rows, wide)
    if not whole_tiles:
        result = result.reshape(chip_count, block_count, block_seen, model_width).transpose(1, 0, 2, 3)
    arrived = lax.all_to_all(result, DP, split_axis=0, concat_axis=0, tiled=True)
    arrived = arrived.reshape(chips_group, block_seen, model_width)
    if folded:
        q_fold = Fold(*q_blocks)
        x = after(x, *q_blocks)
    tokens_grad, sums_one = tokens_back(x, middle_grad, mixed_grad, vec, qkv_whole)

    vector_grad = jnp.concatenate(
        [
            sums_one[:2],
            sums_value[:1],
            sums_two[:3],
            up_sums.reshape(-1, model_width),
            sums_two[3:4],
            mask_grad,
        ],
        axis=0,
    )
    parts = vector_grad.reshape(fsdp_size, vec_rows, dp_size, vec_cols).transpose(2, 0, 1, 3)
    parts = parts.reshape(device_count, vec_rows, vec_cols)
    small = jnp.sum(lax.all_to_all(parts, both, split_axis=0, concat_axis=0, tiled=True), axis=0)

    slot_ids = lax.broadcasted_iota(jnp.int32, (chips_group, block_len, block_seen), 1)
    pick = (seen_places[:, None, :] == slot_ids).astype(BF16)
    gaps = 1.0 - jnp.sum(pick.astype(F32), axis=-1)
    filled = jnp.einsum("cpv,cvd->cpd", pick, arrived, preferred_element_type=F32)
    filled = filled + gaps[..., None] * vec[11]
    full_layout = filled.astype(BF16).reshape(1, chips_group, block_len, model_width)

    if folded:
        feed_fold.step(tokens_grad, arrived)
        q_fold.step(tokens_grad)
        feed_fold.step()
        q_fold.step()
        feed_fold.step()
        q_fold.step()
        feed_sum, squares = last_sum(*feed_fold.step(), jnp.zeros((1, 128), F32), small, 1)
        q_fold.step()
        q_sum, squares = last_sum(*q_fold.step(), squares[0], jnp.zeros_like(small), device_count)
    else:

        def scatter_whole(whole):
            cols = whole.shape[2]
            pieces = whole.reshape(fsdp_size, dp_size, -1, cols).transpose(1, 0, 2, 3)
            pieces = pieces.reshape(-1, cols)
            return lax.psum_scatter(pieces, both, scatter_dimension=0, tiled=True).astype(F32)

        q_sum, u_sum = scatter_whole(q_blocks[0].reshape(fsdp_size, model_width, -1)), scatter_whole(feed_blocks[0])
        pieces = feed_blocks[1].reshape(fsdp_size, slim, dp_size, tall).transpose(2, 0, 1, 3)
        pieces = pieces.reshape(device_count * slim, tall)
        d_sum = lax.psum_scatter(pieces, both, scatter_dimension=0, tiled=True).astype(F32).T

    tokens_all = device_count * chip_count * seq_len
    threshold = 0.05 * model_width * math.sqrt(tokens_all)
    rate = 0.6 / math.sqrt(model_width)
    out_rate = 0.6 / math.sqrt(model_width // 32)
    down_rate = 0.6 / math.sqrt(ff_width)
    if folded:
        squares = lax.all_to_all(squares, both, split_axis=0, concat_axis=0, tiled=True)
        everything = slice(None)
        plan = (
            (0, ((everything, slice(0, wide)),), rate, 0.05, True),
            (0, ((everything, slice(wide, wide + slim)),), out_rate, 0.05, True),
            (1, ((slice(0, rows), everything),), rate, 0.05, True),
            (1, ((slice(rows, rows + half), slice(0, tall)), (slice(rows, rows + half), slice(tall, 2 * tall))), down_rate, 0.05, True),
            (2, ((everything, everything),), 0.45, 0.0, False),
        )
        states = (
            (qkv_weight, qkv_first, qkv_second),
            (out_weight, out_first, out_second),
            (up_weight, up_first, up_second),
            (down_weight.T, down_first.T, down_second.T),
            (vectors, vector_first, vector_second),
        )
        news = adam_all(threshold, plan, squares, q_sum, feed_sum, small, states)
        qkv_out, out_out, up_out = news[0:4], news[4:8], news[8:12]
        down_out = [v.T for v in news[12:16]]
        vec_out, grad_norm = news[16:19], news[19][0, 0]
    else:
        grads = (q_sum[:, :wide], q_sum[:, wide:], u_sum, d_sum, small)
        squares = sum(jnp.sum(grad * grad) for grad in grads)
        squares = jnp.broadcast_to(squares, (device_count, 1))
        grad_total = jnp.sum(lax.all_to_all(squares, both, split_axis=0, concat_axis=0, tiled=True))
        grad_norm = jnp.sqrt(grad_total)
        clip = jnp.minimum(1.0, threshold / grad_norm)

        def stepped(*state):
            news = adam_step(*state)
            return news + (news[2].astype(BF16),)

        qkv_out = stepped(qkv_weight, grads[0], qkv_first, qkv_second, clip, rate, 0.05)
        out_out = stepped(out_weight, grads[1], out_first, out_second, clip, out_rate, 0.05)
        up_out = stepped(up_weight, grads[2], up_first, up_second, clip, rate, 0.05)
        down_out = stepped(down_weight, grads[3], down_first, down_second, clip, down_rate, 0.05)
        vec_out = adam_step(vectors, grads[4], vector_first, vector_second, clip, 0.45, 0.0)
    return (
        full_layout,
        tokens_grad[None],
        *qkv_out,
        *out_out,
        *up_out,
        *down_out,
        *vec_out,
        grad_norm,
    )


def solution(mesh):
    grid = P("dp", "fsdp")
    table = P("fsdp", "dp")
    weights = (grid, grid, grid, grid, table)
    in_specs = (
        P("fsdp", "dp", None, None),
        P("fsdp", None, None),
        P("fsdp", None, "dp", None),
        *weights,
        *weights,
        *weights,
    )
    out_specs = (
        P("fsdp", None, "dp", None),
        P("fsdp", "dp", None, None),
        *(grid,) * 16,
        *(table,) * 3,
        P(),
    )
    return jax.shard_map(
        on_device, mesh=mesh, in_specs=in_specs, out_specs=out_specs, check_vma=False
    )
```
